32 devices in a mesh: fsdp: 8 (over y, x, core), tp: 4 (over z).
Axes of the slice: x: 2, y: 2, z: 4, core: 2. Of those that a mesh axis runs over, the one named last changes fastest.
Arguments:
- tokens: bfloat16 [2, 4, 1536, 1536], P(None, None, ('fsdp', 'tp')), may hold values from -6 to 6
- memory: bfloat16 [2, 4, 64, 1536], replicated, may hold values from -6 to 6
- text_len: int32 [2, 4], replicated, may hold values from 1 to 64, as said below
- cotangent: bfloat16 [2, 4, 1536, 1536], P(None, None, ('fsdp', 'tp')), may hold values from -6 to 6
- gain_one: float32 [1536], replicated, may hold values from 0.5 to 1.5
- bias_one: float32 [1536], replicated, may hold values from -1 to 1
- gain_two: float32 [1536], replicated, may hold values from 0.5 to 1.5
- bias_two: float32 [1536], replicated, may hold values from -1 to 1
- gain_three: float32 [1536], replicated, may hold values from 0.5 to 1.5
- bias_three: float32 [1536], replicated, may hold values from -1 to 1
- w_query: bfloat16 [1536, 1536], P('fsdp', 'tp'), may hold values from -0.15625 to 0.15625
- w_key: bfloat16 [1536, 1536], P('fsdp', 'tp'), may hold values from -0.15625 to 0.15625
- w_value: bfloat16 [1536, 1536], P('fsdp', 'tp'), may hold values from -0.15625 to 0.15625
- w_out: bfloat16 [1536, 1536], P('tp', 'fsdp'), may hold values from -0.4375 to 0.4375
- c_query: bfloat16 [1536, 1536], P('fsdp', 'tp'), may hold values from -0.15625 to 0.15625
- c_key: bfloat16 [1536, 1536], P('fsdp', 'tp'), may hold values from -0.15625 to 0.15625
- c_value: bfloat16 [1536, 1536], P('fsdp', 'tp'), may hold values from -0.15625 to 0.15625
- c_out: bfloat16 [1536, 1536], P('tp', 'fsdp'), may hold values from -0.3125 to 0.3125
- w_up: bfloat16 [1536, 6144], P('fsdp', 'tp'), may hold values from -0.15625 to 0.15625
- w_down: bfloat16 [6144, 1536], P('tp', 'fsdp'), may hold values from -0.109375 to 0.109375
Outputs:
- layer_out: bfloat16 [2, 4, 1536, 1536], P(None, None, ('fsdp', 'tp'))
- grad_tokens: float32 [2, 4, 1536, 1536], P(None, None, ('fsdp', 'tp'))
- grad_memory: float32 [2, 4, 64, 1536], replicated
- grad_gain_one: float32 [1536], replicated
- grad_bias_one: float32 [1536], replicated
- grad_gain_two: float32 [1536], replicated
- grad_bias_two: float32 [1536], replicated
- grad_gain_three: float32 [1536], replicated
- grad_bias_three: float32 [1536], replicated
- grad_w_query: float32 [1536, 1536], P('fsdp', 'tp')
- grad_w_key: float32 [1536, 1536], P('fsdp', 'tp')
- grad_w_value: float32 [1536, 1536], P('fsdp', 'tp')
- grad_w_out: float32 [1536, 1536], P('tp', 'fsdp')
- grad_c_query: float32 [1536, 1536], P('fsdp', 'tp')
- grad_c_key: float32 [1536, 1536], P('fsdp', 'tp')
- grad_c_value: float32 [1536, 1536], P('fsdp', 'tp')
- grad_c_out: float32 [1536, 1536], P('tp', 'fsdp')
- grad_w_up: float32 [1536, 6144], P('fsdp', 'tp')
- grad_w_down: float32 [6144, 1536], P('tp', 'fsdp')
The draws below stay inside these ranges and needn't reach their ends.
Inputs may be any that keep to these rules, and one draw needn't show every extreme that they name: `text_len`: in every micro-batch some clip has all 64 text tokens.
All inputs are finite; a program needn't handle non-finite values.
Results may differ from the reference program's by a relative error of at most 0.02.
Values may be sent and summed in bfloat16 or wider, within the bound.
A program may use at most 232 MiB of HBM per device.

```python
import math
import jax
import jax.numpy as jnp
from jax import lax

D = 1536
HEADS = 24
HD = 64
FF = 6144
TEXT = 64
LEN = 1536
MICRO = 2
CLIPS = 4


def draw_text_len(key, part):
    key = jax.random.fold_in(key, 7)
    first_key, second_key = jax.random.split(key)
    counts = jax.random.randint(first_key, (MICRO, CLIPS), 1, TEXT + 1)
    chosen = jax.random.randint(second_key, (MICRO,), 0, CLIPS)
    full_mask = jnp.arange(CLIPS)[None, :] == chosen[:, None]
    return jnp.where(full_mask, TEXT, counts).astype(jnp.int32)


def block_levels(key, dims, cuts, least, top_value):
    gain = 1.0
    for axis_at, blocks in cuts:
        heights = jax.random.uniform(jax.random.fold_in(jax.random.fold_in(key, 6), axis_at), (blocks,), jnp.float32, least / len(cuts), top_value / len(cuts))
        gain = gain * jnp.repeat(jnp.exp(heights), dims[axis_at] // blocks).reshape((-1,) + (1,) * (len(dims) - 1 - axis_at))
    return gain


def centred(key, extent, scale, bound, cuts=(), held_as=jnp.bfloat16):
    drawn = scale * jax.random.normal(key, extent, jnp.float32)
    if cuts:
        drawn = drawn * block_levels(key, extent, cuts, -0.22, 0.18)
    return jnp.clip(drawn, -bound, bound).astype(held_as)


def setup_inputs(seed: int = 0) -> dict:
    splits = jax.random.split(jax.random.key(seed), 21)
    tokens = centred(splits[0], (MICRO, CLIPS, LEN, D), 1.0, 6.0, ((2, 32),))
    memory = centred(splits[1], (MICRO, CLIPS, TEXT, D), 1.0, 6.0)
    text_len = draw_text_len(jax.random.fold_in(splits[20], 71), 0)
    cotangent = centred(splits[3], (MICRO, CLIPS, LEN, D), 1.0, 6.0, ((2, 32),))
    gain_one = jnp.clip(1.0 + 0.1 * jax.random.normal(splits[4], (D,), jnp.float32), 0.5, 1.5)
    bias_one = centred(splits[5], (D,), 0.2, 1.0, (), jnp.float32)
    gain_two = jnp.clip(1.0 + 0.1 * jax.random.normal(splits[6], (D,), jnp.float32), 0.5, 1.5)
    bias_two = centred(splits[7], (D,), 0.2, 1.0, (), jnp.float32)
    gain_three = jnp.clip(1.0 + 0.1 * jax.random.normal(splits[8], (D,), jnp.float32), 0.5, 1.5)
    bias_three = centred(splits[9], (D,), 0.2, 1.0, (), jnp.float32)
    w_query = centred(splits[10], (D, D), D ** -0.5, 0.15625, ((0, 8), (1, 4)))
    w_key = centred(splits[11], (D, D), D ** -0.5, 0.15625, ((0, 8), (1, 4)))
    w_value = centred(splits[12], (D, D), D ** -0.5, 0.15625, ((0, 8), (1, 4)))
    w_out = centred(splits[13], (D, D), (D // 8) ** -0.5, 0.4375, ((0, 4), (1, 8)))
    c_query = centred(splits[14], (D, D), D ** -0.5, 0.15625, ((0, 8), (1, 4)))
    c_key = centred(splits[15], (D, D), D ** -0.5, 0.15625, ((0, 8), (1, 4)))
    c_value = centred(splits[16], (D, D), D ** -0.5, 0.15625, ((0, 8), (1, 4)))
    c_out = centred(splits[17], (D, D), (D // 4) ** -0.5, 0.3125, ((0, 4), (1, 8)))
    w_up = centred(splits[18], (D, FF), D ** -0.5, 0.15625, ((0, 8), (1, 4)))
    w_down = centred(splits[19], (FF, D), (FF // 2) ** -0.5, 0.109375, ((0, 4), (1, 8)))
    return dict(tokens=tokens, memory=memory, text_len=text_len, cotangent=cotangent, gain_one=gain_one, bias_one=bias_one, gain_two=gain_two, bias_two=bias_two, gain_three=gain_three, bias_three=bias_three, w_query=w_query, w_key=w_key, w_value=w_value, w_out=w_out, c_query=c_query, c_key=c_key, c_value=c_value, c_out=c_out, w_up=w_up, w_down=w_down)


@jax.custom_vjp
def low(v):
    return lax.optimization_barrier(v.astype(jnp.bfloat16)).astype(jnp.float32)

@jax.custom_vjp
def low_back(v):
    return v

def low_keep(v):
    return (low(v), None)

def low_pass(kept, grad):
    return (grad,)

def back_keep(v):
    return (v, None)

def back_low(kept, grad):
    return (low(grad),)
low.defvjp(low_keep, low_pass)
low_back.defvjp(back_keep, back_low)
EPSILON = 1e-05
PRECISE = lax.Precision.HIGHEST

def matmul(left_side, right_side):
    return jnp.dot(left_side, right_side, precision=PRECISE)

def layer_norm(values, gain_vec, bias_vec):
    center = values - lax.optimization_barrier(jnp.mean(values, axis=-1, keepdims=True))
    spread = lax.optimization_barrier(jnp.mean(center * center, axis=-1, keepdims=True))
    return center * lax.rsqrt(spread + EPSILON) * gain_vec + bias_vec

def attend(queries, key_rows, value_rows, allowed):
    factor = 1.0 / math.sqrt(HD)
    scores = low_back(jnp.einsum('qhe,khe->hqk', queries, key_rows, precision=PRECISE) * factor)
    scores = jnp.where(allowed[None], scores, -1e+30)
    weights = low(jax.nn.softmax(scores, axis=-1))
    return jnp.einsum('hqk,khe->qhe', weights, value_rows, precision=PRECISE)

def clip_layer(params, frames, text_block, text_count):
    gain_one, bias_one, gain_two, bias_two, gain_three, bias_three, w_query, w_key, w_value, w_out, c_query, c_key, c_value, c_out, w_up, w_down = params
    length = frames.shape[0]
    normed = low(layer_norm(frames, gain_one, bias_one))
    queries = low_back(low(matmul(normed, w_query))).reshape(length, HEADS, HD)
    key_rows = low_back(low(matmul(normed, w_key))).reshape(length, HEADS, HD)
    value_rows = low_back(low(matmul(normed, w_value))).reshape(length, HEADS, HD)
    position = jnp.arange(length)
    causal = position[None, :] <= position[:, None]
    mixed_self = low_back(low(attend(queries, key_rows, value_rows, causal).reshape(length, D)))
    after_self = frames + low_back(matmul(mixed_self, w_out))
    normed_two = low(layer_norm(after_self, gain_two, bias_two))
    cross_queries = low_back(low(matmul(normed_two, c_query))).reshape(length, HEADS, HD)
    cross_keys = low(matmul(text_block, c_key)).reshape(TEXT, HEADS, HD)
    cross_values = low(matmul(text_block, c_value)).reshape(TEXT, HEADS, HD)
    visible = jnp.broadcast_to(jnp.arange(TEXT)[None, :] < text_count, (length, TEXT))
    mixed_cross = low_back(low(attend(cross_queries, cross_keys, cross_values, visible).reshape(length, D)))
    after_cross = after_self + low_back(matmul(mixed_cross, c_out))
    normed_three = low(layer_norm(after_cross, gain_three, bias_three))
    hidden = low_back(matmul(normed_three, w_up))
    active = low(jax.nn.gelu(hidden))
    return after_cross + low_back(matmul(active, w_down))

def reference(tokens, memory, text_len, cotangent, gain_one, bias_one, gain_two, bias_two, gain_three, bias_three, w_query, w_key, w_value, w_out, c_query, c_key, c_value, c_out, w_up, w_down):
    params = tuple((t.astype(jnp.float32) for t in (gain_one, bias_one, gain_two, bias_two, gain_three, bias_three, w_query, w_key, w_value, w_out, c_query, c_key, c_value, c_out, w_up, w_down)))
    frames = tokens.reshape(MICRO * CLIPS, LEN, D).astype(jnp.float32)
    text_rows = memory.reshape(MICRO * CLIPS, TEXT, D).astype(jnp.float32)
    counts = text_len.reshape(MICRO * CLIPS).astype(jnp.int32)

    def stacked_layer(layer_params, frame_rows, text_states):
        clip_step = jax.checkpoint(clip_layer)
        return lax.map(lambda record: clip_step(layer_params, record[0], record[1], record[2]), (frame_rows, text_states, counts))
    outputs, pull_back = jax.vjp(stacked_layer, params, frames, text_rows)
    param_grads, frame_grads, text_grads = pull_back(cotangent.reshape(MICRO * CLIPS, LEN, D).astype(jnp.float32))
    return (outputs.astype(jnp.bfloat16).reshape(MICRO, CLIPS, LEN, D), frame_grads.reshape(MICRO, CLIPS, LEN, D), text_grads.reshape(MICRO, CLIPS, TEXT, D), param_grads[0], param_grads[1], param_grads[2], param_grads[3], param_grads[4], param_grads[5], param_grads[6], param_grads[7], param_grads[8], param_grads[9], param_grads[10], param_grads[11], param_grads[12], param_grads[13], param_grads[14], param_grads[15])
```

```python
import math

import jax
import jax.numpy as jnp
from jax import lax
from jax.experimental import pallas as pl
from jax.experimental.pallas import tpu as pltpu
from jax.sharding import PartitionSpec as P

HD = 64
MICRO = 2


EPSILON = 1e-05
PRECISE = lax.Precision.HIGHEST
MASKED = -1e30


def layer_norm(values, gain_vec, bias_vec):
    center = values - jnp.mean(values, axis=-1, keepdims=True)
    inverse = lax.rsqrt(jnp.mean(center * center, axis=-1, keepdims=True) + EPSILON)
    scaled = center * inverse
    return (scaled * gain_vec + bias_vec, scaled, inverse)


def norm_back(upstream, scaled, inverse, gain_vec):
    weighted = upstream * gain_vec
    result = inverse * (
        weighted
        - jnp.mean(weighted, axis=-1, keepdims=True)
        - scaled * jnp.mean(weighted * scaled, axis=-1, keepdims=True)
    )
    return (result, jnp.sum(upstream * scaled, axis=(0, 1)), jnp.sum(upstream, axis=(0, 1)))


def spread_rows(values):
    return lax.all_gather(values, "tp", axis=1, tiled=True)


def spread_grads(values):
    return lax.all_gather(values, "tp", axis=1, tiled=True)


def fold_rows(values):
    return lax.psum_scatter(values, "tp", scatter_dimension=1, tiled=True)


def fold_grads(values):
    return lax.psum_scatter(values, "tp", scatter_dimension=1, tiled=True)


def project(left_side, right_side):
    return jnp.einsum("cfd,de->cfe", left_side, right_side, preferred_element_type=jnp.float32)


def project_back(left_side, right_side):
    return jnp.einsum("cfe,de->cfd", left_side, right_side, preferred_element_type=jnp.float32)


def weight_grad(left_side, right_side):
    return jnp.einsum("cfd,cfe->de", left_side, right_side, preferred_element_type=jnp.float32)


def masked_scores(queries, key_rows, allowed):
    factor = 1.0 / math.sqrt(queries.shape[-1])
    scores = (
        jnp.einsum("cqhe,ckhe->chqk", queries, key_rows, preferred_element_type=jnp.float32)
        * factor
    )
    return jnp.where(allowed, scores, MASKED)


def attention_forward(queries, key_rows, value_rows, allowed):
    scores = masked_scores(queries, key_rows, allowed)
    highest = jnp.max(scores, axis=-1, keepdims=True)
    log_total = highest + jnp.log(jnp.sum(jnp.exp(scores - highest), axis=-1, keepdims=True))
    weights = jnp.exp(scores - log_total).astype(jnp.bfloat16)
    mixed = jnp.einsum("chqk,ckhe->cqhe", weights, value_rows, preferred_element_type=jnp.float32)
    return (mixed, log_total)


def score_grads(queries, key_rows, value_rows, allowed, log_total, grad_mixed):
    weights = jnp.exp(masked_scores(queries, key_rows, allowed) - log_total)
    grad_weights = jnp.einsum(
        "cqhe,ckhe->chqk", grad_mixed, value_rows, preferred_element_type=jnp.float32
    )
    row_total = jnp.sum(grad_weights * weights, axis=-1, keepdims=True)
    grad_scores = (weights * (grad_weights - row_total)).astype(jnp.bfloat16)
    return (weights, grad_scores, row_total)


def attention_backward(queries, key_rows, value_rows, allowed, log_total, grad_mixed):
    factor = 1.0 / math.sqrt(queries.shape[-1])
    weights, grad_scores, row_total = score_grads(
        queries, key_rows, value_rows, allowed, log_total, grad_mixed
    )
    grad_queries = (
        jnp.einsum("chqk,ckhe->cqhe", grad_scores, key_rows, preferred_element_type=jnp.float32)
        * factor
    )
    grad_keys = (
        jnp.einsum("chqk,cqhe->ckhe", grad_scores, queries, preferred_element_type=jnp.float32)
        * factor
    )
    grad_values = jnp.einsum(
        "chqk,cqhe->ckhe",
        weights.astype(jnp.bfloat16),
        grad_mixed,
        preferred_element_type=jnp.float32,
    )
    return (grad_queries, grad_keys, grad_values, row_total)


def body(
    tokens,
    memory,
    text_len,
    cotangent,
    gain_one,
    bias_one,
    gain_two,
    bias_two,
    gain_three,
    bias_three,
    w_query,
    w_key,
    w_value,
    w_out,
    c_query,
    c_key,
    c_value,
    c_out,
    w_up,
    w_down,
):
    clips = tokens.shape[1]
    shard_frames = tokens.shape[2] * lax.axis_size("tp")
    text_slots = memory.shape[2]
    local_width = w_query.shape[1]
    local_heads = local_width // HD
    query_pos = lax.axis_index("fsdp") * shard_frames + jnp.arange(shard_frames)
    key_pos = jnp.arange(shard_frames * lax.axis_size("fsdp"))
    causal = (key_pos[None, :] <= query_pos[:, None])[None, None]
    shards = (w_query, w_key, w_value, c_query, c_key, c_value, w_up, w_out, c_out, w_down)
    head_shape = (clips, shard_frames, local_heads, HD)
    text_shape = (clips, text_slots, local_heads, HD)
    outputs = []
    input_grads = []
    text_grads = []
    norm_totals = None
    weight_total = None
    for micro in range(MICRO):
        gathered = (
            lax.all_gather(shards[0], "fsdp", axis=0, tiled=True),
            lax.all_gather(shards[1], "fsdp", axis=0, tiled=True),
            lax.all_gather(shards[2], "fsdp", axis=0, tiled=True),
            lax.all_gather(shards[3], "fsdp", axis=0, tiled=True),
            lax.all_gather(shards[4], "fsdp", axis=0, tiled=True),
            lax.all_gather(shards[5], "fsdp", axis=0, tiled=True),
            lax.all_gather(shards[6], "fsdp", axis=0, tiled=True),
            lax.all_gather(shards[7], "fsdp", axis=1, tiled=True),
            lax.all_gather(shards[8], "fsdp", axis=1, tiled=True),
            lax.all_gather(shards[9], "fsdp", axis=1, tiled=True),
        )
        (
            query_full,
            key_full,
            value_full,
            cross_query,
            cross_key,
            cross_value,
            up_full,
            out_full,
            cross_out,
            down_full,
        ) = gathered
        frames = tokens[micro].astype(jnp.float32)
        text_rows = memory[micro]
        counts = text_len[micro]
        normed_one, scaled_one, inverse_one = layer_norm(frames, gain_one, bias_one)
        rows_one = spread_rows(normed_one.astype(jnp.bfloat16))
        queries = project(rows_one, query_full).astype(jnp.bfloat16).reshape(head_shape)
        key_local = project(rows_one, key_full).astype(jnp.bfloat16)
        value_local = project(rows_one, value_full).astype(jnp.bfloat16)
        key_all, value_all = (
            lax.all_gather(key_local, "fsdp", axis=1, tiled=True),
            lax.all_gather(value_local, "fsdp", axis=1, tiled=True),
        )
        key_all = key_all.reshape(clips, -1, local_heads, HD)
        value_all = value_all.reshape(clips, -1, local_heads, HD)
        mixed_one, total_one = attention_forward(queries, key_all, value_all, causal)
        mixed_one = mixed_one.astype(jnp.bfloat16).reshape(clips, shard_frames, local_width)
        after_self = frames + fold_rows(project(mixed_one, out_full))
        normed_two, scaled_two, inverse_two = layer_norm(after_self, gain_two, bias_two)
        rows_two = spread_rows(normed_two.astype(jnp.bfloat16))
        cross_q = project(rows_two, cross_query).astype(jnp.bfloat16).reshape(head_shape)
        cross_k = project(text_rows, cross_key).astype(jnp.bfloat16).reshape(text_shape)
        cross_v = project(text_rows, cross_value).astype(jnp.bfloat16).reshape(text_shape)
        visible = (jnp.arange(text_slots)[None, :] < counts[:, None])[:, None, None, :]
        mixed_two, total_two = attention_forward(cross_q, cross_k, cross_v, visible)
        mixed_two = mixed_two.astype(jnp.bfloat16).reshape(clips, shard_frames, local_width)
        after_cross = after_self + fold_rows(project(mixed_two, cross_out))
        normed_three, scaled_three, inverse_three = layer_norm(after_cross, gain_three, bias_three)
        rows_three = spread_rows(normed_three.astype(jnp.bfloat16))
        hidden = project(rows_three, up_full)
        active = jax.nn.gelu(hidden).astype(jnp.bfloat16)
        result = after_cross + fold_rows(project(active, down_full))
        outputs.append(result.astype(jnp.bfloat16))
        gathered = (
            lax.all_gather(shards[0], "fsdp", axis=0, tiled=True),
            lax.all_gather(shards[1], "fsdp", axis=0, tiled=True),
            lax.all_gather(shards[2], "fsdp", axis=0, tiled=True),
            lax.all_gather(shards[3], "fsdp", axis=0, tiled=True),
            lax.all_gather(shards[4], "fsdp", axis=0, tiled=True),
            lax.all_gather(shards[5], "fsdp", axis=0, tiled=True),
            lax.all_gather(shards[6], "fsdp", axis=0, tiled=True),
            lax.all_gather(shards[7], "fsdp", axis=1, tiled=True),
            lax.all_gather(shards[8], "fsdp", axis=1, tiled=True),
            lax.all_gather(shards[9], "fsdp", axis=1, tiled=True),
        )
        (
            query_full,
            key_full,
            value_full,
            cross_query,
            cross_key,
            cross_value,
            up_full,
            out_full,
            cross_out,
            down_full,
        ) = gathered
        upstream = cotangent[micro].astype(jnp.float32)
        grad_rows = spread_grads(upstream.astype(jnp.bfloat16))
        grad_down = weight_grad(active, grad_rows)
        grad_active = project_back(grad_rows, down_full)
        _, gelu_pull = jax.vjp(jax.nn.gelu, hidden)
        grad_hidden = gelu_pull(grad_active)[0].astype(jnp.bfloat16)
        grad_up = weight_grad(rows_three, grad_hidden)
        grad_three = fold_grads(project_back(grad_hidden, up_full))
        back_three, gain_g3, bias_g3 = norm_back(
            grad_three, scaled_three, inverse_three, gain_three
        )
        upstream = upstream + back_three
        grad_rows = spread_grads(upstream.astype(jnp.bfloat16))
        grad_cout = weight_grad(mixed_two, grad_rows)
        grad_mixed = project_back(grad_rows, cross_out).astype(jnp.bfloat16).reshape(head_shape)
        grad_cq, grad_ck, grad_cv, _ = attention_backward(
            cross_q, cross_k, cross_v, visible, total_two, grad_mixed
        )
        grad_cq = grad_cq.astype(jnp.bfloat16).reshape(clips, shard_frames, local_width)
        grad_ck = grad_ck.reshape(clips, text_slots, local_width)
        grad_cv = grad_cv.reshape(clips, text_slots, local_width)
        grad_cquery = weight_grad(rows_two, grad_cq)
        text_wide = text_rows.astype(jnp.float32)
        grad_ckey = jnp.einsum("cmd,cme->de", text_wide, grad_ck, precision=PRECISE)
        grad_cvalue = jnp.einsum("cmd,cme->de", text_wide, grad_cv, precision=PRECISE)
        text_grads.append(
            jnp.einsum("cme,de->cmd", grad_ck, cross_key.astype(jnp.float32), precision=PRECISE)
            + jnp.einsum("cme,de->cmd", grad_cv, cross_value.astype(jnp.float32), precision=PRECISE)
        )
        grad_two = fold_grads(project_back(grad_cq, cross_query))
        back_two, gain_g2, bias_g2 = norm_back(grad_two, scaled_two, inverse_two, gain_two)
        upstream = upstream + back_two
        grad_rows = spread_grads(upstream.astype(jnp.bfloat16))
        grad_out = weight_grad(mixed_one, grad_rows)
        grad_mixed = project_back(grad_rows, out_full).astype(jnp.bfloat16).reshape(head_shape)
        grad_q, grad_kall, grad_vall, _ = attention_backward(
            queries, key_all, value_all, causal, total_one, grad_mixed
        )
        grad_kloc, grad_vloc = (
            lax.psum_scatter(
                grad_kall.reshape(clips, -1, local_width).astype(jnp.bfloat16),
                "fsdp",
                scatter_dimension=1,
                tiled=True,
            ).astype(jnp.float32),
            lax.psum_scatter(
                grad_vall.reshape(clips, -1, local_width).astype(jnp.bfloat16),
                "fsdp",
                scatter_dimension=1,
                tiled=True,
            ).astype(jnp.float32),
        )
        grad_q = grad_q.astype(jnp.bfloat16).reshape(clips, shard_frames, local_width)
        grad_kloc = grad_kloc.astype(jnp.bfloat16)
        grad_vloc = grad_vloc.astype(jnp.bfloat16)
        grad_query = weight_grad(rows_one, grad_q)
        grad_key = weight_grad(rows_one, grad_kloc)
        grad_value = weight_grad(rows_one, grad_vloc)
        grad_one = fold_grads(
            project_back(grad_q, query_full)
            + project_back(grad_kloc, key_full)
            + project_back(grad_vloc, value_full)
        )
        back_one, gain_g1, bias_g1 = norm_back(grad_one, scaled_one, inverse_one, gain_one)
        input_grads.append(upstream + back_one)
        norm_parts = (gain_g1, bias_g1, gain_g2, bias_g2, gain_g3, bias_g3)
        norm_totals = norm_parts if micro == 0 else jax.tree.map(jnp.add, norm_totals, norm_parts)
        micro_grads = (
            grad_query,
            grad_key,
            grad_value,
            grad_cquery,
            grad_ckey,
            grad_cvalue,
            grad_up,
            grad_out,
            grad_cout,
            grad_down,
        )
        weight_total = (
            micro_grads if micro == 0 else jax.tree.map(jnp.add, weight_total, micro_grads)
        )
    weight_total = (
        lax.psum_scatter(
            weight_total[0].astype(jnp.bfloat16), "fsdp", scatter_dimension=0, tiled=True
        ).astype(jnp.float32),
        lax.psum_scatter(
            weight_total[1].astype(jnp.bfloat16), "fsdp", scatter_dimension=0, tiled=True
        ).astype(jnp.float32),
        lax.psum_scatter(
            weight_total[2].astype(jnp.bfloat16), "fsdp", scatter_dimension=0, tiled=True
        ).astype(jnp.float32),
        lax.psum_scatter(
            weight_total[3].astype(jnp.bfloat16), "fsdp", scatter_dimension=0, tiled=True
        ).astype(jnp.float32),
        lax.psum_scatter(
            weight_total[4].astype(jnp.bfloat16), "fsdp", scatter_dimension=0, tiled=True
        ).astype(jnp.float32),
        lax.psum_scatter(
            weight_total[5].astype(jnp.bfloat16), "fsdp", scatter_dimension=0, tiled=True
        ).astype(jnp.float32),
        lax.psum_scatter(
            weight_total[6].astype(jnp.bfloat16), "fsdp", scatter_dimension=0, tiled=True
        ).astype(jnp.float32),
        lax.psum_scatter(
            weight_total[7].astype(jnp.bfloat16), "fsdp", scatter_dimension=1, tiled=True
        ).astype(jnp.float32),
        lax.psum_scatter(
            weight_total[8].astype(jnp.bfloat16), "fsdp", scatter_dimension=1, tiled=True
        ).astype(jnp.float32),
        lax.psum_scatter(
            weight_total[9].astype(jnp.bfloat16), "fsdp", scatter_dimension=1, tiled=True
        ).astype(jnp.float32),
    )
    summed = lax.psum(
        (
            jnp.stack(text_grads),
            norm_totals[0],
            norm_totals[1],
            norm_totals[2],
            norm_totals[3],
            norm_totals[4],
            norm_totals[5],
        ),
        ("fsdp", "tp"),
    )
    (
        fin_query,
        fin_key,
        fin_value,
        fin_cquery,
        fin_ckey,
        fin_cvalue,
        fin_up,
        fin_out,
        fin_cout,
        fin_down,
    ) = weight_total
    return (
        jnp.stack(outputs),
        jnp.stack(input_grads),
        summed[0],
        summed[1],
        summed[2],
        summed[3],
        summed[4],
        summed[5],
        summed[6],
        fin_query,
        fin_key,
        fin_value,
        fin_out,
        fin_cquery,
        fin_ckey,
        fin_cvalue,
        fin_cout,
        fin_up,
        fin_down,
    )


def pair_swap(values, axis_name):
    return lax.ppermute(values, axis_name, [(0, 1), (1, 0)])


def ring_shift(values, distance):
    size = lax.axis_size("z")
    return lax.ppermute(values, "z", [(i, (i + distance) % size) for i in range(size)])


def ring_flip(values, bit):
    size = lax.axis_size("z")
    return lax.ppermute(values, "z", [(i, i ^ bit) for i in range(size)])


def take(values, index, axis=0):
    return lax.dynamic_index_in_dim(values, index, axis, keepdims=False)


def place(values, piece, index, axis):
    return lax.dynamic_update_index_in_dim(values, piece, index, axis)


def ordered(index, own, other):
    return jnp.where(index == 0, jnp.stack([own, other]), jnp.stack([other, own]))


def to_clip(values):
    at_y, at_z, size = lax.axis_index("y"), lax.axis_index("z"), lax.axis_size("z")
    got = pair_swap(take(values, 1 - at_y), "y")
    rows = ordered(at_y, take(values, at_y), got)
    out = rows
    for distance in range(1, size):
        piece = ring_shift(take(rows, lax.rem(at_z + distance, size), 1), distance)
        out = place(out, piece, lax.rem(at_z + size - distance, size), 1)
    return out


def from_clip(values):
    at_y, at_z, size = lax.axis_index("y"), lax.axis_index("z"), lax.axis_size("z")
    out = values
    for distance in range(1, size):
        piece = ring_shift(take(values, lax.rem(at_z + distance, size), 1), distance)
        out = place(out, piece, lax.rem(at_z + size - distance, size), 1)
    got = pair_swap(take(out, 1 - at_y), "y")
    return ordered(at_y, take(out, at_y), got)


def group_rows(values):
    at_x, at_c = lax.axis_index("x"), lax.axis_index("c")
    across = pair_swap(values, "x")
    near = ordered(at_c, values, pair_swap(values, "c"))
    far = ordered(at_c, across, pair_swap(across, "c"))
    whole = ordered(at_x, near, far)
    return jnp.transpose(whole, (2, 0, 1, 3, 4)).reshape(-1, values.shape[-1])


def group_sum(values):
    at_x, at_c = lax.axis_index("x"), lax.axis_index("c")
    parts = values.astype(jnp.bfloat16).reshape(2, 2, 2, -1, values.shape[-1])
    far_mine = take(take(parts, 1 - at_x, 1), at_c, 1)
    far_send = take(take(parts, 1 - at_x, 1), 1 - at_c, 1)
    near_mine = take(take(parts, at_x, 1), at_c, 1)
    near_send = take(take(parts, at_x, 1), 1 - at_c, 1)
    far = far_mine.astype(jnp.float32) + pair_swap(far_send, "c").astype(jnp.float32)
    got = pair_swap(far.astype(jnp.bfloat16), "x")
    near = near_mine.astype(jnp.float32) + pair_swap(near_send, "c").astype(jnp.float32)
    return near + got.astype(jnp.float32)


def ring_gather(own):
    at_z, size = lax.axis_index("z"), lax.axis_size("z")
    out = place(jnp.zeros((size,) + own.shape, own.dtype), own, at_z, 0)
    piece = own
    for distance in range(1, size):
        piece = ring_shift(piece, 1)
        out = place(out, piece, lax.rem(at_z + size - distance, size), 0)
    return out


def ring_sum(parts):
    at_z, size = lax.axis_index("z"), lax.axis_size("z")
    moving = take(parts, lax.rem(at_z + size - 1, size))
    for step in range(1, size):
        got = ring_shift(moving, 1)
        mine = take(parts, lax.rem(at_z + 2 * size - 1 - step, size))
        total = got.astype(jnp.float32) + mine.astype(jnp.float32)
        moving = total.astype(jnp.bfloat16)
    return total


def gather_units(shard, count):
    at_y, at_x, at_c = lax.axis_index("y"), lax.axis_index("x"), lax.axis_index("c")
    rows = shard.shape[0]
    width = shard.shape[1] // count // 2
    split = jnp.transpose(shard.reshape(rows, count, 2, width), (2, 1, 0, 3))
    mine = ordered(at_x, take(split, at_x), pair_swap(take(split, 1 - at_x), "x"))
    ring = ring_gather(mine)
    size = ring.shape[0]
    across = pair_swap(ring, "y")

    def halves(values):
        by_core = values.reshape((2, size // 2) + values.shape[1:])
        return ordered(at_c, take(by_core, at_c), pair_swap(take(by_core, 1 - at_c), "c"))

    whole = ordered(at_y, halves(ring), halves(across))
    whole = jnp.transpose(whole, (0, 3, 1, 5, 4, 2, 6))
    return whole.reshape(8 * rows, count, (size // 2) * width)


def sum_units(grad):
    at_y, at_x, at_c = lax.axis_index("y"), lax.axis_index("x"), lax.axis_index("c")
    size = lax.axis_size("z")
    dim, count, units = grad.shape
    rows = dim // 8
    width = units // (size // 2)
    parts = grad.astype(jnp.bfloat16).reshape(2, 2, 2, rows, count, size // 2, width)
    parts = jnp.transpose(parts, (2, 0, 5, 1, 4, 3, 6))
    mine, away = take(parts, at_c), pair_swap(take(parts, 1 - at_c), "c")
    whole = ordered(at_c, mine, away)
    whole = jnp.swapaxes(whole, 0, 1)
    got = pair_swap(take(whole, 1 - at_y), "y").astype(jnp.float32)
    total = (take(whole, at_y).astype(jnp.float32) + got).astype(jnp.bfloat16)
    total = ring_sum(total.reshape((size,) + total.shape[2:])).astype(jnp.bfloat16)
    mine, away = take(total, at_x), pair_swap(take(total, 1 - at_x), "x")
    halves = ordered(at_x, mine, away)
    return jnp.transpose(halves, (2, 1, 0, 3)).reshape(rows, -1).astype(jnp.float32)


def gather_whole(shard, count):
    at_y, at_x, at_c = lax.axis_index("y"), lax.axis_index("x"), lax.axis_index("c")
    rows = shard.shape[0]
    width = shard.shape[1] // count
    ring = ring_gather(jnp.transpose(shard.reshape(rows, count, width), (1, 0, 2)))
    pair = ordered(at_y, ring, pair_swap(ring, "y"))
    quad = ordered(at_x, pair, pair_swap(pair, "x"))
    whole = ordered(at_c, quad, pair_swap(quad, "c"))
    whole = jnp.transpose(whole, (4, 2, 1, 0, 5, 3, 6))
    return whole.reshape(count, 8 * rows, -1)


def sum_whole(grads):
    at_y, at_x, at_c = lax.axis_index("y"), lax.axis_index("x"), lax.axis_index("c")
    size = lax.axis_size("z")
    count, dim, units = grads.shape
    rows = dim // 8
    parts = grads.astype(jnp.bfloat16).reshape(count, 2, 2, 2, rows, size, units // size)
    parts = jnp.transpose(parts, (3, 2, 1, 5, 0, 4, 6))

    def fold(values, at, name):
        got = pair_swap(take(values, 1 - at), name).astype(jnp.float32)
        return (take(values, at).astype(jnp.float32) + got).astype(jnp.bfloat16)

    parts = fold(fold(fold(parts, at_c, "c"), at_x, "x"), at_y, "y")
    total = ring_sum(parts)
    return jnp.transpose(total, (1, 0, 2)).reshape(rows, -1)


def everywhere(values):
    for name in ("c", "x", "y"):
        values = values + pair_swap(values, name)
    bit = 1
    while bit < lax.axis_size("z"):
        values = values + ring_flip(values, bit)
        bit *= 2
    return values


def dot_nt(left, right):
    return lax.dot_general(left, right, (((1,), (1,)), ((), ())), preferred_element_type=jnp.float32)


def dot_nn(left, right):
    return lax.dot_general(left, right, (((1,), (0,)), ((), ())), preferred_element_type=jnp.float32)


def dot_tn(left, right):
    return lax.dot_general(left, right, (((0,), (0,)), ((), ())), preferred_element_type=jnp.float32)


BLOCK = 256


def diagonal_mask(size):
    row = lax.broadcasted_iota(jnp.int32, (size, size), 0)
    column = lax.broadcasted_iota(jnp.int32, (size, size), 1)
    return column <= row


def self_forward_kernel(q_ref, k_ref, v_ref, o_ref, l_ref):
    frames = q_ref.shape[0]
    mask = diagonal_mask(BLOCK)
    for head in range(2):
        lanes = slice(head * HD, (head + 1) * HD)
        for at in range(0, frames, BLOCK):
            rows = slice(at, at + BLOCK)
            q = q_ref[rows, lanes] * jnp.bfloat16(1.0 / math.sqrt(HD))
            near = jnp.where(mask, dot_nt(q, k_ref[rows, lanes]), MASKED)
            top = jnp.max(near, axis=-1, keepdims=True)
            if at:
                past = dot_nt(q, k_ref[0:at, lanes])
                top = jnp.maximum(top, jnp.max(past, axis=-1, keepdims=True))
            near = jnp.exp(near - top)
            total = jnp.sum(near, axis=-1, keepdims=True)
            out = dot_nn(near.astype(jnp.bfloat16), v_ref[rows, lanes])
            if at:
                past = jnp.exp(past - top)
                total = total + jnp.sum(past, axis=-1, keepdims=True)
                out = out + dot_nn(past.astype(jnp.bfloat16), v_ref[0:at, lanes])
            o_ref[rows, lanes] = (out / total).astype(jnp.bfloat16)
            l_ref[rows, lanes] = jnp.broadcast_to(top + jnp.log(total), (BLOCK, HD))


def self_backward_kernel(
    q_ref, k_ref, v_ref, o_ref, l_ref, g_ref, dq_ref, dk_ref, dv_ref, dk_sum, dv_sum
):
    frames = q_ref.shape[0]
    mask = diagonal_mask(BLOCK)
    factor = 1.0 / math.sqrt(HD)
    dk_sum[...] = jnp.zeros_like(dk_sum)
    dv_sum[...] = jnp.zeros_like(dv_sum)
    for head in range(2):
        lanes = slice(head * HD, (head + 1) * HD)
        for at in range(0, frames, BLOCK):
            rows = slice(at, at + BLOCK)
            q = q_ref[rows, lanes] * jnp.bfloat16(factor)
            grad = g_ref[rows, lanes]
            q_turned = q.astype(jnp.float32).T.astype(jnp.bfloat16)
            grad_turned = grad.astype(jnp.float32).T.astype(jnp.bfloat16)
            log_total = l_ref[rows, lanes][:, 0:1]
            row_total = jnp.sum(
                grad.astype(jnp.float32) * o_ref[rows, lanes].astype(jnp.float32),
                axis=-1,
                keepdims=True,
            )
            dq = None
            for columns in (rows, slice(0, at)):
                if columns.stop == 0:
                    continue
                keys = k_ref[columns, lanes]
                weights = jnp.exp(dot_nt(q, keys) - log_total)
                if columns is rows:
                    weights = jnp.where(mask, weights, 0.0)
                back = dot_nt(grad, v_ref[columns, lanes])
                scores = (weights * (back - row_total)).astype(jnp.bfloat16)
                part = dot_nn(scores, keys)
                dq = part if dq is None else dq + part
                dk_sum[lanes, columns] += dot_nn(q_turned, scores)
                dv_sum[lanes, columns] += dot_nn(grad_turned, weights.astype(jnp.bfloat16))
            dq_ref[rows, lanes] = (dq * factor).astype(jnp.bfloat16)
    for at in range(0, frames, BLOCK):
        rows = slice(at, at + BLOCK)
        dk_ref[rows, :] = dk_sum[:, rows].T.astype(jnp.bfloat16)
        dv_ref[rows, :] = dv_sum[:, rows].T.astype(jnp.bfloat16)


def pair_spec(rows, offset=0):
    return pl.BlockSpec((rows, 2 * HD), lambda i: (0, i + offset))


def self_forward(qkv):
    frames, width = qkv.shape[0], qkv.shape[1] // 3
    pairs = width // (2 * HD)
    cost = pl.CostEstimate(
        flops=8 * frames * frames * width, bytes_accessed=14 * frames * width, transcendentals=0
    )
    return pl.pallas_call(
        self_forward_kernel,
        grid=(pairs,),
        in_specs=[pair_spec(frames, i * pairs) for i in range(3)],
        out_specs=[pair_spec(frames)] * 2,
        out_shape=[
            jax.ShapeDtypeStruct((frames, width), jnp.bfloat16),
            jax.ShapeDtypeStruct((frames, width), jnp.float32),
        ],
        compiler_params=pltpu.CompilerParams(vmem_limit_bytes=40 * 2**20),
        cost_estimate=cost,
    )(qkv, qkv, qkv)


def self_backward(qkv, mixed, log_total, grad_mixed):
    frames, width = mixed.shape
    pairs = width // (2 * HD)
    cost = pl.CostEstimate(
        flops=20 * frames * frames * width, bytes_accessed=20 * frames * width, transcendentals=0
    )
    return pl.pallas_call(
        self_backward_kernel,
        grid=(pairs,),
        in_specs=[pair_spec(frames, i * pairs) for i in range(3)] + [pair_spec(frames)] * 3,
        out_specs=[pair_spec(frames)] * 3,
        out_shape=[jax.ShapeDtypeStruct((frames, width), jnp.bfloat16)] * 3,
        scratch_shapes=[pltpu.VMEM((2 * HD, frames), jnp.float32)] * 2,
        compiler_params=pltpu.CompilerParams(vmem_limit_bytes=40 * 2**20),
        cost_estimate=cost,
    )(qkv, qkv, qkv, mixed, log_total, grad_mixed)


def block_pair(values):
    low = lax.broadcasted_iota(jnp.int32, values.shape, 1) < HD
    zero = jnp.zeros_like(values)
    return jnp.concatenate([jnp.where(low, values, zero), jnp.where(low, zero, values)], axis=0)


def by_half(low, values, reduce, empty):
    first = reduce(jnp.where(low, values, empty), axis=-1, keepdims=True)
    second = reduce(jnp.where(low, empty, values), axis=-1, keepdims=True)
    return jnp.where(low, first, second)


def cross_weights(count, queries, keys):
    slots = keys.shape[0] // 2
    scores = dot_nt(queries, keys)
    lane = lax.broadcasted_iota(jnp.int32, scores.shape, 1)
    low = lane < slots
    scores = jnp.where(jnp.where(low, lane, lane - slots) < count, scores, MASKED)
    raised = jnp.exp(scores - by_half(low, scores, jnp.max, MASKED))
    return raised / by_half(low, raised, jnp.sum, 0.0), low


def cross_forward_kernel(count_ref, q_ref, k_ref, v_ref, o_ref):
    queries = q_ref[...] * jnp.bfloat16(1.0 / math.sqrt(HD))
    weights, _ = cross_weights(count_ref[0], queries, block_pair(k_ref[...]))
    o_ref[...] = dot_nn(weights.astype(jnp.bfloat16), block_pair(v_ref[...])).astype(jnp.bfloat16)


def cross_backward_kernel(count_ref, q_ref, k_ref, v_ref, g_ref, dq_ref, dk_ref, dv_ref):
    factor = 1.0 / math.sqrt(HD)
    queries = q_ref[...] * jnp.bfloat16(factor)
    keys = block_pair(k_ref[...])
    weights, low = cross_weights(count_ref[0], queries, keys)
    grad = g_ref[...]
    back = dot_nt(grad, block_pair(v_ref[...]))
    scores = weights * (back - by_half(low, back * weights, jnp.sum, 0.0))
    scores = scores.astype(jnp.bfloat16)
    dq_ref[...] = (dot_nn(scores, keys) * factor).astype(jnp.bfloat16)
    slots = k_ref.shape[0]
    dims_low = lax.broadcasted_iota(jnp.int32, k_ref.shape, 1) < HD
    dk = dot_tn(scores, queries)
    dk_ref[...] = jnp.where(dims_low, dk[:slots], dk[slots:])
    dv = dot_tn(weights.astype(jnp.bfloat16), grad)
    dv_ref[...] = jnp.where(dims_low, dv[:slots], dv[slots:])


def cross_forward(count, queries, keys_values):
    rows, width = queries.shape
    slots = keys_values.shape[0]
    pairs = width // (2 * HD)
    return pl.pallas_call(
        cross_forward_kernel,
        grid=(pairs,),
        in_specs=[
            pl.BlockSpec(memory_space=pltpu.SMEM),
            pair_spec(rows),
            pair_spec(slots),
            pair_spec(slots, pairs),
        ],
        out_specs=pair_spec(rows),
        out_shape=jax.ShapeDtypeStruct((rows, width), jnp.bfloat16),
        cost_estimate=pl.CostEstimate(
            flops=8 * rows * slots * width, bytes_accessed=6 * rows * width, transcendentals=0
        ),
    )(count, queries, keys_values, keys_values)


def cross_backward(count, queries, keys_values, grad_mixed):
    rows, width = queries.shape
    slots = keys_values.shape[0]
    pairs = width // (2 * HD)
    return pl.pallas_call(
        cross_backward_kernel,
        grid=(pairs,),
        in_specs=[
            pl.BlockSpec(memory_space=pltpu.SMEM),
            pair_spec(rows),
            pair_spec(slots),
            pair_spec(slots, pairs),
            pair_spec(rows),
        ],
        out_specs=[pair_spec(rows), pair_spec(slots), pair_spec(slots)],
        out_shape=[
            jax.ShapeDtypeStruct((rows, width), jnp.bfloat16),
            jax.ShapeDtypeStruct((slots, width), jnp.float32),
            jax.ShapeDtypeStruct((slots, width), jnp.float32),
        ],
        cost_estimate=pl.CostEstimate(
            flops=20 * rows * slots * width, bytes_accessed=10 * rows * width, transcendentals=0
        ),
    )(count, queries, keys_values, keys_values, grad_mixed)


def clip_body(
    tokens,
    memory,
    text_len,
    cotangent,
    gain_one,
    bias_one,
    gain_two,
    bias_two,
    gain_three,
    bias_three,
    w_query,
    w_key,
    w_value,
    w_out,
    c_query,
    c_key,
    c_value,
    c_out,
    w_up,
    w_down,
):
    at_y, at_x, at_c, at_z = (lax.axis_index(name) for name in ("y", "x", "c", "z"))
    model = tokens.shape[-1]
    shard_rows, shard_width = w_query.shape
    slots = memory.shape[2]

    frames = to_clip(tokens).reshape(2, -1, model).astype(jnp.float32)
    attend_shard = jnp.concatenate([w_query, w_key, w_value, w_out.T], axis=1)
    attend_full = gather_units(attend_shard, 4)
    qkv_full = attend_full[:, :3].reshape(model, -1)
    out_full = attend_full[:, 3]
    cross_full = gather_whole(jnp.concatenate([c_query, c_out.T], axis=1), 2)
    cross_query, cross_out = cross_full[0], cross_full[1]
    up_full = gather_units(w_up, 1)[:, 0]
    down_full = gather_units(w_down.T, 1)[:, 0]
    upstream = to_clip(cotangent).reshape(2, -1, model)
    grad_rows3 = group_rows(upstream)

    at_f = (at_y * 2 + at_x) * 2 + at_c
    text_flat = memory.reshape(-1, model)
    text_mine = lax.dynamic_slice_in_dim(text_flat, at_f * shard_rows, shard_rows, 1)
    text_shard = jnp.concatenate([c_key, c_value], axis=1)
    text_part = dot_nn(text_mine, text_shard).astype(jnp.bfloat16)
    text_part = text_part.reshape(2, -1, slots, 2 * shard_width)
    got = pair_swap(take(text_part, 1 - at_y), "y").astype(jnp.float32)
    text_part = (take(text_part, at_y).astype(jnp.float32) + got).astype(jnp.bfloat16)
    size = text_part.shape[0]
    text_clip = text_part
    for distance in range(1, size):
        piece = ring_shift(take(text_part, lax.rem(at_z + distance, size)), distance)
        text_clip = place(text_clip, piece, lax.rem(at_z + size - distance, size), 0)
    text_clip = text_clip.astype(jnp.float32)
    for name in ("x", "c"):
        text_clip = text_clip.astype(jnp.bfloat16)
        text_clip = text_clip.astype(jnp.float32) + pair_swap(text_clip, name).astype(jnp.float32)
    text_clip = text_clip.astype(jnp.bfloat16).reshape(size, slots, 2, shard_width)
    keys_values = jnp.transpose(text_clip, (1, 2, 0, 3)).reshape(slots, -1)
    count = take(take(text_len, at_y), at_z).reshape(1)

    normed_one, scaled_one, inverse_one = layer_norm(frames, gain_one, bias_one)
    rows_one = group_rows(normed_one.astype(jnp.bfloat16))
    qkv = dot_nn(rows_one, qkv_full).astype(jnp.bfloat16)
    mixed_one, log_total = self_forward(qkv)
    after_self = frames + group_sum(dot_nt(mixed_one, out_full))
    normed_two, scaled_two, inverse_two = layer_norm(after_self, gain_two, bias_two)
    rows_two = normed_two.astype(jnp.bfloat16).reshape(-1, model)
    cross_q = dot_nn(rows_two, cross_query).astype(jnp.bfloat16)
    mixed_two = cross_forward(count, cross_q, keys_values)
    after_cross = after_self + dot_nt(mixed_two, cross_out).reshape(after_self.shape)
    normed_three, scaled_three, inverse_three = layer_norm(after_cross, gain_three, bias_three)
    rows_three = group_rows(normed_three.astype(jnp.bfloat16))
    hidden = dot_nn(rows_three, up_full)
    active = jax.nn.gelu(hidden).astype(jnp.bfloat16)

    grad_active = dot_nn(grad_rows3, down_full)
    _, gelu_pull = jax.vjp(jax.nn.gelu, hidden)
    grad_hidden = gelu_pull(grad_active)[0].astype(jnp.bfloat16)
    grad_three = group_sum(dot_nt(grad_hidden, up_full))
    back_three, gain_g3, bias_g3 = norm_back(grad_three, scaled_three, inverse_three, gain_three)
    grad_two_rows = upstream.astype(jnp.float32) + back_three
    fin_down = sum_units(dot_tn(grad_rows3, active)[:, None])
    fin_up = sum_units(dot_tn(rows_three, grad_hidden)[:, None])

    result = after_cross + group_sum(dot_nt(active, down_full))
    result = from_clip(result.astype(jnp.bfloat16).reshape(2, size, -1, model))

    grad_rows2 = grad_two_rows.astype(jnp.bfloat16).reshape(-1, model)
    grad_mixed2 = dot_nn(grad_rows2, cross_out).astype(jnp.bfloat16)
    grad_cq, grad_ck, grad_cv = cross_backward(count, cross_q, keys_values, grad_mixed2)
    grad_two = dot_nt(grad_cq, cross_query).reshape(after_self.shape)
    back_two, gain_g2, bias_g2 = norm_back(grad_two, scaled_two, inverse_two, gain_two)
    grad_one_rows = grad_two_rows + back_two
    fin_cross = sum_whole(jnp.stack([dot_tn(rows_two, grad_cq), dot_tn(grad_rows2, mixed_two)]))
    fin_cquery, fin_cout = fin_cross[:, :shard_width], fin_cross[:, shard_width:].T

    grad_text = jnp.stack([grad_ck, grad_cv]).reshape(2, slots, size, shard_width)
    grad_text = jnp.transpose(grad_text, (2, 1, 0, 3)).reshape(size, slots, 2 * shard_width)
    for name in ("x", "c"):
        grad_text = grad_text.astype(jnp.bfloat16)
        grad_text = grad_text.astype(jnp.float32) + pair_swap(grad_text, name).astype(jnp.float32)
    grad_text = grad_text.astype(jnp.bfloat16)
    spread = grad_text
    for distance in range(1, size):
        piece = ring_shift(take(grad_text, lax.rem(at_z + distance, size)), distance)
        spread = place(spread, piece, lax.rem(at_z + size - distance, size), 0)
    spread = ordered(at_y, spread, pair_swap(spread, "y")).reshape(-1, 2 * shard_width)
    fin_text = dot_tn(text_mine, spread)
    fin_ckey, fin_cvalue = fin_text[:, :shard_width], fin_text[:, shard_width:]
    grad_memory = dot_nt(spread, text_shard)
    bit = 1
    while bit < size:
        grad_memory = grad_memory.astype(jnp.bfloat16)
        grad_memory = grad_memory.astype(jnp.float32) + ring_flip(grad_memory, bit).astype(
            jnp.float32
        )
        bit *= 2
    grad_memory = grad_memory.astype(jnp.bfloat16)
    for at, name in ((at_c, "c"), (at_x, "x"), (at_y, "y")):
        grad_memory = ordered(at, grad_memory, pair_swap(grad_memory, name))
    grad_memory = jnp.transpose(grad_memory.reshape(8, -1, shard_rows), (1, 0, 2))
    grad_memory = grad_memory.reshape(memory.shape).astype(jnp.float32)

    grad_rows1 = group_rows(grad_one_rows.astype(jnp.bfloat16))
    grad_mixed1 = dot_nn(grad_rows1, out_full).astype(jnp.bfloat16)
    grad_q, grad_k, grad_v = self_backward(qkv, mixed_one, log_total, grad_mixed1)
    grad_qkv = jnp.concatenate([grad_q, grad_k, grad_v], axis=1)
    grad_one = group_sum(dot_nt(grad_qkv, qkv_full))
    back_one, gain_g1, bias_g1 = norm_back(grad_one, scaled_one, inverse_one, gain_one)
    input_grad = (grad_one_rows + back_one).astype(jnp.bfloat16)
    input_grad = from_clip(input_grad.reshape(2, size, -1, model)).astype(jnp.float32)
    grad_attend = jnp.concatenate(
        [dot_tn(rows_one, grad_qkv), dot_tn(grad_rows1, mixed_one)], axis=1
    )
    fin_attend = sum_units(grad_attend.reshape(model, 4, -1))
    fin_query, fin_key, fin_value, fin_out = (
        fin_attend[:, i * shard_width : (i + 1) * shard_width] for i in range(4)
    )

    early = everywhere(jnp.stack([gain_g2, bias_g2, gain_g3, bias_g3]))
    late = everywhere(jnp.stack([gain_g1, bias_g1]))
    return (
        result,
        input_grad,
        grad_memory,
        late[0],
        late[1],
        early[0],
        early[1],
        early[2],
        early[3],
        fin_query,
        fin_key,
        fin_value,
        fin_out.T,
        fin_cquery,
        fin_ckey,
        fin_cvalue,
        fin_cout,
        fin_up,
        fin_down.T,
    )


def clip_groups(mesh):
    outer, inner = mesh.shape["fsdp"], mesh.shape["tp"]
    return (2, 2, 2, inner) if outer == 8 and inner == 4 else None


def solution(mesh):
    sizes = clip_groups(mesh)
    if sizes is None:
        rows, columns, program, used = "fsdp", "tp", body, mesh
    else:
        rows, columns, program = ("y", "x", "c"), "z", clip_body
        used = jax.sharding.Mesh(mesh.devices.reshape(sizes), ("y", "x", "c", "z"))
    both = ("fsdp", "tp") if sizes is None else ("y", "x", "c", "z")
    frames = P(None, None, both, None)
    tall, wide = P(rows, columns), P(columns, rows)
    weights = (tall, tall, tall, wide, tall, tall, tall, wide, tall, wide)
    return jax.shard_map(
        program,
        mesh=used,
        in_specs=(frames, P(), P(), frames) + (P(),) * 6 + weights,
        out_specs=(frames, frames, P()) + (P(),) * 6 + weights,
        check_vma=False,
    )
```

```python
import math

import jax
import jax.numpy as jnp
from jax import lax
from jax.experimental import pallas as pl
from jax.experimental.pallas import tpu as pltpu
from jax.sharding import PartitionSpec as P

HD = 64
MICRO = 2


EPSILON = 1e-05
PRECISE = lax.Precision.HIGHEST
MASKED = -1e30


def layer_norm(values, gain_vec, bias_vec):
    center = values - jnp.mean(values, axis=-1, keepdims=True)
    inverse = lax.rsqrt(jnp.mean(center * center, axis=-1, keepdims=True) + EPSILON)
    scaled = center * inverse
    return (scaled * gain_vec + bias_vec, scaled, inverse)


def norm_back(upstream, scaled, inverse, gain_vec):
    weighted = upstream * gain_vec
    result = inverse * (
        weighted
        - jnp.mean(weighted, axis=-1, keepdims=True)
        - scaled * jnp.mean(weighted * scaled, axis=-1, keepdims=True)
    )
    return (result, jnp.sum(upstream * scaled, axis=(0, 1)), jnp.sum(upstream, axis=(0, 1)))


def spread_rows(values):
    return lax.all_gather(values, "tp", axis=1, tiled=True)


def spread_grads(values):
    return lax.all_gather(values, "tp", axis=1, tiled=True)


def fold_rows(values):
    return lax.psum_scatter(values, "tp", scatter_dimension=1, tiled=True)


def fold_grads(values):
    return lax.psum_scatter(values, "tp", scatter_dimension=1, tiled=True)


def project(left_side, right_side):
    return jnp.einsum("cfd,de->cfe", left_side, right_side, preferred_element_type=jnp.float32)


def project_back(left_side, right_side):
    return jnp.einsum("cfe,de->cfd", left_side, right_side, preferred_element_type=jnp.float32)


def weight_grad(left_side, right_side):
    return jnp.einsum("cfd,cfe->de", left_side, right_side, preferred_element_type=jnp.float32)


def masked_scores(queries, key_rows, allowed):
    factor = 1.0 / math.sqrt(queries.shape[-1])
    scores = (
        jnp.einsum("cqhe,ckhe->chqk", queries, key_rows, preferred_element_type=jnp.float32)
        * factor
    )
    return jnp.where(allowed, scores, MASKED)


def attention_forward(queries, key_rows, value_rows, allowed):
    scores = masked_scores(queries, key_rows, allowed)
    highest = jnp.max(scores, axis=-1, keepdims=True)
    log_total = highest + jnp.log(jnp.sum(jnp.exp(scores - highest), axis=-1, keepdims=True))
    weights = jnp.exp(scores - log_total).astype(jnp.bfloat16)
    mixed = jnp.einsum("chqk,ckhe->cqhe", weights, value_rows, preferred_element_type=jnp.float32)
    return (mixed, log_total)


def score_grads(queries, key_rows, value_rows, allowed, log_total, grad_mixed):
    weights = jnp.exp(masked_scores(queries, key_rows, allowed) - log_total)
    grad_weights = jnp.einsum(
        "cqhe,ckhe->chqk", grad_mixed, value_rows, preferred_element_type=jnp.float32
    )
    row_total = jnp.sum(grad_weights * weights, axis=-1, keepdims=True)
    grad_scores = (weights * (grad_weights - row_total)).astype(jnp.bfloat16)
    return (weights, grad_scores, row_total)


def attention_backward(queries, key_rows, value_rows, allowed, log_total, grad_mixed):
    factor = 1.0 / math.sqrt(queries.shape[-1])
    weights, grad_scores, row_total = score_grads(
        queries, key_rows, value_rows, allowed, log_total, grad_mixed
    )
    grad_queries = (
        jnp.einsum("chqk,ckhe->cqhe", grad_scores, key_rows, preferred_element_type=jnp.float32)
        * factor
    )
    grad_keys = (
        jnp.einsum("chqk,cqhe->ckhe", grad_scores, queries, preferred_element_type=jnp.float32)
        * factor
    )
    grad_values = jnp.einsum(
        "chqk,cqhe->ckhe",
        weights.astype(jnp.bfloat16),
        grad_mixed,
        preferred_element_type=jnp.float32,
    )
    return (grad_queries, grad_keys, grad_values, row_total)


def body(
    tokens,
    memory,
    text_len,
    cotangent,
    gain_one,
    bias_one,
    gain_two,
    bias_two,
    gain_three,
    bias_three,
    w_query,
    w_key,
    w_value,
    w_out,
    c_query,
    c_key,
    c_value,
    c_out,
    w_up,
    w_down,
):
    clips = tokens.shape[1]
    shard_frames = tokens.shape[2] * lax.axis_size("tp")
    text_slots = memory.shape[2]
    local_width = w_query.shape[1]
    local_heads = local_width // HD
    query_pos = lax.axis_index("fsdp") * shard_frames + jnp.arange(shard_frames)
    key_pos = jnp.arange(shard_frames * lax.axis_size("fsdp"))
    causal = (key_pos[None, :] <= query_pos[:, None])[None, None]
    shards = (w_query, w_key, w_value, c_query, c_key, c_value, w_up, w_out, c_out, w_down)
    head_shape = (clips, shard_frames, local_heads, HD)
    text_shape = (clips, text_slots, local_heads, HD)
    outputs = []
    input_grads = []
    text_grads = []
    norm_totals = None
    weight_total = None
    for micro in range(MICRO):
        gathered = (
            lax.all_gather(shards[0], "fsdp", axis=0, tiled=True),
            lax.all_gather(shards[1], "fsdp", axis=0, tiled=True),
            lax.all_gather(shards[2], "fsdp", axis=0, tiled=True),
            lax.all_gather(shards[3], "fsdp", axis=0, tiled=True),
            lax.all_gather(shards[4], "fsdp", axis=0, tiled=True),
            lax.all_gather(shards[5], "fsdp", axis=0, tiled=True),
            lax.all_gather(shards[6], "fsdp", axis=0, tiled=True),
            lax.all_gather(shards[7], "fsdp", axis=1, tiled=True),
            lax.all_gather(shards[8], "fsdp", axis=1, tiled=True),
            lax.all_gather(shards[9], "fsdp", axis=1, tiled=True),
        )
        (
            query_full,
            key_full,
            value_full,
            cross_query,
            cross_key,
            cross_value,
            up_full,
            out_full,
            cross_out,
            down_full,
        ) = gathered
        frames = tokens[micro].astype(jnp.float32)
        text_rows = memory[micro]
        counts = text_len[micro]
        normed_one, scaled_one, inverse_one = layer_norm(frames, gain_one, bias_one)
        rows_one = spread_rows(normed_one.astype(jnp.bfloat16))
        queries = project(rows_one, query_full).astype(jnp.bfloat16).reshape(head_shape)
        key_local = project(rows_one, key_full).astype(jnp.bfloat16)
        value_local = project(rows_one, value_full).astype(jnp.bfloat16)
        key_all, value_all = (
            lax.all_gather(key_local, "fsdp", axis=1, tiled=True),
            lax.all_gather(value_local, "fsdp", axis=1, tiled=True),
        )
        key_all = key_all.reshape(clips, -1, local_heads, HD)
        value_all = value_all.reshape(clips, -1, local_heads, HD)
        mixed_one, total_one = attention_forward(queries, key_all, value_all, causal)
        mixed_one = mixed_one.astype(jnp.bfloat16).reshape(clips, shard_frames, local_width)
        after_self = frames + fold_rows(project(mixed_one, out_full))
        normed_two, scaled_two, inverse_two = layer_norm(after_self, gain_two, bias_two)
        rows_two = spread_rows(normed_two.astype(jnp.bfloat16))
        cross_q = project(rows_two, cross_query).astype(jnp.bfloat16).reshape(head_shape)
        cross_k = project(text_rows, cross_key).astype(jnp.bfloat16).reshape(text_shape)
        cross_v = project(text_rows, cross_value).astype(jnp.bfloat16).reshape(text_shape)
        visible = (jnp.arange(text_slots)[None, :] < counts[:, None])[:, None, None, :]
        mixed_two, total_two = attention_forward(cross_q, cross_k, cross_v, visible)
        mixed_two = mixed_two.astype(jnp.bfloat16).reshape(clips, shard_frames, local_width)
        after_cross = after_self + fold_rows(project(mixed_two, cross_out))
        normed_three, scaled_three, inverse_three = layer_norm(after_cross, gain_three, bias_three)
        rows_three = spread_rows(normed_three.astype(jnp.bfloat16))
        hidden = project(rows_three, up_full)
        active = jax.nn.gelu(hidden).astype(jnp.bfloat16)
        result = after_cross + fold_rows(project(active, down_full))
        outputs.append(result.astype(jnp.bfloat16))
        gathered = (
            lax.all_gather(shards[0], "fsdp", axis=0, tiled=True),
            lax.all_gather(shards[1], "fsdp", axis=0, tiled=True),
            lax.all_gather(shards[2], "fsdp", axis=0, tiled=True),
            lax.all_gather(shards[3], "fsdp", axis=0, tiled=True),
            lax.all_gather(shards[4], "fsdp", axis=0, tiled=True),
            lax.all_gather(shards[5], "fsdp", axis=0, tiled=True),
            lax.all_gather(shards[6], "fsdp", axis=0, tiled=True),
            lax.all_gather(shards[7], "fsdp", axis=1, tiled=True),
            lax.all_gather(shards[8], "fsdp", axis=1, tiled=True),
            lax.all_gather(shards[9], "fsdp", axis=1, tiled=True),
        )
        (
            query_full,
            key_full,
            value_full,
            cross_query,
            cross_key,
            cross_value,
            up_full,
            out_full,
            cross_out,
            down_full,
        ) = gathered
        upstream = cotangent[micro].astype(jnp.float32)
        grad_rows = spread_grads(upstream.astype(jnp.bfloat16))
        grad_down = weight_grad(active, grad_rows)
        grad_active = project_back(grad_rows, down_full)
        _, gelu_pull = jax.vjp(jax.nn.gelu, hidden)
        grad_hidden = gelu_pull(grad_active)[0].astype(jnp.bfloat16)
        grad_up = weight_grad(rows_three, grad_hidden)
        grad_three = fold_grads(project_back(grad_hidden, up_full))
        back_three, gain_g3, bias_g3 = norm_back(
            grad_three, scaled_three, inverse_three, gain_three
        )
        upstream = upstream + back_three
        grad_rows = spread_grads(upstream.astype(jnp.bfloat16))
        grad_cout = weight_grad(mixed_two, grad_rows)
        grad_mixed = project_back(grad_rows, cross_out).astype(jnp.bfloat16).reshape(head_shape)
        grad_cq, grad_ck, grad_cv, _ = attention_backward(
            cross_q, cross_k, cross_v, visible, total_two, grad_mixed
        )
        grad_cq = grad_cq.astype(jnp.bfloat16).reshape(clips, shard_frames, local_width)
        grad_ck = grad_ck.reshape(clips, text_slots, local_width)
        grad_cv = grad_cv.reshape(clips, text_slots, local_width)
        grad_cquery = weight_grad(rows_two, grad_cq)
        text_wide = text_rows.astype(jnp.float32)
        grad_ckey = jnp.einsum("cmd,cme->de", text_wide, grad_ck, precision=PRECISE)
        grad_cvalue = jnp.einsum("cmd,cme->de", text_wide, grad_cv, precision=PRECISE)
        text_grads.append(
            jnp.einsum("cme,de->cmd", grad_ck, cross_key.astype(jnp.float32), precision=PRECISE)
            + jnp.einsum("cme,de->cmd", grad_cv, cross_value.astype(jnp.float32), precision=PRECISE)
        )
        grad_two = fold_grads(project_back(grad_cq, cross_query))
        back_two, gain_g2, bias_g2 = norm_back(grad_two, scaled_two, inverse_two, gain_two)
        upstream = upstream + back_two
        grad_rows = spread_grads(upstream.astype(jnp.bfloat16))
        grad_out = weight_grad(mixed_one, grad_rows)
        grad_mixed = project_back(grad_rows, out_full).astype(jnp.bfloat16).reshape(head_shape)
        grad_q, grad_kall, grad_vall, _ = attention_backward(
            queries, key_all, value_all, causal, total_one, grad_mixed
        )
        grad_kloc, grad_vloc = (
            lax.psum_scatter(
                grad_kall.reshape(clips, -1, local_width).astype(jnp.bfloat16),
                "fsdp",
                scatter_dimension=1,
                tiled=True,
            ).astype(jnp.float32),
            lax.psum_scatter(
                grad_vall.reshape(clips, -1, local_width).astype(jnp.bfloat16),
                "fsdp",
                scatter_dimension=1,
                tiled=True,
            ).astype(jnp.float32),
        )
        grad_q = grad_q.astype(jnp.bfloat16).reshape(clips, shard_frames, local_width)
        grad_kloc = grad_kloc.astype(jnp.bfloat16)
        grad_vloc = grad_vloc.astype(jnp.bfloat16)
        grad_query = weight_grad(rows_one, grad_q)
        grad_key = weight_grad(rows_one, grad_kloc)
        grad_value = weight_grad(rows_one, grad_vloc)
        grad_one = fold_grads(
            project_back(grad_q, query_full)
            + project_back(grad_kloc, key_full)
            + project_back(grad_vloc, value_full)
        )
        back_one, gain_g1, bias_g1 = norm_back(grad_one, scaled_one, inverse_one, gain_one)
        input_grads.append(upstream + back_one)
        norm_parts = (gain_g1, bias_g1, gain_g2, bias_g2, gain_g3, bias_g3)
        norm_totals = norm_parts if micro == 0 else jax.tree.map(jnp.add, norm_totals, norm_parts)
        micro_grads = (
            grad_query,
            grad_key,
            grad_value,
            grad_cquery,
            grad_ckey,
            grad_cvalue,
            grad_up,
            grad_out,
            grad_cout,
            grad_down,
        )
        weight_total = (
            micro_grads if micro == 0 else jax.tree.map(jnp.add, weight_total, micro_grads)
        )
    weight_total = (
        lax.psum_scatter(
            weight_total[0].astype(jnp.bfloat16), "fsdp", scatter_dimension=0, tiled=True
        ).astype(jnp.float32),
        lax.psum_scatter(
            weight_total[1].astype(jnp.bfloat16), "fsdp", scatter_dimension=0, tiled=True
        ).astype(jnp.float32),
        lax.psum_scatter(
            weight_total[2].astype(jnp.bfloat16), "fsdp", scatter_dimension=0, tiled=True
        ).astype(jnp.float32),
        lax.psum_scatter(
            weight_total[3].astype(jnp.bfloat16), "fsdp", scatter_dimension=0, tiled=True
        ).astype(jnp.float32),
        lax.psum_scatter(
            weight_total[4].astype(jnp.bfloat16), "fsdp", scatter_dimension=0, tiled=True
        ).astype(jnp.float32),
        lax.psum_scatter(
            weight_total[5].astype(jnp.bfloat16), "fsdp", scatter_dimension=0, tiled=True
        ).astype(jnp.float32),
        lax.psum_scatter(
            weight_total[6].astype(jnp.bfloat16), "fsdp", scatter_dimension=0, tiled=True
        ).astype(jnp.float32),
        lax.psum_scatter(
            weight_total[7].astype(jnp.bfloat16), "fsdp", scatter_dimension=1, tiled=True
        ).astype(jnp.float32),
        lax.psum_scatter(
            weight_total[8].astype(jnp.bfloat16), "fsdp", scatter_dimension=1, tiled=True
        ).astype(jnp.float32),
        lax.psum_scatter(
            weight_total[9].astype(jnp.bfloat16), "fsdp", scatter_dimension=1, tiled=True
        ).astype(jnp.float32),
    )
    summed = lax.psum(
        (
            jnp.stack(text_grads),
            norm_totals[0],
            norm_totals[1],
            norm_totals[2],
            norm_totals[3],
            norm_totals[4],
            norm_totals[5],
        ),
        ("fsdp", "tp"),
    )
    (
        fin_query,
        fin_key,
        fin_value,
        fin_cquery,
        fin_ckey,
        fin_cvalue,
        fin_up,
        fin_out,
        fin_cout,
        fin_down,
    ) = weight_total
    return (
        jnp.stack(outputs),
        jnp.stack(input_grads),
        summed[0],
        summed[1],
        summed[2],
        summed[3],
        summed[4],
        summed[5],
        summed[6],
        fin_query,
        fin_key,
        fin_value,
        fin_out,
        fin_cquery,
        fin_ckey,
        fin_cvalue,
        fin_cout,
        fin_up,
        fin_down,
    )


BLOCK = 256
SCALE = 1.0 / math.sqrt(HD)
PIECES = 4


def pair_swap(values, axis_name):
    return lax.ppermute(values, axis_name, [(0, 1), (1, 0)])


def ring_shift(values, distance):
    size = lax.axis_size("z")
    return lax.ppermute(values, "z", [(i, (i + distance) % size) for i in range(size)])


def ring_flip(values, bit):
    size = lax.axis_size("z")
    return lax.ppermute(values, "z", [(i, i ^ bit) for i in range(size)])


def take(values, index, axis=0):
    return lax.dynamic_index_in_dim(values, index, axis, keepdims=False)


def place(values, piece, index, axis=0):
    return lax.dynamic_update_index_in_dim(values, piece, index, axis)


def ordered(index, own, other):
    return jnp.where(index == 0, jnp.stack([own, other]), jnp.stack([other, own]))


def wide(values):
    return values.astype(jnp.float32)


def narrow(values):
    return values.astype(jnp.bfloat16)


def exchange_clips(values):
    return lax.all_to_all(values, ("y", "z"), 0, 0, tiled=True)


def group_rows(own):
    across = pair_swap(own, "x")
    return [own, pair_swap(own, "c"), across, pair_swap(across, "c")]


def group_terms(parts):
    far = wide(parts[2]) + wide(pair_swap(parts[3], "c"))
    return [parts[0], pair_swap(parts[1], "c"), pair_swap(narrow(far), "x")]


def ring_gather(own):
    at_z, size = lax.axis_index("z"), lax.axis_size("z")
    out = place(jnp.zeros((size,) + own.shape, own.dtype), own, at_z)
    piece = own
    for distance in range(1, size):
        piece = ring_shift(piece, 1)
        out = place(out, piece, lax.rem(at_z + size - distance, size))
    return out


def ring_sum(parts):
    at_z, size = lax.axis_index("z"), lax.axis_size("z")
    moving = take(parts, lax.rem(at_z + size - 1, size))
    for step in range(1, size):
        got = ring_shift(moving, 1)
        mine = take(parts, lax.rem(at_z + 2 * size - 1 - step, size))
        total = wide(got) + wide(mine)
        moving = narrow(total)
    return total


def everywhere(values):
    for name in ("c", "x", "y"):
        values = values + pair_swap(values, name)
    bit = 1
    while bit < lax.axis_size("z"):
        values = values + ring_flip(values, bit)
        bit *= 2
    return values


def gather_attend(shards):
    at_x, at_c = lax.axis_index("x"), lax.axis_index("c")
    rows, units = shards[0].shape
    split = jnp.stack([shard.reshape(rows, 2, units // 2) for shard in shards], axis=1)
    split = jnp.transpose(split, (2, 0, 1, 3)).reshape(2, rows, -1)
    mine = jnp.stack([take(split, at_x), pair_swap(take(split, 1 - at_x), "x")])
    near = ring_gather(mine)
    across = pair_swap(near, "y")
    half = near.shape[0] // 2

    def sibling(values):
        return pair_swap(lax.dynamic_slice_in_dim(values, (1 - at_c) * half, half, 0), "c")

    return [near, across, sibling(near), sibling(across)]


def sum_attend(grad):
    at_x, at_c = lax.axis_index("x"), lax.axis_index("c")
    away = pair_swap(take(grad, 1 - at_c), "c")
    whole = ordered(at_c, take(grad, at_c), away)
    rows, width = whole.shape[-2:]
    whole = whole.reshape((-1, 2, rows, width))
    total = lax.psum_scatter(whole, ("z", "y"), scatter_dimension=0, tiled=True).reshape(2, rows, width)
    halves = ordered(at_x, take(total, at_x), pair_swap(take(total, 1 - at_x), "x"))
    halves = wide(halves).reshape(2, rows, 4, width // 4)
    return [
        jnp.concatenate([halves[0, :, i], halves[1, :, i]], axis=1) for i in range(4)
    ]


def gather_units(shard):
    at_x, at_c = lax.axis_index("x"), lax.axis_index("c")
    rows = shard.shape[0]
    split = jnp.transpose(shard.reshape(rows, 2, 2, -1), (1, 2, 0, 3))
    mine = take(split, at_x)
    other = pair_swap(take(split, 1 - at_x), "x")
    pair = jnp.stack([mine, other], axis=1)
    pair = jnp.stack([take(pair, at_c), pair_swap(take(pair, 1 - at_c), "c")], axis=1)
    own = pair.reshape((1, PIECES) + pair.shape[2:])
    return lax.all_gather(own, ("y", "z"), axis=0, tiled=True)


def sum_units(grad):
    at_x, at_c = lax.axis_index("x"), lax.axis_index("c")
    grad = grad.reshape((-1,) + grad.shape[2:])
    total = lax.psum_scatter(grad, ("y", "z"), scatter_dimension=0, tiled=True)[0]
    away = pair_swap(total[2:], "x")
    pair = ordered(at_x, total[:2], away)
    whole = ordered(at_c, pair[:, 0], pair_swap(pair[:, 1], "c"))
    whole = jnp.transpose(wide(whole), (2, 1, 0, 3))
    return whole.reshape(whole.shape[0], -1)


def gather_whole(shard):
    near = ring_gather(shard)
    pieces = [near, pair_swap(near, "y")]
    pieces = pieces + [pair_swap(piece, "x") for piece in pieces]
    return pieces + [pair_swap(piece, "c") for piece in pieces]


def sum_whole(grad):
    at_y, at_x, at_c = lax.axis_index("y"), lax.axis_index("x"), lax.axis_index("c")
    for at, name in ((at_c, "c"), (at_x, "x"), (at_y, "y")):
        got = pair_swap(take(grad, 1 - at), name)
        grad = narrow(wide(take(grad, at)) + wide(got))
    return ring_sum(grad)


def dot_nt(left, right):
    return lax.dot_general(left, right, (((1,), (1,)), ((), ())), preferred_element_type=jnp.float32)


def dot_nn(left, right):
    return lax.dot_general(left, right, (((1,), (0,)), ((), ())), preferred_element_type=jnp.float32)


def dot_tn(left, right):
    return lax.dot_general(left, right, (((0,), (0,)), ((), ())), preferred_element_type=jnp.float32)


def whole_spec(array):
    return pl.BlockSpec(array.shape, lambda *_: (0,) * len(array.shape))


ANYWHERE = pl.BlockSpec(memory_space=pl.ANY)
SCALARS = pl.BlockSpec(memory_space=pltpu.SMEM)


def like(shape, dtype=jnp.bfloat16):
    return jax.ShapeDtypeStruct(shape, dtype)


def diagonal_mask(size):
    row = lax.broadcasted_iota(jnp.int32, (size, size), 0)
    column = lax.broadcasted_iota(jnp.int32, (size, size), 1)
    return column <= row


def block_of(at_y, at_x, at_c):
    return (at_y * 2 + at_x) * 2 + at_c


def natural_rows(ids, piece, upper, rows):
    at_x, at_c = ids[1], ids[2]
    member = (at_x ^ (piece // 2)) * 2 + (at_c ^ (piece % 2))
    return pl.ds(pl.multiple_of((upper * PIECES + member) * rows, rows), rows)


def attend_copies(ids, pieces, weights, sem):
    at_y, at_x, at_c = ids[0], ids[1], ids[2]
    rows = pieces[0].shape[-2]
    half = pieces[2].shape[0]
    copies = []
    for index, piece in enumerate(pieces):
        sibling, other_y = index // 2, index % 2
        for at in range(half):
            for other_x in range(2):
                block = block_of(at_y ^ other_y, at_x ^ other_x, at_c ^ sibling)
                source = piece.at[at, other_x] if sibling else piece.at[at_c * half + at, other_x]
                target = weights.at[at, pl.ds(pl.multiple_of(block * rows, rows), rows)]
                copies.append(pltpu.make_async_copy(source, target, sem.at[len(copies)]))
    return copies


def attend_forward_kernel(ids, *refs):
    rows_in, pieces = refs[0:4], refs[4:8]
    parts, qkv, mixed_out, log_out = refs[8:12], refs[12], refs[13], refs[14]
    weights, mixed, sem = refs[15:18]
    copies = attend_copies(ids, pieces, weights, sem)
    for copy in copies:
        copy.start()
    for copy in copies:
        copy.wait()
    halves, frames, width = qkv.shape
    third = width // 3
    rows = rows_in[0].shape[0] // 2
    for at in range(halves):
        for piece in range(PIECES):
            out = narrow(dot_nn(rows_in[piece][...], weights[at, :, :width]))
            for upper in range(2):
                qkv[at, natural_rows(ids, piece, upper, rows), :] = out[upper * rows : (upper + 1) * rows]
    mask = diagonal_mask(BLOCK)
    log_out[...] = jnp.zeros_like(log_out)
    lane = lax.broadcasted_iota(jnp.int32, (BLOCK, log_out.shape[1]), 1)

    def half_heads(at, carry):
        for head in range(third // HD):
            q_lanes, k_lanes, v_lanes = (
                slice(i * third + head * HD, i * third + (head + 1) * HD) for i in range(3)
            )
            for start in range(0, frames, BLOCK):
                block = slice(start, start + BLOCK)
                q = qkv[at, block, q_lanes] * jnp.bfloat16(SCALE)
                near = jnp.where(mask, dot_nt(q, qkv[at, block, k_lanes]), MASKED)
                top = jnp.max(near, axis=-1, keepdims=True)
                if start:
                    past = dot_nt(q, qkv[at, 0:start, k_lanes])
                    top = jnp.maximum(top, jnp.max(past, axis=-1, keepdims=True))
                near = jnp.exp(near - top)
                total = jnp.sum(near, axis=-1, keepdims=True)
                out = dot_nn(narrow(near), qkv[at, block, v_lanes])
                if start:
                    past = jnp.exp(past - top)
                    total = total + jnp.sum(past, axis=-1, keepdims=True)
                    out = out + dot_nn(narrow(past), qkv[at, 0:start, v_lanes])
                mixed[at, block, head * HD : (head + 1) * HD] = narrow(out / total)
                log_total = top + jnp.log(total)
                log_out[block, :] = jnp.where(
                    lane == at * (third // HD) + head, log_total, log_out[block, :]
                )
        return carry

    lax.fori_loop(0, halves, half_heads, 0)
    for piece in range(PIECES):
        for upper in range(2):
            here = natural_rows(ids, piece, upper, rows)
            there = slice(upper * rows, (upper + 1) * rows)
            out = None
            for at in range(halves):
                own = mixed[at, here, :]
                mixed_out[at, piece, there, :] = own
                term = dot_nt(own, weights[at, :, width:])
                out = term if out is None else out + term
            parts[piece][there, :] = narrow(out)


def attend_backward_kernel(ids, *refs):
    rows_in, pieces = refs[0:4], refs[4:8]
    qkv, mixed_in, log_in = refs[8], refs[9], refs[10]
    parts, grad_out = refs[11:15], refs[15]
    weights, grads, totals, back, dk_sum, dv_sum, sem = refs[16:23]
    copies = attend_copies(ids, pieces, weights, sem)
    for copy in copies:
        copy.start()
    for copy in copies:
        copy.wait()
    halves, frames, width = qkv.shape
    third = width // 3
    heads = third // HD
    rows = rows_in[0].shape[0] // 2
    for at in range(halves):
        for piece in range(PIECES):
            out = narrow(dot_nn(rows_in[piece][...], weights[at, :, width:]))
            product = wide(out) * wide(mixed_in[at, piece])
            lane = lax.broadcasted_iota(jnp.int32, (2 * rows, totals.shape[2]), 1)
            sums = jnp.zeros((2 * rows, totals.shape[2]), jnp.float32)
            for head in range(heads):
                one = jnp.sum(product[:, head * HD : (head + 1) * HD], axis=-1, keepdims=True)
                sums = jnp.where(lane == head, one, sums)
            for upper in range(2):
                here = natural_rows(ids, piece, upper, rows)
                there = slice(upper * rows, (upper + 1) * rows)
                grads[at, here, :] = out[there]
                totals[at, here, :] = sums[there]
    mask = diagonal_mask(BLOCK)

    def half_heads(at, carry):
        dk_sum[...] = jnp.zeros_like(dk_sum)
        dv_sum[...] = jnp.zeros_like(dv_sum)
        for head in range(heads):
            q_lanes, k_lanes, v_lanes = (
                slice(i * third + head * HD, i * third + (head + 1) * HD) for i in range(3)
            )
            o_lanes = slice(head * HD, (head + 1) * HD)
            log_lane = lax.broadcasted_iota(jnp.int32, (BLOCK, log_in.shape[1]), 1)
            for start in range(0, frames, BLOCK):
                block = slice(start, start + BLOCK)
                q = qkv[at, block, q_lanes] * jnp.bfloat16(SCALE)
                grad = grads[at, block, o_lanes]
                q_turned = narrow(wide(q).T)
                grad_turned = narrow(wide(grad).T)
                log_total = jnp.sum(
                    jnp.where(log_lane == at * heads + head, log_in[block, :], 0.0),
                    axis=-1,
                    keepdims=True,
                )
                row_total = totals[at, block, head : head + 1]
                dq = None
                for columns in (block, slice(0, start)):
                    if columns.stop == 0:
                        continue
                    keys = qkv[at, columns, k_lanes]
                    weight = jnp.exp(dot_nt(q, keys) - log_total)
                    if columns is block:
                        weight = jnp.where(mask, weight, 0.0)
                    grad_weight = dot_nt(grad, qkv[at, columns, v_lanes])
                    scores = narrow(weight * (grad_weight - row_total))
                    part = dot_nn(scores, keys)
                    dq = part if dq is None else dq + part
                    dk_sum[o_lanes, columns] += dot_nn(q_turned, scores)
                    dv_sum[o_lanes, columns] += dot_nn(grad_turned, narrow(weight))
                back[at, block, q_lanes] = narrow(dq * SCALE)
        for start in range(0, frames, BLOCK):
            block = slice(start, start + BLOCK)
            back[at, block, third : 2 * third] = narrow(dk_sum[:, block].T)
            back[at, block, 2 * third :] = narrow(dv_sum[:, block].T)
        return carry

    lax.fori_loop(0, halves, half_heads, 0)
    for piece in range(PIECES):
        for at in range(halves):
            for upper in range(2):
                there = slice(upper * rows, (upper + 1) * rows)
                grad_out[at, piece, there, :] = back[at, natural_rows(ids, piece, upper, rows), :]
        out = None
        for at in range(halves):
            term = dot_nt(grad_out[at, piece], weights[at, :, :width])
            out = term if out is None else out + term
        parts[piece][...] = narrow(out)


def attend_forward(ids, rows_in, pieces):
    rows, model = rows_in[0].shape
    halves, units = pieces[2].shape[0], pieces[0].shape[-1]
    width = units // 4
    frames = PIECES * rows
    outs = [like((rows, model))] * PIECES + [
        like((halves, frames, 3 * width)),
        like((halves, PIECES, rows, width)),
        like((frames, 128), jnp.float32),
    ]
    out = pl.pallas_call(
        attend_forward_kernel,
        in_specs=[SCALARS] + [pl.BlockSpec(memory_space=pltpu.VMEM)] * PIECES + [ANYWHERE] * 4,
        out_specs=[pl.BlockSpec(memory_space=pltpu.VMEM)] * len(outs),
        out_shape=outs,
        scratch_shapes=[
            pltpu.VMEM((halves, model, units), jnp.bfloat16),
            pltpu.VMEM((halves, frames, width), jnp.bfloat16),
            pltpu.SemaphoreType.DMA((8 * halves,)),
        ],
        compiler_params=pltpu.CompilerParams(vmem_limit_bytes=56 * 2**20),
        cost_estimate=pl.CostEstimate(
            flops=30 * 10**9, bytes_accessed=24 * 2**20, transcendentals=0
        ),
        name="attend_forward",
    )(ids, *rows_in, *pieces)
    return out[:4], out[4], out[5], out[6]


def attend_backward(ids, rows_in, pieces, qkv, mixed, log_total):
    rows, model = rows_in[0].shape
    halves, units = pieces[2].shape[0], pieces[0].shape[-1]
    frames, width = qkv.shape[1], qkv.shape[2] // 3
    outs = [like((rows, model))] * PIECES + [like((halves, PIECES, rows, 3 * width))]
    vmem = pl.BlockSpec(memory_space=pltpu.VMEM)
    out = pl.pallas_call(
        attend_backward_kernel,
        in_specs=[SCALARS] + [vmem] * PIECES + [ANYWHERE] * 4 + [vmem] * 3,
        out_specs=[vmem] * len(outs),
        out_shape=outs,
        scratch_shapes=[
            pltpu.VMEM((halves, model, units), jnp.bfloat16),
            pltpu.VMEM((halves, frames, width), jnp.bfloat16),
            pltpu.VMEM((halves, frames, 128), jnp.float32),
            pltpu.VMEM((halves, frames, 3 * width), jnp.bfloat16),
            pltpu.VMEM((width, frames), jnp.float32),
            pltpu.VMEM((width, frames), jnp.float32),
            pltpu.SemaphoreType.DMA((8 * halves,)),
        ],
        compiler_params=pltpu.CompilerParams(vmem_limit_bytes=58 * 2**20),
        cost_estimate=pl.CostEstimate(
            flops=50 * 10**9, bytes_accessed=24 * 2**20, transcendentals=0
        ),
        name="attend_backward",
    )(ids, *rows_in, *pieces, qkv, mixed, log_total)
    return out[:4], out[4]


def attend_grads_kernel(ids, *refs):
    normed, grads = refs[0:4], refs[4:8]
    grad_qkv, mixed, out = refs[8:11]
    halves, _, _, width = grad_qkv.shape
    rows = out.shape[-2]
    for at in range(halves):
        left = right = None
        for piece in range(PIECES):
            one = dot_tn(normed[piece][...], grad_qkv[at, piece])
            two = dot_tn(grads[piece][...], mixed[at, piece])
            left = one if left is None else left + one
            right = two if right is None else right + two
        for core in range(2):
            block = slice(core * rows, (core + 1) * rows)
            out[core, at, 0, 0, :, :width] = narrow(left[block])
            out[core, at, 0, 0, :, width:] = narrow(right[block])


def attend_grads(ids, normed, grads, grad_qkv, mixed):
    rows, model = normed[0].shape
    halves, units = mixed.shape[0], 4 * mixed.shape[-1]
    strip = model // 4
    column = pl.BlockSpec((rows, strip), lambda i, ids: (0, i))
    return pl.pallas_call(
        attend_grads_kernel,
        grid_spec=pltpu.PrefetchScalarGridSpec(
            num_scalar_prefetch=1,
            grid=(4,),
            in_specs=[column] * 8 + [whole_spec(grad_qkv), whole_spec(mixed)],
            out_specs=pl.BlockSpec(
                (2, halves, 1, 1, strip // 2, units), lambda i, ids: (0, 0, i // 2, i % 2, 0, 0)
            ),
        ),
        out_shape=like((2, halves, 2, 2, strip // 2, units)),
        compiler_params=pltpu.CompilerParams(vmem_limit_bytes=40 * 2**20),
        cost_estimate=pl.CostEstimate(
            flops=8 * 10**9, bytes_accessed=20 * 2**20, transcendentals=0
        ),
        name="attend_grads",
    )(ids, *normed, *grads, grad_qkv, mixed)


def gelu_both(values):
    factor = math.sqrt(2.0 / math.pi)
    square = values * values
    bent = jnp.tanh(factor * values * (1.0 + 0.044715 * square))
    slope = 0.5 * (1.0 + bent) + 0.5 * values * (1.0 - bent * bent) * factor * (
        1.0 + 3.0 * 0.044715 * square
    )
    return 0.5 * values * (1.0 + bent), slope


def feed_kernel(ids, *refs):
    rows_in, grads_in, up_in, down_in = refs[0:4], refs[4:8], refs[8], refs[9]
    result_out, back_out, active_out, hidden_out = refs[10:14], refs[14:18], refs[18], refs[19]
    rows_all, grads_all, up, down, result, back, active, hidden, w_sem, in_sem, out_sem = refs[20:]
    at_x, at_c = ids[1], ids[2]
    rows, model = rows_in[0].shape
    shard_rows, width = up_in.shape[-2:]
    groups = up_in.shape[0] // 2
    copies = []
    for which, (source, target) in enumerate(((up_in, up), (down_in, down))):
        for other_y in range(2):
            for at_z in range(groups):
                for piece in range(PIECES):
                    block = block_of(other_y, at_x ^ (piece // 2), at_c ^ (piece % 2))
                    place_rows = pl.ds(pl.multiple_of(block * shard_rows, shard_rows), shard_rows)
                    lanes = slice((at_z % 2) * width, (at_z % 2 + 1) * width)
                    copies.append(
                        pltpu.make_async_copy(
                            source.at[other_y * groups + at_z, piece],
                            target.at[at_z // 2, place_rows, lanes],
                            w_sem.at[len(copies)],
                        )
                    )
    for piece in range(PIECES):
        copies.append(
            pltpu.make_async_copy(rows_in[piece], rows_all.at[piece], in_sem.at[2 * piece])
        )
        copies.append(
            pltpu.make_async_copy(grads_in[piece], grads_all.at[piece], in_sem.at[2 * piece + 1])
        )
    for copy in copies:
        copy.start()
    for copy in copies:
        copy.wait()
    blocks = groups // 2

    def outputs(piece, slot):
        return [
            pltpu.make_async_copy(source.at[slot], target, out_sem.at[slot, i])
            for i, (source, target) in enumerate(
                (
                    (result, result_out[piece]),
                    (back, back_out[piece]),
                    (active, active_out.at[piece]),
                    (hidden, hidden_out.at[piece]),
                )
            )
        ]

    for piece in range(PIECES):
        slot = piece % 2
        if piece >= 2:
            for copy in outputs(piece - 2, slot):
                copy.wait()

        def one_block(at, carry):
            own = rows_all[piece]
            value, slope = gelu_both(dot_nn(own, up[at]))
            value = narrow(value)
            change = narrow(dot_nn(grads_all[piece], down[at]) * slope)
            lanes = pl.ds(pl.multiple_of(at * 2 * width, 2 * width), 2 * width)
            active[slot, :, lanes] = value
            hidden[slot, :, lanes] = change
            return carry

        lax.fori_loop(0, blocks, one_block, 0)

        def one_result(at, carry):
            here = pl.ds(pl.multiple_of(at * 2 * width, 2 * width), 2 * width)
            first = second = None
            for part in range(blocks):
                lanes = slice(part * 2 * width, (part + 1) * 2 * width)
                one = dot_nt(active[slot, :, lanes], down[part, here, :])
                two = dot_nt(hidden[slot, :, lanes], up[part, here, :])
                first = one if first is None else first + one
                second = two if second is None else second + two
            result[slot, :, here] = narrow(first)
            back[slot, :, here] = narrow(second)
            return carry

        lax.fori_loop(0, model // (2 * width), one_result, 0)
        for copy in outputs(piece, slot):
            copy.start()
    for piece in (PIECES - 2, PIECES - 1):
        for copy in outputs(piece, piece % 2):
            copy.wait()


def feed(ids, rows_in, grads_in, up, down):
    rows, model = rows_in[0].shape
    units = up.shape[0] // 2 * up.shape[-1]
    outs = [like((rows, model))] * 8 + [like((PIECES, rows, units))] * 2
    blocks = up.shape[0] // 4
    weight = pltpu.VMEM((blocks, model, 2 * up.shape[-1]), jnp.bfloat16)
    out = pl.pallas_call(
        feed_kernel,
        in_specs=[SCALARS] + [ANYWHERE] * 10,
        out_specs=[ANYWHERE] * 10,
        out_shape=outs,
        scratch_shapes=[
            pltpu.VMEM((PIECES, rows, model), jnp.bfloat16),
            pltpu.VMEM((PIECES, rows, model), jnp.bfloat16),
            weight,
            weight,
            pltpu.VMEM((2, rows, model), jnp.bfloat16),
            pltpu.VMEM((2, rows, model), jnp.bfloat16),
            pltpu.VMEM((2, rows, units), jnp.bfloat16),
            pltpu.VMEM((2, rows, units), jnp.bfloat16),
            pltpu.SemaphoreType.DMA((2 * up.shape[0] * PIECES,)),
            pltpu.SemaphoreType.DMA((2 * PIECES,)),
            pltpu.SemaphoreType.DMA((2, 4)),
        ],
        compiler_params=pltpu.CompilerParams(vmem_limit_bytes=56 * 2**20),
        cost_estimate=pl.CostEstimate(
            flops=8 * PIECES * rows * model * units, bytes_accessed=36 * 2**20, transcendentals=0
        ),
        name="feed_forward",
    )(ids, *rows_in, *grads_in, up, down)
    return out[0:4], out[4:8], out[8], out[9]


def feed_grads_kernel(ids, *refs):
    left, right, out = refs[0:4], refs[4], refs[5]
    rows, width = out.shape[-2:]
    at_c = ids[2]
    for at_z in range(out.shape[1]):
        total = None
        for piece in range(PIECES):
            one = dot_tn(left[piece][...], right[piece, :, at_z * width : (at_z + 1) * width])
            total = one if total is None else total + one
        for core in range(2):
            out[0, at_z, 0, at_c ^ core] = narrow(total[core * rows : (core + 1) * rows])


def feed_grads(ids, left, right):
    rows, model = left[0].shape
    units = right.shape[-1]
    groups = lax.axis_size("z")
    strip = model // 4
    shape = (2, groups, 2, 2, strip // 2, units // groups)
    out = pl.pallas_call(
        feed_grads_kernel,
        grid_spec=pltpu.PrefetchScalarGridSpec(
            num_scalar_prefetch=1,
            grid=(4,),
            in_specs=[pl.BlockSpec((rows, strip), lambda i, ids: (0, i))] * 4 + [whole_spec(right)],
            out_specs=pl.BlockSpec(
                (1, groups, 1, 2, strip // 2, units // groups),
                lambda i, ids: (i // 2, 0, (i % 2) ^ ids[1], 0, 0, 0),
            ),
        ),
        out_shape=like(shape),
        compiler_params=pltpu.CompilerParams(vmem_limit_bytes=40 * 2**20),
        cost_estimate=pl.CostEstimate(
            flops=2 * PIECES * rows * model * units, bytes_accessed=16 * 2**20, transcendentals=0
        ),
        name="feed_grads",
    )(ids, *left, right)
    return out.reshape(2, groups, PIECES, strip // 2, units // groups)


def block_pair(values):
    low = lax.broadcasted_iota(jnp.int32, values.shape, 1) < HD
    zero = jnp.zeros_like(values)
    return jnp.concatenate([jnp.where(low, values, zero), jnp.where(low, zero, values)], axis=0)


def by_half(low, values, reduce, empty):
    first = reduce(jnp.where(low, values, empty), axis=-1, keepdims=True)
    second = reduce(jnp.where(low, empty, values), axis=-1, keepdims=True)
    return jnp.where(low, first, second)


def cross_weights(count, queries, keys):
    slots = keys.shape[0] // 2
    scores = dot_nt(queries, keys)
    lane = lax.broadcasted_iota(jnp.int32, scores.shape, 1)
    low = lane < slots
    scores = jnp.where(jnp.where(low, lane, lane - slots) < count, scores, MASKED)
    raised = jnp.exp(scores - by_half(low, scores, jnp.max, MASKED))
    return raised / by_half(low, raised, jnp.sum, 0.0), low


def cross_copies(ids, pieces, weights, sem):
    rows = pieces[0].shape[-2]
    copies = []
    for index, piece in enumerate(pieces):
        block = block_of(ids[0] ^ (index % 2), ids[1] ^ (index // 2 % 2), ids[2] ^ (index // 4))
        target = weights.at[:, pl.ds(pl.multiple_of(block * rows, rows), rows)]
        copies.append(pltpu.make_async_copy(piece, target, sem.at[index]))
    return copies


def lanes_of(at, size):
    return pl.ds(pl.multiple_of(at * size, size), size)


def cross_forward_kernel(ids, count, *refs):
    tokens, terms, norms, keys_values, pieces = refs[0], refs[1:4], refs[4], refs[5], refs[6:14]
    self_out, normed_out, queries, mixed, cross_out, rows_out = refs[14:20]
    weights, sem = refs[20:22]
    copies = cross_copies(ids, pieces, weights, sem)
    for copy in copies:
        copy.start()
    after_self = wide(tokens[...])
    for term in terms:
        after_self = after_self + wide(term[...])
    self_out[...] = after_self
    normed = narrow(layer_norm(after_self, norms[0:1, :], norms[1:2, :])[0])
    normed_out[...] = normed
    for copy in copies:
        copy.wait()
    width = weights.shape[2] // 2
    model = tokens.shape[1]
    for at in range(weights.shape[0]):
        out = dot_nn(normed_out[...], weights[at, :, :width])
        queries[:, at * width : (at + 1) * width] = narrow(out)

    def one_pair(at, carry):
        lanes = lanes_of(at, 2 * HD)
        query = queries[:, lanes] * jnp.bfloat16(SCALE)
        keys = block_pair(keys_values[:, lanes])
        values = block_pair(keys_values[:, lanes_of(at + model // (2 * HD), 2 * HD)])
        weight, _ = cross_weights(count[0], query, keys)
        mixed[:, lanes] = narrow(dot_nn(narrow(weight), values))
        return carry

    lax.fori_loop(0, model // (2 * HD), one_pair, 0)
    after_cross = self_out[...]
    for at in range(weights.shape[0]):
        after_cross = after_cross + dot_nt(
            mixed[:, at * width : (at + 1) * width], weights[at, :, width:]
        )
    cross_out[...] = after_cross
    rows_out[...] = narrow(layer_norm(after_cross, norms[2:3, :], norms[3:4, :])[0])


def cross_forward(ids, count, tokens, terms, norms, keys_values, pieces):
    rows, model = tokens.shape
    outs = [
        like((rows, model), jnp.float32),
        like((rows, model)),
        like((rows, model)),
        like((rows, model)),
        like((rows, model), jnp.float32),
        like((rows, model)),
    ]
    vmem = pl.BlockSpec(memory_space=pltpu.VMEM)
    size, shard_rows, width = pieces[0].shape
    return pl.pallas_call(
        cross_forward_kernel,
        in_specs=[SCALARS] * 2 + [vmem] * 6 + [ANYWHERE] * 8,
        out_specs=[vmem] * len(outs),
        out_shape=outs,
        scratch_shapes=[
            pltpu.VMEM((size, 8 * shard_rows, width), jnp.bfloat16),
            pltpu.SemaphoreType.DMA((8,)),
        ],
        compiler_params=pltpu.CompilerParams(vmem_limit_bytes=48 * 2**20),
        cost_estimate=pl.CostEstimate(
            flops=12 * 10**9, bytes_accessed=24 * 2**20, transcendentals=0
        ),
        name="cross_forward",
    )(ids, count, tokens, *terms, norms, keys_values, *pieces)


def norm_gradient(upstream, values, gain_vec, bias_vec):
    _, scaled, inverse = layer_norm(values, gain_vec, bias_vec)
    weighted = upstream * gain_vec
    result = inverse * (
        weighted
        - jnp.mean(weighted, axis=-1, keepdims=True)
        - scaled * jnp.mean(weighted * scaled, axis=-1, keepdims=True)
    )
    return (
        result,
        jnp.sum(upstream * scaled, axis=0, keepdims=True),
        jnp.sum(upstream, axis=0, keepdims=True),
    )


def cross_backward_kernel(ids, count, *refs):
    upstream, terms, norms, keys_values = refs[0], refs[1:4], refs[4], refs[5]
    self_in, cross_in, queries, pieces = refs[6], refs[7], refs[8], refs[9:17]
    grad_out, first_out, second_out, dq_out, dkv_out, norm_out = refs[17:23]
    weights, grads, sem = refs[23:26]
    copies = cross_copies(ids, pieces, weights, sem)
    for copy in copies:
        copy.start()
    grad_three = wide(terms[0][...]) + wide(terms[1][...]) + wide(terms[2][...])
    back, gain_g, bias_g = norm_gradient(
        grad_three, cross_in[...], norms[2:3, :], norms[3:4, :]
    )
    norm_out[2:3, :] = gain_g
    norm_out[3:4, :] = bias_g
    grad_two = wide(upstream[...]) + back
    grad_out[...] = grad_two
    second_out[...] = narrow(grad_two)
    for copy in copies:
        copy.wait()
    width = weights.shape[2] // 2
    model = upstream.shape[1]
    slots = keys_values.shape[0]
    for at in range(weights.shape[0]):
        out = dot_nn(second_out[...], weights[at, :, width:])
        grads[:, at * width : (at + 1) * width] = narrow(out)
    dims_low = lax.broadcasted_iota(jnp.int32, (slots, 2 * HD), 1) < HD

    def one_pair(at, carry):
        lanes = lanes_of(at, 2 * HD)
        value_lanes = lanes_of(at + model // (2 * HD), 2 * HD)
        query = queries[:, lanes] * jnp.bfloat16(SCALE)
        keys = block_pair(keys_values[:, lanes])
        weight, low = cross_weights(count[0], query, keys)
        grad = grads[:, lanes]
        grad_weight = dot_nt(grad, block_pair(keys_values[:, value_lanes]))
        scores = weight * (grad_weight - by_half(low, grad_weight * weight, jnp.sum, 0.0))
        scores = narrow(scores)
        dq_out[:, lanes] = narrow(dot_nn(scores, keys) * SCALE)
        dk = dot_tn(scores, query)
        dkv_out[:, lanes] = narrow(jnp.where(dims_low, dk[:slots], dk[slots:]))
        dv = dot_tn(narrow(weight), grad)
        dkv_out[:, value_lanes] = narrow(jnp.where(dims_low, dv[:slots], dv[slots:]))
        return carry

    lax.fori_loop(0, model // (2 * HD), one_pair, 0)
    grad_two_rows = None
    for at in range(weights.shape[0]):
        term = dot_nt(dq_out[:, at * width : (at + 1) * width], weights[at, :, :width])
        grad_two_rows = term if grad_two_rows is None else grad_two_rows + term
    back, gain_g, bias_g = norm_gradient(grad_two_rows, self_in[...], norms[0:1, :], norms[1:2, :])
    norm_out[0:1, :] = gain_g
    norm_out[1:2, :] = bias_g
    grad_one = grad_out[...] + back
    grad_out[...] = grad_one
    first_out[...] = narrow(grad_one)


def cross_backward(
    ids, count, upstream, terms, norms, keys_values, after_self, after_cross, queries, pieces
):
    rows, model = upstream.shape
    slots = keys_values.shape[0]
    outs = [
        like((rows, model), jnp.float32),
        like((rows, model)),
        like((rows, model)),
        like((rows, model)),
        like((slots, 2 * model)),
        like((4, model), jnp.float32),
    ]
    vmem = pl.BlockSpec(memory_space=pltpu.VMEM)
    size, shard_rows, width = pieces[0].shape
    return pl.pallas_call(
        cross_backward_kernel,
        in_specs=[SCALARS] * 2 + [vmem] * 9 + [ANYWHERE] * 8,
        out_specs=[vmem] * len(outs),
        out_shape=outs,
        scratch_shapes=[
            pltpu.VMEM((size, 8 * shard_rows, width), jnp.bfloat16),
            pltpu.VMEM((rows, model), jnp.bfloat16),
            pltpu.SemaphoreType.DMA((8,)),
        ],
        compiler_params=pltpu.CompilerParams(vmem_limit_bytes=56 * 2**20),
        cost_estimate=pl.CostEstimate(
            flops=16 * 10**9, bytes_accessed=28 * 2**20, transcendentals=0
        ),
        name="cross_backward",
    )(
        ids,
        count,
        upstream,
        *terms,
        norms,
        keys_values,
        after_self,
        after_cross,
        queries,
        *pieces,
    )


def cross_grads_kernel(normed, grad_queries, grads, mixed, out):
    rows, width = out.shape[-2], out.shape[-1] // 2
    for at in range(out.shape[3]):
        lanes = slice(at * width, (at + 1) * width)
        left = dot_tn(normed[...], grad_queries[:, lanes])
        right = dot_tn(grads[...], mixed[:, lanes])
        for core in range(2):
            block = slice(core * rows, (core + 1) * rows)
            out[core, 0, 0, at, :, :width] = narrow(left[block])
            out[core, 0, 0, at, :, width:] = narrow(right[block])


def cross_grads(normed, grad_queries, grads, mixed):
    rows, model = normed.shape
    size = lax.axis_size("z")
    strip = model // 4
    column = pl.BlockSpec((rows, strip), lambda i: (0, i))
    return pl.pallas_call(
        cross_grads_kernel,
        grid=(4,),
        in_specs=[column, whole_spec(grad_queries), column, whole_spec(mixed)],
        out_specs=pl.BlockSpec(
            (2, 1, 1, size, strip // 2, 2 * (model // size)),
            lambda i: (0, i % 2, i // 2, 0, 0, 0),
        ),
        out_shape=like((2, 2, 2, size, strip // 2, 2 * (model // size))),
        compiler_params=pltpu.CompilerParams(vmem_limit_bytes=40 * 2**20),
        cost_estimate=pl.CostEstimate(
            flops=4 * rows * model * model, bytes_accessed=14 * 2**20, transcendentals=0
        ),
        name="cross_grads",
    )(normed, grad_queries, grads, mixed)


def clip_body(
    tokens,
    memory,
    text_len,
    cotangent,
    gain_one,
    bias_one,
    gain_two,
    bias_two,
    gain_three,
    bias_three,
    w_query,
    w_key,
    w_value,
    w_out,
    c_query,
    c_key,
    c_value,
    c_out,
    w_up,
    w_down,
):
    at_y, at_x, at_c, at_z = (lax.axis_index(name) for name in ("y", "x", "c", "z"))
    ids = jnp.stack([at_y, at_x, at_c, at_z]).astype(jnp.int32)
    model = tokens.shape[-1]
    shard_rows, shard_width = w_query.shape
    slots = memory.shape[2]
    size = lax.axis_size("z")
    frame_block = tokens.shape[2]

    attend_pieces = gather_attend([w_query, w_key, w_value, w_out.T])
    clip_tokens = exchange_clips(tokens.reshape(-1, frame_block, model)).reshape(-1, model)
    frames = wide(clip_tokens)
    normed_one, scaled_one, inverse_one = layer_norm(frames[None], gain_one, bias_one)
    rows_one = group_rows(narrow(normed_one)[0])
    upstream = exchange_clips(cotangent.reshape(-1, frame_block, model)).reshape(-1, model)
    cross_pieces = gather_whole(jnp.concatenate([c_query, c_out.T], axis=1))
    up_full = gather_units(w_up)
    down_full = gather_units(w_down.T)
    grad_rows3 = group_rows(upstream)

    at_f = block_of(at_y, at_x, at_c)
    text_flat = memory.reshape(-1, model)
    text_mine = lax.dynamic_slice_in_dim(text_flat, at_f * shard_rows, shard_rows, 1)
    text_shard = jnp.concatenate([c_key, c_value], axis=1)
    text_part = narrow(dot_nn(text_mine, text_shard)).reshape(2, -1, slots, 2 * shard_width)
    got = wide(pair_swap(take(text_part, 1 - at_y), "y"))
    text_part = narrow(wide(take(text_part, at_y)) + got)
    text_clip = text_part
    for distance in range(1, size):
        piece = ring_shift(take(text_part, lax.rem(at_z + distance, size)), distance)
        text_clip = place(text_clip, piece, lax.rem(at_z + size - distance, size))
    for name in ("x", "c"):
        text_clip = narrow(wide(text_clip) + wide(pair_swap(text_clip, name)))
    text_clip = text_clip.reshape(size, slots, 2, shard_width)
    keys_values = jnp.transpose(text_clip, (1, 2, 0, 3)).reshape(slots, -1)
    count = take(take(text_len, at_y), at_z).reshape(1)
    norms = jnp.stack([gain_two, bias_two, gain_three, bias_three])

    self_parts, qkv, mixed_one, log_total = attend_forward(ids, rows_one, attend_pieces)
    after_self, rows_two, cross_q, mixed_two, after_cross, own_three = cross_forward(
        ids, count, clip_tokens, group_terms(self_parts), norms, keys_values, cross_pieces
    )
    rows_three = group_rows(own_three)

    feed_parts, back_parts, active, grad_hidden = feed(
        ids, rows_three, grad_rows3, up_full, down_full
    )
    back_terms = group_terms(back_parts)
    fin_down = sum_units(feed_grads(ids, grad_rows3, active))
    fin_up = sum_units(feed_grads(ids, rows_three, grad_hidden))
    feed_terms = group_terms(feed_parts)
    result = after_cross + wide(feed_terms[0]) + wide(feed_terms[1]) + wide(feed_terms[2])
    result = exchange_clips(narrow(result).reshape(-1, frame_block, model)).reshape(tokens.shape)

    grad_one_rows, own_one, own_two, grad_cq, grad_text, norm_grads = cross_backward(
        ids,
        count,
        upstream,
        back_terms,
        norms,
        keys_values,
        after_self,
        after_cross,
        cross_q,
        cross_pieces,
    )
    grad_rows1 = group_rows(own_one)
    fin_cross = sum_whole(cross_grads(rows_two, grad_cq, own_two, mixed_two))
    fin_cquery, fin_cout = fin_cross[:, :shard_width], fin_cross[:, shard_width:].T

    grad_text = grad_text.reshape(slots, 2, size, shard_width)
    grad_text = jnp.transpose(grad_text, (2, 0, 1, 3)).reshape(size, slots, 2 * shard_width)
    for name in ("x", "c"):
        grad_text = narrow(wide(grad_text) + wide(pair_swap(grad_text, name)))
    spread = grad_text
    for distance in range(1, size):
        piece = ring_shift(take(grad_text, lax.rem(at_z + distance, size)), distance)
        spread = place(spread, piece, lax.rem(at_z + size - distance, size))
    spread = ordered(at_y, spread, pair_swap(spread, "y")).reshape(-1, 2 * shard_width)
    fin_text = dot_tn(text_mine, spread)
    fin_ckey, fin_cvalue = fin_text[:, :shard_width], fin_text[:, shard_width:]
    grad_memory = narrow(dot_nt(spread, text_shard))
    bit = 1
    while bit < size:
        grad_memory = narrow(wide(grad_memory) + wide(ring_flip(grad_memory, bit)))
        bit *= 2
    for at, name in ((at_c, "c"), (at_x, "x"), (at_y, "y")):
        grad_memory = ordered(at, grad_memory, pair_swap(grad_memory, name))
    grad_memory = jnp.transpose(grad_memory.reshape(8, -1, shard_rows), (1, 0, 2))
    grad_memory = wide(grad_memory.reshape(memory.shape))

    self_back, grad_qkv = attend_backward(
        ids, grad_rows1, attend_pieces, qkv, mixed_one, log_total
    )
    terms = group_terms(self_back)
    grad_one = wide(terms[0]) + wide(terms[1]) + wide(terms[2])
    back_one, gain_g1, bias_g1 = norm_back(grad_one[None], scaled_one, inverse_one, gain_one)
    input_grad = narrow(grad_one_rows + back_one[0])
    input_grad = exchange_clips(input_grad.reshape(-1, frame_block, model))
    input_grad = wide(input_grad).reshape(tokens.shape)
    fin_query, fin_key, fin_value, fin_out = sum_attend(
        attend_grads(ids, rows_one, grad_rows1, grad_qkv, mixed_one)
    )

    early = everywhere(norm_grads)
    late = everywhere(jnp.stack([gain_g1, bias_g1]))
    return (
        result,
        input_grad,
        grad_memory,
        late[0],
        late[1],
        early[0],
        early[1],
        early[2],
        early[3],
        fin_query,
        fin_key,
        fin_value,
        fin_out.T,
        fin_cquery,
        fin_ckey,
        fin_cvalue,
        fin_cout,
        fin_up,
        fin_down.T,
    )


def clip_groups(mesh):
    outer, inner = mesh.shape["fsdp"], mesh.shape["tp"]
    return (2, 2, 2, inner) if outer == 8 and inner == 4 else None


def solution(mesh):
    sizes = clip_groups(mesh)
    if sizes is None:
        rows, columns, program, used = "fsdp", "tp", body, mesh
    else:
        rows, columns, program = ("y", "x", "c"), "z", clip_body
        used = jax.sharding.Mesh(mesh.devices.reshape(sizes), ("y", "x", "c", "z"))
    both = ("fsdp", "tp") if sizes is None else ("y", "x", "c", "z")
    frames = P(None, None, both, None)
    tall, wide = P(rows, columns), P(columns, rows)
    weights = (tall, tall, tall, wide, tall, tall, tall, wide, tall, wide)
    return jax.shard_map(
        program,
        mesh=used,
        in_specs=(frames, P(), P(), frames) + (P(),) * 6 + weights,
        out_specs=(frames, frames, P()) + (P(),) * 6 + weights,
        check_vma=False,
    )
```

```python
import functools
import math

import jax
import jax.numpy as jnp
from jax import lax
from jax.experimental import pallas as pl
from jax.experimental.pallas import tpu as pltpu
from jax.sharding import PartitionSpec as P

HD = 64
MICRO = 2


EPSILON = 1e-05
PRECISE = lax.Precision.HIGHEST
MASKED = -1e30


def layer_norm(values, gain_vec, bias_vec):
    center = values - jnp.mean(values, axis=-1, keepdims=True)
    inverse = lax.rsqrt(jnp.mean(center * center, axis=-1, keepdims=True) + EPSILON)
    scaled = center * inverse
    return (scaled * gain_vec + bias_vec, scaled, inverse)


def norm_back(upstream, scaled, inverse, gain_vec):
    weighted = upstream * gain_vec
    result = inverse * (
        weighted
        - jnp.mean(weighted, axis=-1, keepdims=True)
        - scaled * jnp.mean(weighted * scaled, axis=-1, keepdims=True)
    )
    return (result, jnp.sum(upstream * scaled, axis=(0, 1)), jnp.sum(upstream, axis=(0, 1)))


def spread_rows(values):
    return lax.all_gather(values, "tp", axis=1, tiled=True)


def spread_grads(values):
    return lax.all_gather(values, "tp", axis=1, tiled=True)


def fold_rows(values):
    return lax.psum_scatter(values, "tp", scatter_dimension=1, tiled=True)


def fold_grads(values):
    return lax.psum_scatter(values, "tp", scatter_dimension=1, tiled=True)


def project(left_side, right_side):
    return jnp.einsum("cfd,de->cfe", left_side, right_side, preferred_element_type=jnp.float32)


def project_back(left_side, right_side):
    return jnp.einsum("cfe,de->cfd", left_side, right_side, preferred_element_type=jnp.float32)


def weight_grad(left_side, right_side):
    return jnp.einsum("cfd,cfe->de", left_side, right_side, preferred_element_type=jnp.float32)


def masked_scores(queries, key_rows, allowed):
    factor = 1.0 / math.sqrt(queries.shape[-1])
    scores = (
        jnp.einsum("cqhe,ckhe->chqk", queries, key_rows, preferred_element_type=jnp.float32)
        * factor
    )
    return jnp.where(allowed, scores, MASKED)


def attention_forward(queries, key_rows, value_rows, allowed):
    scores = masked_scores(queries, key_rows, allowed)
    highest = jnp.max(scores, axis=-1, keepdims=True)
    log_total = highest + jnp.log(jnp.sum(jnp.exp(scores - highest), axis=-1, keepdims=True))
    weights = jnp.exp(scores - log_total).astype(jnp.bfloat16)
    mixed = jnp.einsum("chqk,ckhe->cqhe", weights, value_rows, preferred_element_type=jnp.float32)
    return (mixed, log_total)


def score_grads(queries, key_rows, value_rows, allowed, log_total, grad_mixed):
    weights = jnp.exp(masked_scores(queries, key_rows, allowed) - log_total)
    grad_weights = jnp.einsum(
        "cqhe,ckhe->chqk", grad_mixed, value_rows, preferred_element_type=jnp.float32
    )
    row_total = jnp.sum(grad_weights * weights, axis=-1, keepdims=True)
    grad_scores = (weights * (grad_weights - row_total)).astype(jnp.bfloat16)
    return (weights, grad_scores, row_total)


def attention_backward(queries, key_rows, value_rows, allowed, log_total, grad_mixed):
    factor = 1.0 / math.sqrt(queries.shape[-1])
    weights, grad_scores, row_total = score_grads(
        queries, key_rows, value_rows, allowed, log_total, grad_mixed
    )
    grad_queries = (
        jnp.einsum("chqk,ckhe->cqhe", grad_scores, key_rows, preferred_element_type=jnp.float32)
        * factor
    )
    grad_keys = (
        jnp.einsum("chqk,cqhe->ckhe", grad_scores, queries, preferred_element_type=jnp.float32)
        * factor
    )
    grad_values = jnp.einsum(
        "chqk,cqhe->ckhe",
        weights.astype(jnp.bfloat16),
        grad_mixed,
        preferred_element_type=jnp.float32,
    )
    return (grad_queries, grad_keys, grad_values, row_total)


def body(
    tokens,
    memory,
    text_len,
    cotangent,
    gain_one,
    bias_one,
    gain_two,
    bias_two,
    gain_three,
    bias_three,
    w_query,
    w_key,
    w_value,
    w_out,
    c_query,
    c_key,
    c_value,
    c_out,
    w_up,
    w_down,
):
    clips = tokens.shape[1]
    shard_frames = tokens.shape[2] * lax.axis_size("tp")
    text_slots = memory.shape[2]
    local_width = w_query.shape[1]
    local_heads = local_width // HD
    query_pos = lax.axis_index("fsdp") * shard_frames + jnp.arange(shard_frames)
    key_pos = jnp.arange(shard_frames * lax.axis_size("fsdp"))
    causal = (key_pos[None, :] <= query_pos[:, None])[None, None]
    shards = (w_query, w_key, w_value, c_query, c_key, c_value, w_up, w_out, c_out, w_down)
    head_shape = (clips, shard_frames, local_heads, HD)
    text_shape = (clips, text_slots, local_heads, HD)
    outputs = []
    input_grads = []
    text_grads = []
    norm_totals = None
    weight_total = None
    for micro in range(MICRO):
        gathered = (
            lax.all_gather(shards[0], "fsdp", axis=0, tiled=True),
            lax.all_gather(shards[1], "fsdp", axis=0, tiled=True),
            lax.all_gather(shards[2], "fsdp", axis=0, tiled=True),
            lax.all_gather(shards[3], "fsdp", axis=0, tiled=True),
            lax.all_gather(shards[4], "fsdp", axis=0, tiled=True),
            lax.all_gather(shards[5], "fsdp", axis=0, tiled=True),
            lax.all_gather(shards[6], "fsdp", axis=0, tiled=True),
            lax.all_gather(shards[7], "fsdp", axis=1, tiled=True),
            lax.all_gather(shards[8], "fsdp", axis=1, tiled=True),
            lax.all_gather(shards[9], "fsdp", axis=1, tiled=True),
        )
        (
            query_full,
            key_full,
            value_full,
            cross_query,
            cross_key,
            cross_value,
            up_full,
            out_full,
            cross_out,
            down_full,
        ) = gathered
        frames = tokens[micro].astype(jnp.float32)
        text_rows = memory[micro]
        counts = text_len[micro]
        normed_one, scaled_one, inverse_one = layer_norm(frames, gain_one, bias_one)
        rows_one = spread_rows(normed_one.astype(jnp.bfloat16))
        queries = project(rows_one, query_full).astype(jnp.bfloat16).reshape(head_shape)
        key_local = project(rows_one, key_full).astype(jnp.bfloat16)
        value_local = project(rows_one, value_full).astype(jnp.bfloat16)
        key_all, value_all = (
            lax.all_gather(key_local, "fsdp", axis=1, tiled=True),
            lax.all_gather(value_local, "fsdp", axis=1, tiled=True),
        )
        key_all = key_all.reshape(clips, -1, local_heads, HD)
        value_all = value_all.reshape(clips, -1, local_heads, HD)
        mixed_one, total_one = attention_forward(queries, key_all, value_all, causal)
        mixed_one = mixed_one.astype(jnp.bfloat16).reshape(clips, shard_frames, local_width)
        after_self = frames + fold_rows(project(mixed_one, out_full))
        normed_two, scaled_two, inverse_two = layer_norm(after_self, gain_two, bias_two)
        rows_two = spread_rows(normed_two.astype(jnp.bfloat16))
        cross_q = project(rows_two, cross_query).astype(jnp.bfloat16).reshape(head_shape)
        cross_k = project(text_rows, cross_key).astype(jnp.bfloat16).reshape(text_shape)
        cross_v = project(text_rows, cross_value).astype(jnp.bfloat16).reshape(text_shape)
        visible = (jnp.arange(text_slots)[None, :] < counts[:, None])[:, None, None, :]
        mixed_two, total_two = attention_forward(cross_q, cross_k, cross_v, visible)
        mixed_two = mixed_two.astype(jnp.bfloat16).reshape(clips, shard_frames, local_width)
        after_cross = after_self + fold_rows(project(mixed_two, cross_out))
        normed_three, scaled_three, inverse_three = layer_norm(after_cross, gain_three, bias_three)
        rows_three = spread_rows(normed_three.astype(jnp.bfloat16))
        hidden = project(rows_three, up_full)
        active = jax.nn.gelu(hidden).astype(jnp.bfloat16)
        result = after_cross + fold_rows(project(active, down_full))
        outputs.append(result.astype(jnp.bfloat16))
        gathered = (
            lax.all_gather(shards[0], "fsdp", axis=0, tiled=True),
            lax.all_gather(shards[1], "fsdp", axis=0, tiled=True),
            lax.all_gather(shards[2], "fsdp", axis=0, tiled=True),
            lax.all_gather(shards[3], "fsdp", axis=0, tiled=True),
            lax.all_gather(shards[4], "fsdp", axis=0, tiled=True),
            lax.all_gather(shards[5], "fsdp", axis=0, tiled=True),
            lax.all_gather(shards[6], "fsdp", axis=0, tiled=True),
            lax.all_gather(shards[7], "fsdp", axis=1, tiled=True),
            lax.all_gather(shards[8], "fsdp", axis=1, tiled=True),
            lax.all_gather(shards[9], "fsdp", axis=1, tiled=True),
        )
        (
            query_full,
            key_full,
            value_full,
            cross_query,
            cross_key,
            cross_value,
            up_full,
            out_full,
            cross_out,
            down_full,
        ) = gathered
        upstream = cotangent[micro].astype(jnp.float32)
        grad_rows = spread_grads(upstream.astype(jnp.bfloat16))
        grad_down = weight_grad(active, grad_rows)
        grad_active = project_back(grad_rows, down_full)
        _, gelu_pull = jax.vjp(jax.nn.gelu, hidden)
        grad_hidden = gelu_pull(grad_active)[0].astype(jnp.bfloat16)
        grad_up = weight_grad(rows_three, grad_hidden)
        grad_three = fold_grads(project_back(grad_hidden, up_full))
        back_three, gain_g3, bias_g3 = norm_back(
            grad_three, scaled_three, inverse_three, gain_three
        )
        upstream = upstream + back_three
        grad_rows = spread_grads(upstream.astype(jnp.bfloat16))
        grad_cout = weight_grad(mixed_two, grad_rows)
        grad_mixed = project_back(grad_rows, cross_out).astype(jnp.bfloat16).reshape(head_shape)
        grad_cq, grad_ck, grad_cv, _ = attention_backward(
            cross_q, cross_k, cross_v, visible, total_two, grad_mixed
        )
        grad_cq = grad_cq.astype(jnp.bfloat16).reshape(clips, shard_frames, local_width)
        grad_ck = grad_ck.reshape(clips, text_slots, local_width)
        grad_cv = grad_cv.reshape(clips, text_slots, local_width)
        grad_cquery = weight_grad(rows_two, grad_cq)
        text_wide = text_rows.astype(jnp.float32)
        grad_ckey = jnp.einsum("cmd,cme->de", text_wide, grad_ck, precision=PRECISE)
        grad_cvalue = jnp.einsum("cmd,cme->de", text_wide, grad_cv, precision=PRECISE)
        text_grads.append(
            jnp.einsum("cme,de->cmd", grad_ck, cross_key.astype(jnp.float32), precision=PRECISE)
            + jnp.einsum("cme,de->cmd", grad_cv, cross_value.astype(jnp.float32), precision=PRECISE)
        )
        grad_two = fold_grads(project_back(grad_cq, cross_query))
        back_two, gain_g2, bias_g2 = norm_back(grad_two, scaled_two, inverse_two, gain_two)
        upstream = upstream + back_two
        grad_rows = spread_grads(upstream.astype(jnp.bfloat16))
        grad_out = weight_grad(mixed_one, grad_rows)
        grad_mixed = project_back(grad_rows, out_full).astype(jnp.bfloat16).reshape(head_shape)
        grad_q, grad_kall, grad_vall, _ = attention_backward(
            queries, key_all, value_all, causal, total_one, grad_mixed
        )
        grad_kloc, grad_vloc = (
            lax.psum_scatter(
                grad_kall.reshape(clips, -1, local_width).astype(jnp.bfloat16),
                "fsdp",
                scatter_dimension=1,
                tiled=True,
            ).astype(jnp.float32),
            lax.psum_scatter(
                grad_vall.reshape(clips, -1, local_width).astype(jnp.bfloat16),
                "fsdp",
                scatter_dimension=1,
                tiled=True,
            ).astype(jnp.float32),
        )
        grad_q = grad_q.astype(jnp.bfloat16).reshape(clips, shard_frames, local_width)
        grad_kloc = grad_kloc.astype(jnp.bfloat16)
        grad_vloc = grad_vloc.astype(jnp.bfloat16)
        grad_query = weight_grad(rows_one, grad_q)
        grad_key = weight_grad(rows_one, grad_kloc)
        grad_value = weight_grad(rows_one, grad_vloc)
        grad_one = fold_grads(
            project_back(grad_q, query_full)
            + project_back(grad_kloc, key_full)
            + project_back(grad_vloc, value_full)
        )
        back_one, gain_g1, bias_g1 = norm_back(grad_one, scaled_one, inverse_one, gain_one)
        input_grads.append(upstream + back_one)
        norm_parts = (gain_g1, bias_g1, gain_g2, bias_g2, gain_g3, bias_g3)
        norm_totals = norm_parts if micro == 0 else jax.tree.map(jnp.add, norm_totals, norm_parts)
        micro_grads = (
            grad_query,
            grad_key,
            grad_value,
            grad_cquery,
            grad_ckey,
            grad_cvalue,
            grad_up,
            grad_out,
            grad_cout,
            grad_down,
        )
        weight_total = (
            micro_grads if micro == 0 else jax.tree.map(jnp.add, weight_total, micro_grads)
        )
    weight_total = (
        lax.psum_scatter(
            weight_total[0].astype(jnp.bfloat16), "fsdp", scatter_dimension=0, tiled=True
        ).astype(jnp.float32),
        lax.psum_scatter(
            weight_total[1].astype(jnp.bfloat16), "fsdp", scatter_dimension=0, tiled=True
        ).astype(jnp.float32),
        lax.psum_scatter(
            weight_total[2].astype(jnp.bfloat16), "fsdp", scatter_dimension=0, tiled=True
        ).astype(jnp.float32),
        lax.psum_scatter(
            weight_total[3].astype(jnp.bfloat16), "fsdp", scatter_dimension=0, tiled=True
        ).astype(jnp.float32),
        lax.psum_scatter(
            weight_total[4].astype(jnp.bfloat16), "fsdp", scatter_dimension=0, tiled=True
        ).astype(jnp.float32),
        lax.psum_scatter(
            weight_total[5].astype(jnp.bfloat16), "fsdp", scatter_dimension=0, tiled=True
        ).astype(jnp.float32),
        lax.psum_scatter(
            weight_total[6].astype(jnp.bfloat16), "fsdp", scatter_dimension=0, tiled=True
        ).astype(jnp.float32),
        lax.psum_scatter(
            weight_total[7].astype(jnp.bfloat16), "fsdp", scatter_dimension=1, tiled=True
        ).astype(jnp.float32),
        lax.psum_scatter(
            weight_total[8].astype(jnp.bfloat16), "fsdp", scatter_dimension=1, tiled=True
        ).astype(jnp.float32),
        lax.psum_scatter(
            weight_total[9].astype(jnp.bfloat16), "fsdp", scatter_dimension=1, tiled=True
        ).astype(jnp.float32),
    )
    summed = lax.psum(
        (
            jnp.stack(text_grads),
            norm_totals[0],
            norm_totals[1],
            norm_totals[2],
            norm_totals[3],
            norm_totals[4],
            norm_totals[5],
        ),
        ("fsdp", "tp"),
    )
    (
        fin_query,
        fin_key,
        fin_value,
        fin_cquery,
        fin_ckey,
        fin_cvalue,
        fin_up,
        fin_out,
        fin_cout,
        fin_down,
    ) = weight_total
    return (
        jnp.stack(outputs),
        jnp.stack(input_grads),
        summed[0],
        summed[1],
        summed[2],
        summed[3],
        summed[4],
        summed[5],
        summed[6],
        fin_query,
        fin_key,
        fin_value,
        fin_out,
        fin_cquery,
        fin_ckey,
        fin_cvalue,
        fin_cout,
        fin_up,
        fin_down,
    )


BLOCK = 256
SCALE = 1.0 / math.sqrt(HD)
PIECES = 4


def pair_swap(values, axis_name):
    return lax.ppermute(values, axis_name, [(0, 1), (1, 0)])


def ring_shift(values, distance):
    size = lax.axis_size("z")
    return lax.ppermute(values, "z", [(i, (i + distance) % size) for i in range(size)])


def ring_flip(values, bit):
    size = lax.axis_size("z")
    return lax.ppermute(values, "z", [(i, i ^ bit) for i in range(size)])


def take(values, index, axis=0):
    return lax.dynamic_index_in_dim(values, index, axis, keepdims=False)


def place(values, piece, index, axis=0):
    return lax.dynamic_update_index_in_dim(values, piece, index, axis)


def ordered(index, own, other):
    return jnp.where(index == 0, jnp.stack([own, other]), jnp.stack([other, own]))


def wide(values):
    return values.astype(jnp.float32)


def narrow(values):
    return values.astype(jnp.bfloat16)


def exchange_clips(values):
    return lax.all_to_all(values, ("y", "z"), 0, 0, tiled=True)


def group_rows(own):
    across = pair_swap(own, "x")
    return [own, pair_swap(own, "c"), across, pair_swap(across, "c")]


def group_terms(parts):
    far = wide(parts[2]) + wide(pair_swap(parts[3], "c"))
    return [parts[0], pair_swap(parts[1], "c"), pair_swap(narrow(far), "x")]


def everywhere(values):
    for name in ("c", "x", "y"):
        values = values + pair_swap(values, name)
    bit = 1
    while bit < lax.axis_size("z"):
        values = values + ring_flip(values, bit)
        bit *= 2
    return values


def after(values, *others):
    return lax.optimization_barrier((values, others))[0]


def split_heads(shards):
    rows, units = shards[0].shape
    split = jnp.stack([shard.reshape(rows, 2, units // 2) for shard in shards], axis=1)
    return jnp.transpose(split, (2, 0, 1, 3)).reshape(2, rows, -1)


def join_heads(own, away):
    halves = wide(ordered(lax.axis_index("x"), own, away))
    rows, width = own.shape
    halves = halves.reshape(2, rows, 4, width // 4)
    return [jnp.concatenate([halves[0, :, i], halves[1, :, i]], axis=1) for i in range(4)]


def gather_units(shard, gate):
    at_x, at_c = lax.axis_index("x"), lax.axis_index("c")
    rows = shard.shape[0]
    split = jnp.transpose(shard.reshape(rows, 2, 2, -1), (1, 2, 0, 3))
    mine = take(split, at_x)
    other = pair_swap(take(split, 1 - at_x), "x")
    pair = jnp.stack([mine, other], axis=1)
    pair = jnp.stack([take(pair, at_c), pair_swap(take(pair, 1 - at_c), "c")], axis=1)
    own = after(pair.reshape((1, PIECES) + pair.shape[2:]), gate)
    return lax.all_gather(own, ("y", "z"), axis=0, tiled=True)


def sum_units(grad):
    at_x, at_c = lax.axis_index("x"), lax.axis_index("c")
    grad = grad.reshape((-1,) + grad.shape[2:])
    total = lax.psum_scatter(grad, ("y", "z"), scatter_dimension=0, tiled=True)[0]
    away = pair_swap(total[2:], "x")
    pair = ordered(at_x, total[:2], away)
    whole = ordered(at_c, pair[:, 0], pair_swap(pair[:, 1], "c"))
    whole = jnp.transpose(wide(whole), (2, 1, 0, 3))
    return whole.reshape(whole.shape[0], -1)


def gather_whole(shard, gate):
    pieces = [after(shard, gate)]
    for _ in range(1, lax.axis_size("z")):
        pieces.append(ring_shift(pieces[-1], 1))
    pieces = [jnp.stack(pieces)]
    pieces = pieces + [pair_swap(pieces[0], "y")]
    pieces = pieces + [pair_swap(piece, "x") for piece in pieces]
    return pieces + [pair_swap(piece, "c") for piece in pieces]


def fold_pair(kept, sent, name):
    return wide(kept) + wide(pair_swap(sent, name))


def sum_whole(keep, send):
    got = pair_swap(send, "c")
    away = narrow(wide(keep[1]) + wide(got[1]))
    near = narrow(wide(keep[0]) + wide(got[0]))
    got = pair_swap(away, "x")
    away = narrow(wide(near[1]) + wide(got[1]))
    near = narrow(wide(near[0]) + wide(got[0]))
    parts = narrow(wide(near) + wide(pair_swap(away, "y")))
    size = parts.shape[0]
    moving = parts[1]
    for step in range(2, size + 1):
        total = wide(ring_shift(moving, 1)) + wide(parts[step % size])
        moving = narrow(total)
    return total


def dot_nt(left, right):
    return lax.dot_general(left, right, (((1,), (1,)), ((), ())), preferred_element_type=jnp.float32)


def dot_nn(left, right):
    return lax.dot_general(left, right, (((1,), (0,)), ((), ())), preferred_element_type=jnp.float32)


def dot_tn(left, right):
    return lax.dot_general(left, right, (((0,), (0,)), ((), ())), preferred_element_type=jnp.float32)


def whole_spec(array):
    return pl.BlockSpec(array.shape, lambda *_: (0,) * len(array.shape))


ANYWHERE = pl.BlockSpec(memory_space=pl.ANY)
SCALARS = pl.BlockSpec(memory_space=pltpu.SMEM)


def like(shape, dtype=jnp.bfloat16):
    return jax.ShapeDtypeStruct(shape, dtype)


def diagonal_mask(size):
    row = lax.broadcasted_iota(jnp.int32, (size, size), 0)
    column = lax.broadcasted_iota(jnp.int32, (size, size), 1)
    return column <= row


def block_of(at_y, at_x, at_c):
    return (at_y * 2 + at_x) * 2 + at_c


def natural_rows(ids, piece, upper, rows):
    at_x, at_c = ids[1], ids[2]
    member = (at_x ^ (piece // 2)) * 2 + (at_c ^ (piece % 2))
    return pl.ds(pl.multiple_of((upper * PIECES + member) * rows, rows), rows)


def attend_forward_kernel(ids, *refs):
    rows_in, weights = refs[0:4], refs[4]
    parts, qkv, mixed_out, log_out, mixed = refs[5:9], refs[9], refs[10], refs[11], refs[12]
    halves, frames, width = qkv.shape
    third = width // 3
    rows = rows_in[0].shape[0] // 2
    for at in range(halves):
        for piece in range(PIECES):
            out = narrow(dot_nn(rows_in[piece][...], weights[at, :, :width]))
            for upper in range(2):
                qkv[at, natural_rows(ids, piece, upper, rows), :] = out[upper * rows : (upper + 1) * rows]
    mask = diagonal_mask(BLOCK)
    log_out[...] = jnp.zeros_like(log_out)
    lane = lax.broadcasted_iota(jnp.int32, (BLOCK, log_out.shape[1]), 1)

    def half_heads(at, carry):
        for head in range(third // HD):
            q_lanes, k_lanes, v_lanes = (
                slice(i * third + head * HD, i * third + (head + 1) * HD) for i in range(3)
            )
            for start in range(0, frames, BLOCK):
                block = slice(start, start + BLOCK)
                q = qkv[at, block, q_lanes] * jnp.bfloat16(SCALE)
                near = jnp.where(mask, dot_nt(q, qkv[at, block, k_lanes]), MASKED)
                top = jnp.max(near, axis=-1, keepdims=True)
                if start:
                    past = dot_nt(q, qkv[at, 0:start, k_lanes])
                    top = jnp.maximum(top, jnp.max(past, axis=-1, keepdims=True))
                near = jnp.exp(near - top)
                total = jnp.sum(near, axis=-1, keepdims=True)
                out = dot_nn(narrow(near), qkv[at, block, v_lanes])
                if start:
                    past = jnp.exp(past - top)
                    total = total + jnp.sum(past, axis=-1, keepdims=True)
                    out = out + dot_nn(narrow(past), qkv[at, 0:start, v_lanes])
                mixed[at, block, head * HD : (head + 1) * HD] = narrow(out / total)
                log_total = top + jnp.log(total)
                log_out[block, :] = jnp.where(
                    lane == at * (third // HD) + head, log_total, log_out[block, :]
                )
        return carry

    lax.fori_loop(0, halves, half_heads, 0)
    for piece in range(PIECES):
        for upper in range(2):
            here = natural_rows(ids, piece, upper, rows)
            there = slice(upper * rows, (upper + 1) * rows)
            out = None
            for at in range(halves):
                own = mixed[at, here, :]
                mixed_out[at, piece, there, :] = own
                term = dot_nt(own, weights[at, :, width:])
                out = term if out is None else out + term
            parts[piece][there, :] = narrow(out)


def attend_backward_kernel(ids, *refs):
    rows_in, weights = refs[0:4], refs[4]
    qkv, mixed_in, log_in = refs[5], refs[6], refs[7]
    parts, grad_out = refs[8:12], refs[12]
    grads, totals, back, dk_sum, dv_sum = refs[13:18]
    halves, frames, width = qkv.shape
    third = width // 3
    heads = third // HD
    rows = rows_in[0].shape[0] // 2
    for at in range(halves):
        for piece in range(PIECES):
            out = narrow(dot_nn(rows_in[piece][...], weights[at, :, width:]))
            product = wide(out) * wide(mixed_in[at, piece])
            lane = lax.broadcasted_iota(jnp.int32, (2 * rows, totals.shape[2]), 1)
            sums = jnp.zeros((2 * rows, totals.shape[2]), jnp.float32)
            for head in range(heads):
                one = jnp.sum(product[:, head * HD : (head + 1) * HD], axis=-1, keepdims=True)
                sums = jnp.where(lane == head, one, sums)
            for upper in range(2):
                here = natural_rows(ids, piece, upper, rows)
                there = slice(upper * rows, (upper + 1) * rows)
                grads[at, here, :] = out[there]
                totals[at, here, :] = sums[there]
    mask = diagonal_mask(BLOCK)

    def half_heads(at, carry):
        dk_sum[...] = jnp.zeros_like(dk_sum)
        dv_sum[...] = jnp.zeros_like(dv_sum)
        for head in range(heads):
            q_lanes, k_lanes, v_lanes = (
                slice(i * third + head * HD, i * third + (head + 1) * HD) for i in range(3)
            )
            o_lanes = slice(head * HD, (head + 1) * HD)
            log_lane = lax.broadcasted_iota(jnp.int32, (BLOCK, log_in.shape[1]), 1)
            for start in range(0, frames, BLOCK):
                block = slice(start, start + BLOCK)
                q = qkv[at, block, q_lanes] * jnp.bfloat16(SCALE)
                grad = grads[at, block, o_lanes]
                q_turned = narrow(wide(q).T)
                grad_turned = narrow(wide(grad).T)
                log_total = jnp.sum(
                    jnp.where(log_lane == at * heads + head, log_in[block, :], 0.0),
                    axis=-1,
                    keepdims=True,
                )
                row_total = totals[at, block, head : head + 1]
                dq = None
                for columns in (block, slice(0, start)):
                    if columns.stop == 0:
                        continue
                    keys = qkv[at, columns, k_lanes]
                    weight = jnp.exp(dot_nt(q, keys) - log_total)
                    if columns is block:
                        weight = jnp.where(mask, weight, 0.0)
                    grad_weight = dot_nt(grad, qkv[at, columns, v_lanes])
                    scores = narrow(weight * (grad_weight - row_total))
                    part = dot_nn(scores, keys)
                    dq = part if dq is None else dq + part
                    dk_sum[o_lanes, columns] += dot_nn(q_turned, scores)
                    dv_sum[o_lanes, columns] += dot_nn(grad_turned, narrow(weight))
                back[at, block, q_lanes] = narrow(dq * SCALE)
        for start in range(0, frames, BLOCK):
            block = slice(start, start + BLOCK)
            back[at, block, third : 2 * third] = narrow(dk_sum[:, block].T)
            back[at, block, 2 * third :] = narrow(dv_sum[:, block].T)
        return carry

    lax.fori_loop(0, halves, half_heads, 0)
    for piece in range(PIECES):
        for at in range(halves):
            for upper in range(2):
                there = slice(upper * rows, (upper + 1) * rows)
                grad_out[at, piece, there, :] = back[at, natural_rows(ids, piece, upper, rows), :]
        out = None
        for at in range(halves):
            term = dot_nt(grad_out[at, piece], weights[at, :, :width])
            out = term if out is None else out + term
        parts[piece][...] = narrow(out)


def attend_forward(ids, rows_in, weights):
    rows, model = rows_in[0].shape
    halves, _, units = weights.shape
    width = units // 4
    frames = PIECES * rows
    outs = [like((rows, model))] * PIECES + [
        like((halves, frames, 3 * width)),
        like((halves, PIECES, rows, width)),
        like((frames, 128), jnp.float32),
    ]
    out = pl.pallas_call(
        attend_forward_kernel,
        in_specs=[SCALARS] + [pl.BlockSpec(memory_space=pltpu.VMEM)] * (PIECES + 1),
        out_specs=[pl.BlockSpec(memory_space=pltpu.VMEM)] * len(outs),
        out_shape=outs,
        scratch_shapes=[
            pltpu.VMEM((halves, frames, width), jnp.bfloat16),
        ],
        compiler_params=pltpu.CompilerParams(vmem_limit_bytes=56 * 2**20),
        cost_estimate=pl.CostEstimate(
            flops=30 * 10**9, bytes_accessed=24 * 2**20, transcendentals=0
        ),
        name="attend_forward",
    )(ids, *rows_in, weights)
    return out[:4], out[4], out[5], out[6]


def attend_backward(ids, rows_in, weights, qkv, mixed, log_total):
    rows, model = rows_in[0].shape
    halves, _, units = weights.shape
    frames, width = qkv.shape[1], qkv.shape[2] // 3
    outs = [like((rows, model))] * PIECES + [like((halves, PIECES, rows, 3 * width))]
    vmem = pl.BlockSpec(memory_space=pltpu.VMEM)
    out = pl.pallas_call(
        attend_backward_kernel,
        in_specs=[SCALARS] + [vmem] * (PIECES + 4),
        out_specs=[vmem] * len(outs),
        out_shape=outs,
        scratch_shapes=[
            pltpu.VMEM((halves, frames, width), jnp.bfloat16),
            pltpu.VMEM((halves, frames, 128), jnp.float32),
            pltpu.VMEM((halves, frames, 3 * width), jnp.bfloat16),
            pltpu.VMEM((width, frames), jnp.float32),
            pltpu.VMEM((width, frames), jnp.float32),
        ],
        compiler_params=pltpu.CompilerParams(vmem_limit_bytes=58 * 2**20),
        cost_estimate=pl.CostEstimate(
            flops=50 * 10**9, bytes_accessed=24 * 2**20, transcendentals=0
        ),
        name="attend_backward",
    )(ids, *rows_in, weights, qkv, mixed, log_total)
    return out[:4], out[4]


def attend_grads_kernel(ids, *refs):
    normed, grads = refs[0:4], refs[4:8]
    grad_qkv, mixed, out = refs[8:11]
    halves, _, _, width = grad_qkv.shape
    rows = out.shape[-2]
    at_c = ids[2]
    for at in range(halves):
        left = right = None
        for piece in range(PIECES):
            one = dot_tn(normed[piece][...], grad_qkv[at, piece])
            two = dot_tn(grads[piece][...], mixed[at, piece])
            left = one if left is None else left + one
            right = two if right is None else right + two
        for core in range(2):
            block = slice(core * rows, (core + 1) * rows)
            out[at_c ^ core, at, 0, :, :width] = narrow(left[block])
            out[at_c ^ core, at, 0, :, width:] = narrow(right[block])


def attend_grads(ids, normed, grads, grad_qkv, mixed, other_y):
    rows, model = normed[0].shape
    halves, units = mixed.shape[0], 4 * mixed.shape[-1]
    strip = model // 4
    column = pl.BlockSpec((rows, strip), lambda i, ids: (0, (ids[0] ^ other_y) * 2 + i))
    return pl.pallas_call(
        attend_grads_kernel,
        grid_spec=pltpu.PrefetchScalarGridSpec(
            num_scalar_prefetch=1,
            grid=(2,),
            in_specs=[column] * 8 + [whole_spec(grad_qkv), whole_spec(mixed)],
            out_specs=pl.BlockSpec(
                (2, halves, 1, strip // 2, units), lambda i, ids: (0, 0, i ^ ids[1], 0, 0)
            ),
        ),
        out_shape=like((2, halves, 2, strip // 2, units)),
        compiler_params=pltpu.CompilerParams(vmem_limit_bytes=40 * 2**20),
        cost_estimate=pl.CostEstimate(
            flops=6 * 10**9, bytes_accessed=12 * 2**20, transcendentals=0
        ),
        name="attend_grads",
    )(ids, *normed, *grads, grad_qkv, mixed)


def gelu_both(values):
    factor = math.sqrt(2.0 / math.pi)
    square = values * values
    bent = jnp.tanh(factor * values * (1.0 + 0.044715 * square))
    slope = 0.5 * (1.0 + bent) + 0.5 * values * (1.0 - bent * bent) * factor * (
        1.0 + 3.0 * 0.044715 * square
    )
    return 0.5 * values * (1.0 + bent), slope


def feed_kernel(ids, *refs):
    rows_in, grads_in, up_in, down_in = refs[0:4], refs[4:8], refs[8], refs[9]
    result_out, back_out, active_out, hidden_out = refs[10:14], refs[14:18], refs[18], refs[19]
    rows_all, grads_all, up, down, result, back, active, hidden, w_sem, in_sem, out_sem = refs[20:]
    at_x, at_c = ids[1], ids[2]
    rows, model = rows_in[0].shape
    shard_rows, width = up_in.shape[-2:]
    groups = up_in.shape[0] // 2
    copies = []
    for which, (source, target) in enumerate(((up_in, up), (down_in, down))):
        for other_y in range(2):
            for at_z in range(groups):
                for piece in range(PIECES):
                    block = block_of(other_y, at_x ^ (piece // 2), at_c ^ (piece % 2))
                    place_rows = pl.ds(pl.multiple_of(block * shard_rows, shard_rows), shard_rows)
                    lanes = slice((at_z % 2) * width, (at_z % 2 + 1) * width)
                    copies.append(
                        pltpu.make_async_copy(
                            source.at[other_y * groups + at_z, piece],
                            target.at[at_z // 2, place_rows, lanes],
                            w_sem.at[len(copies)],
                        )
                    )
    for piece in range(PIECES):
        copies.append(
            pltpu.make_async_copy(rows_in[piece], rows_all.at[piece], in_sem.at[2 * piece])
        )
        copies.append(
            pltpu.make_async_copy(grads_in[piece], grads_all.at[piece], in_sem.at[2 * piece + 1])
        )
    for copy in copies:
        copy.start()
    for copy in copies:
        copy.wait()
    blocks = groups // 2

    def outputs(piece, slot):
        return [
            pltpu.make_async_copy(source.at[slot], target, out_sem.at[slot, i])
            for i, (source, target) in enumerate(
                (
                    (result, result_out[piece]),
                    (back, back_out[piece]),
                    (active, active_out.at[piece]),
                    (hidden, hidden_out.at[piece]),
                )
            )
        ]

    for piece in range(PIECES):
        slot = piece % 2
        if piece >= 2:
            for copy in outputs(piece - 2, slot):
                copy.wait()

        def one_block(at, carry):
            own = rows_all[piece]
            value, slope = gelu_both(dot_nn(own, up[at]))
            value = narrow(value)
            change = narrow(dot_nn(grads_all[piece], down[at]) * slope)
            lanes = pl.ds(pl.multiple_of(at * 2 * width, 2 * width), 2 * width)
            active[slot, :, lanes] = value
            hidden[slot, :, lanes] = change
            return carry

        lax.fori_loop(0, blocks, one_block, 0)

        def one_result(at, carry):
            here = pl.ds(pl.multiple_of(at * 2 * width, 2 * width), 2 * width)
            first = second = None
            for part in range(blocks):
                lanes = slice(part * 2 * width, (part + 1) * 2 * width)
                one = dot_nt(active[slot, :, lanes], down[part, here, :])
                two = dot_nt(hidden[slot, :, lanes], up[part, here, :])
                first = one if first is None else first + one
                second = two if second is None else second + two
            result[slot, :, here] = narrow(first)
            back[slot, :, here] = narrow(second)
            return carry

        lax.fori_loop(0, model // (2 * width), one_result, 0)
        for copy in outputs(piece, slot):
            copy.start()
    for piece in (PIECES - 2, PIECES - 1):
        for copy in outputs(piece, piece % 2):
            copy.wait()


def feed(ids, rows_in, grads_in, up, down):
    rows, model = rows_in[0].shape
    units = up.shape[0] // 2 * up.shape[-1]
    outs = [like((rows, model))] * 8 + [like((PIECES, rows, units))] * 2
    blocks = up.shape[0] // 4
    weight = pltpu.VMEM((blocks, model, 2 * up.shape[-1]), jnp.bfloat16)
    out = pl.pallas_call(
        feed_kernel,
        in_specs=[SCALARS] + [ANYWHERE] * 10,
        out_specs=[ANYWHERE] * 10,
        out_shape=outs,
        scratch_shapes=[
            pltpu.VMEM((PIECES, rows, model), jnp.bfloat16),
            pltpu.VMEM((PIECES, rows, model), jnp.bfloat16),
            weight,
            weight,
            pltpu.VMEM((2, rows, model), jnp.bfloat16),
            pltpu.VMEM((2, rows, model), jnp.bfloat16),
            pltpu.VMEM((2, rows, units), jnp.bfloat16),
            pltpu.VMEM((2, rows, units), jnp.bfloat16),
            pltpu.SemaphoreType.DMA((2 * up.shape[0] * PIECES,)),
            pltpu.SemaphoreType.DMA((2 * PIECES,)),
            pltpu.SemaphoreType.DMA((2, 4)),
        ],
        compiler_params=pltpu.CompilerParams(vmem_limit_bytes=56 * 2**20),
        cost_estimate=pl.CostEstimate(
            flops=8 * PIECES * rows * model * units, bytes_accessed=36 * 2**20, transcendentals=0
        ),
        name="feed_forward",
    )(ids, *rows_in, *grads_in, up, down)
    return out[0:4], out[4:8], out[8], out[9]


def feed_grads_kernel(ids, *refs):
    left, right, out = refs[0:4], refs[4], refs[5]
    rows, width = out.shape[-2:]
    at_c = ids[2]
    for at_z in range(out.shape[1]):
        total = None
        for piece in range(PIECES):
            one = dot_tn(left[piece][...], right[piece, :, at_z * width : (at_z + 1) * width])
            total = one if total is None else total + one
        for core in range(2):
            out[0, at_z, 0, at_c ^ core] = narrow(total[core * rows : (core + 1) * rows])


def feed_grads(ids, left, right):
    rows, model = left[0].shape
    units = right.shape[-1]
    groups = lax.axis_size("z")
    strip = model // 4
    shape = (2, groups, 2, 2, strip // 2, units // groups)
    out = pl.pallas_call(
        feed_grads_kernel,
        grid_spec=pltpu.PrefetchScalarGridSpec(
            num_scalar_prefetch=1,
            grid=(4,),
            in_specs=[pl.BlockSpec((rows, strip), lambda i, ids: (0, i))] * 4 + [whole_spec(right)],
            out_specs=pl.BlockSpec(
                (1, groups, 1, 2, strip // 2, units // groups),
                lambda i, ids: (i // 2, 0, (i % 2) ^ ids[1], 0, 0, 0),
            ),
        ),
        out_shape=like(shape),
        compiler_params=pltpu.CompilerParams(vmem_limit_bytes=40 * 2**20),
        cost_estimate=pl.CostEstimate(
            flops=2 * PIECES * rows * model * units, bytes_accessed=16 * 2**20, transcendentals=0
        ),
        name="feed_grads",
    )(ids, *left, right)
    return out.reshape(2, groups, PIECES, strip // 2, units // groups)


def block_pair(values):
    low = lax.broadcasted_iota(jnp.int32, values.shape, 1) < HD
    zero = jnp.zeros_like(values)
    return jnp.concatenate([jnp.where(low, values, zero), jnp.where(low, zero, values)], axis=0)


def by_half(low, values, reduce, empty):
    first = reduce(jnp.where(low, values, empty), axis=-1, keepdims=True)
    second = reduce(jnp.where(low, empty, values), axis=-1, keepdims=True)
    return jnp.where(low, first, second)


def cross_weights(count, queries, keys):
    slots = keys.shape[0] // 2
    scores = dot_nt(queries, keys)
    lane = lax.broadcasted_iota(jnp.int32, scores.shape, 1)
    low = lane < slots
    scores = jnp.where(jnp.where(low, lane, lane - slots) < count, scores, MASKED)
    raised = jnp.exp(scores - by_half(low, scores, jnp.max, MASKED))
    return raised / by_half(low, raised, jnp.sum, 0.0), low


def cross_copies(ids, pieces, weights, sem):
    rows = pieces[0].shape[-2]
    copies = []
    for index, piece in enumerate(pieces):
        block = block_of(ids[0] ^ (index % 2), ids[1] ^ (index // 2 % 2), ids[2] ^ (index // 4))
        for distance in range(piece.shape[0]):
            at_z = (ids[3] + piece.shape[0] - distance) % piece.shape[0]
            target = weights.at[at_z, pl.ds(pl.multiple_of(block * rows, rows), rows)]
            copies.append(pltpu.make_async_copy(piece.at[distance], target, sem.at[len(copies)]))
    return copies


def lanes_of(at, size):
    return pl.ds(pl.multiple_of(at * size, size), size)


def cross_forward_kernel(ids, count, *refs):
    tokens, terms, norms, keys_values, pieces = refs[0], refs[1:4], refs[4], refs[5], refs[6:14]
    self_out, normed_out, queries, mixed, cross_out, rows_out = refs[14:20]
    weights, sem = refs[20:22]
    copies = cross_copies(ids, pieces, weights, sem)
    for copy in copies:
        copy.start()
    after_self = wide(tokens[...])
    for term in terms:
        after_self = after_self + wide(term[...])
    self_out[...] = after_self
    normed = narrow(layer_norm(after_self, norms[0:1, :], norms[1:2, :])[0])
    normed_out[...] = normed
    for copy in copies:
        copy.wait()
    width = weights.shape[2] // 2
    model = tokens.shape[1]
    for at in range(weights.shape[0]):
        out = dot_nn(normed_out[...], weights[at, :, :width])
        queries[:, at * width : (at + 1) * width] = narrow(out)

    def one_pair(at, carry):
        lanes = lanes_of(at, 2 * HD)
        query = queries[:, lanes] * jnp.bfloat16(SCALE)
        keys = block_pair(keys_values[:, lanes])
        values = block_pair(keys_values[:, lanes_of(at + model // (2 * HD), 2 * HD)])
        weight, _ = cross_weights(count[0], query, keys)
        mixed[:, lanes] = narrow(dot_nn(narrow(weight), values))
        return carry

    lax.fori_loop(0, model // (2 * HD), one_pair, 0)
    after_cross = self_out[...]
    for at in range(weights.shape[0]):
        after_cross = after_cross + dot_nt(
            mixed[:, at * width : (at + 1) * width], weights[at, :, width:]
        )
    cross_out[...] = after_cross
    rows_out[...] = narrow(layer_norm(after_cross, norms[2:3, :], norms[3:4, :])[0])


def cross_forward(ids, count, tokens, terms, norms, keys_values, pieces):
    rows, model = tokens.shape
    outs = [
        like((rows, model), jnp.float32),
        like((rows, model)),
        like((rows, model)),
        like((rows, model)),
        like((rows, model), jnp.float32),
        like((rows, model)),
    ]
    vmem = pl.BlockSpec(memory_space=pltpu.VMEM)
    size, shard_rows, width = pieces[0].shape
    return pl.pallas_call(
        cross_forward_kernel,
        in_specs=[SCALARS] * 2 + [vmem] * 6 + [ANYWHERE] * 8,
        out_specs=[vmem] * len(outs),
        out_shape=outs,
        scratch_shapes=[
            pltpu.VMEM((size, 8 * shard_rows, width), jnp.bfloat16),
            pltpu.SemaphoreType.DMA((8 * size,)),
        ],
        compiler_params=pltpu.CompilerParams(vmem_limit_bytes=48 * 2**20),
        cost_estimate=pl.CostEstimate(
            flops=12 * 10**9, bytes_accessed=24 * 2**20, transcendentals=0
        ),
        name="cross_forward",
    )(ids, count, tokens, *terms, norms, keys_values, *pieces)


def norm_gradient(upstream, values, gain_vec, bias_vec):
    _, scaled, inverse = layer_norm(values, gain_vec, bias_vec)
    weighted = upstream * gain_vec
    result = inverse * (
        weighted
        - jnp.mean(weighted, axis=-1, keepdims=True)
        - scaled * jnp.mean(weighted * scaled, axis=-1, keepdims=True)
    )
    return (
        result,
        jnp.sum(upstream * scaled, axis=0, keepdims=True),
        jnp.sum(upstream, axis=0, keepdims=True),
    )


def cross_backward_kernel(ids, count, *refs):
    upstream, terms, norms, keys_values = refs[0], refs[1:4], refs[4], refs[5]
    self_in, cross_in, queries, pieces = refs[6], refs[7], refs[8], refs[9:17]
    grad_out, first_out, second_out, dq_out, dkv_out, norm_out = refs[17:23]
    weights, grads, sem = refs[23:26]
    copies = cross_copies(ids, pieces, weights, sem)
    for copy in copies:
        copy.start()
    grad_three = wide(terms[0][...]) + wide(terms[1][...]) + wide(terms[2][...])
    back, gain_g, bias_g = norm_gradient(
        grad_three, cross_in[...], norms[2:3, :], norms[3:4, :]
    )
    norm_out[2:3, :] = gain_g
    norm_out[3:4, :] = bias_g
    grad_two = wide(upstream[...]) + back
    grad_out[...] = grad_two
    second_out[...] = narrow(grad_two)
    for copy in copies:
        copy.wait()
    width = weights.shape[2] // 2
    model = upstream.shape[1]
    slots = keys_values.shape[0]
    for at in range(weights.shape[0]):
        out = dot_nn(second_out[...], weights[at, :, width:])
        grads[:, at * width : (at + 1) * width] = narrow(out)
    dims_low = lax.broadcasted_iota(jnp.int32, (slots, 2 * HD), 1) < HD

    def one_pair(at, carry):
        lanes = lanes_of(at, 2 * HD)
        value_lanes = lanes_of(at + model // (2 * HD), 2 * HD)
        query = queries[:, lanes] * jnp.bfloat16(SCALE)
        keys = block_pair(keys_values[:, lanes])
        weight, low = cross_weights(count[0], query, keys)
        grad = grads[:, lanes]
        grad_weight = dot_nt(grad, block_pair(keys_values[:, value_lanes]))
        scores = weight * (grad_weight - by_half(low, grad_weight * weight, jnp.sum, 0.0))
        scores = narrow(scores)
        dq_out[:, lanes] = narrow(dot_nn(scores, keys) * SCALE)
        dk = dot_tn(scores, query)
        dkv_out[:, lanes] = narrow(jnp.where(dims_low, dk[:slots], dk[slots:]))
        dv = dot_tn(narrow(weight), grad)
        dkv_out[:, value_lanes] = narrow(jnp.where(dims_low, dv[:slots], dv[slots:]))
        return carry

    lax.fori_loop(0, model // (2 * HD), one_pair, 0)
    grad_two_rows = None
    for at in range(weights.shape[0]):
        term = dot_nt(dq_out[:, at * width : (at + 1) * width], weights[at, :, :width])
        grad_two_rows = term if grad_two_rows is None else grad_two_rows + term
    back, gain_g, bias_g = norm_gradient(grad_two_rows, self_in[...], norms[0:1, :], norms[1:2, :])
    norm_out[0:1, :] = gain_g
    norm_out[1:2, :] = bias_g
    grad_one = grad_out[...] + back
    grad_out[...] = grad_one
    first_out[...] = narrow(grad_one)


def cross_backward(
    ids, count, upstream, terms, norms, keys_values, after_self, after_cross, queries, pieces
):
    rows, model = upstream.shape
    slots = keys_values.shape[0]
    outs = [
        like((rows, model), jnp.float32),
        like((rows, model)),
        like((rows, model)),
        like((rows, model)),
        like((slots, 2 * model)),
        like((4, model), jnp.float32),
    ]
    vmem = pl.BlockSpec(memory_space=pltpu.VMEM)
    size, shard_rows, width = pieces[0].shape
    return pl.pallas_call(
        cross_backward_kernel,
        in_specs=[SCALARS] * 2 + [vmem] * 9 + [ANYWHERE] * 8,
        out_specs=[vmem] * len(outs),
        out_shape=outs,
        scratch_shapes=[
            pltpu.VMEM((size, 8 * shard_rows, width), jnp.bfloat16),
            pltpu.VMEM((rows, model), jnp.bfloat16),
            pltpu.SemaphoreType.DMA((8 * size,)),
        ],
        compiler_params=pltpu.CompilerParams(vmem_limit_bytes=56 * 2**20),
        cost_estimate=pl.CostEstimate(
            flops=16 * 10**9, bytes_accessed=28 * 2**20, transcendentals=0
        ),
        name="cross_backward",
    )(
        ids,
        count,
        upstream,
        *terms,
        norms,
        keys_values,
        after_self,
        after_cross,
        queries,
        *pieces,
    )


def cross_grads_kernel(ids, normed, grad_queries, grads, mixed, keep, send):
    size, rows, width = keep.shape[2], keep.shape[3], keep.shape[4] // 2
    first = ids[2] == 0
    for at in range(size):
        lanes = slice(at * width, (at + 1) * width)
        distance = (ids[3] + size - at) % size
        for part, (left, right) in enumerate(((normed, grad_queries), (grads, mixed))):
            out = narrow(dot_tn(left[...], right[:, lanes]))
            there = slice(part * width, (part + 1) * width)
            keep[0, 0, distance, :, there] = jnp.where(first, out[:rows], out[rows:])
            send[0, 0, distance, :, there] = jnp.where(first, out[rows:], out[:rows])


def cross_grads(ids, normed, grad_queries, grads, mixed):
    rows, model = normed.shape
    size = lax.axis_size("z")
    strip = model // 4
    column = pl.BlockSpec((rows, strip), lambda i, ids: (0, i))
    shape = (2, 2, size, strip // 2, 2 * (model // size))
    out = pl.BlockSpec(
        (1, 1) + shape[2:], lambda i, ids: ((i % 2) ^ ids[1], (i // 2) ^ ids[0], 0, 0, 0)
    )
    return pl.pallas_call(
        cross_grads_kernel,
        grid_spec=pltpu.PrefetchScalarGridSpec(
            num_scalar_prefetch=1,
            grid=(4,),
            in_specs=[column, whole_spec(grad_queries), column, whole_spec(mixed)],
            out_specs=[out, out],
        ),
        out_shape=[like(shape), like(shape)],
        compiler_params=pltpu.CompilerParams(vmem_limit_bytes=40 * 2**20),
        cost_estimate=pl.CostEstimate(
            flops=4 * rows * model * model, bytes_accessed=14 * 2**20, transcendentals=0
        ),
        name="cross_grads",
    )(ids, normed, grad_queries, grads, mixed)


MESH = pl.DeviceIdType.MESH


def where_am_i():
    return tuple(lax.axis_index(name) for name in ("y", "x", "c", "z"))


def send_to(source, target, send_sem, recv_sem, device):
    return pltpu.make_async_remote_copy(
        src_ref=source,
        dst_ref=target,
        send_sem=send_sem,
        recv_sem=recv_sem,
        device_id=device,
        device_id_type=MESH,
    )


def groups_around(size):
    at_y, at_x, at_c, at_z = where_am_i()
    return [
        ((at_y + step // size) % 2, at_x, at_c, (at_z + step % size) % size)
        for step in range(2 * size)
    ]


def meet(size):
    at_y, at_x, at_c, at_z = where_am_i()
    others = groups_around(size)[1:]
    others += [(at_y, 1 - at_x, at_c, at_z), (at_y, at_x, 1 - at_c, at_z)]
    barrier = pltpu.get_barrier_semaphore()
    for other in others:
        pl.semaphore_signal(barrier, inc=1, device_id=other, device_id_type=MESH)
    pl.semaphore_wait(barrier, len(others))


def exchange_copies(source, target, size, send_sem, recv_sem):
    at_y, _, _, at_z = where_am_i()
    here = at_y * size + at_z
    copies = []
    for step, group in enumerate(groups_around(size)):
        there = group[0] * size + group[3]
        if step == 0:
            copies.append(pltpu.make_async_copy(source.at[there], target.at[here], recv_sem.at[0]))
        else:
            copies.append(
                send_to(
                    source.at[there], target.at[here], send_sem.at[step], recv_sem.at[step], group
                )
            )
    return copies


def block_rows(at_y, at_x, at_c, rows):
    return pl.ds(pl.multiple_of(((at_y * 2 + at_x) * 2 + at_c) * rows, rows), rows)


def start_kernel(
    size,
    tokens,
    split,
    norm,
    clip_out,
    rows_own,
    rows_c,
    rows_x,
    rows_xc,
    weights,
    held,
    clip,
    normed,
    clip_send,
    clip_recv,
    x_sem,
    ring_send,
    ring_recv,
    y_send,
    y_recv,
    c_send,
    c_recv,
    c_local,
    row_sem,
    out_sem,
):
    at_y, at_x, at_c, at_z = where_am_i()
    rows = split.shape[1]
    half = size // 2
    x_side = (at_y, 1 - at_x, at_c, at_z)
    y_side = (1 - at_y, at_x, at_c, at_z)
    c_side = (at_y, at_x, 1 - at_c, at_z)
    z_next = (at_y, at_x, at_c, (at_z + 1) % size)
    meet(size)
    frames = exchange_copies(tokens, clip, size, clip_send, clip_recv)
    for copy in frames:
        copy.start()
    first = pltpu.make_async_copy(split.at[at_x], held.at[0, 0, 0], out_sem.at[0])
    first.start()
    over = send_to(split.at[1 - at_x], held.at[0, 0, 1], x_sem.at[0], x_sem.at[1], x_side)
    over.start()

    def ring(step, side):
        return send_to(
            held.at[step, 0, side],
            held.at[step + 1, 0, side],
            ring_send.at[step, side],
            ring_recv.at[step, side],
            z_next,
        )

    def across(step, side):
        return send_to(
            held.at[step, 0, side],
            held.at[step, 1, side],
            y_send.at[step, side],
            y_recv.at[step, side],
            y_side,
        )

    def settle(step, other_y, side):
        target = weights.at[
            step % half, block_rows((at_y + other_y) % 2, (at_x + side) % 2, at_c, rows)
        ]
        source = held.at[step, other_y, side]
        slot = (step % half, other_y, side)
        local = pltpu.make_async_copy(source, target, c_local.at[slot])
        remote = send_to(source, target, c_send.at[slot], c_recv.at[slot], c_side)
        return local, remote

    def settle_start(step, other_y, side):
        local, remote = settle(step, other_y, side)

        @pl.when(at_c == step // half)
        def _():
            local.start()

        @pl.when(at_c != step // half)
        def _():
            remote.start()

    for side in range(2):
        if side == 0:
            first.wait()
        else:
            over.wait_recv()
        ring(0, side).start()
        across(0, side).start()
        settle_start(0, 0, side)
    for step in range(1, size):
        if step == size - 1:
            for copy in frames:
                if copy is frames[0]:
                    copy.wait()
                else:
                    copy.wait_recv()
            keep = pltpu.make_async_copy(clip, clip_out, out_sem.at[1])
            keep.start()
            gain, bias = norm[0:1, :], norm[1:2, :]

            def one_block(at, carry):
                here = pl.ds(pl.multiple_of(at * clip.shape[1], clip.shape[1]), clip.shape[1])
                normed[here, :] = narrow(layer_norm(wide(clip[at]), gain, bias)[0])
                return carry

            lax.fori_loop(0, clip.shape[0], one_block, 0)
            own = pltpu.make_async_copy(normed, rows_own, out_sem.at[2])
            to_x = send_to(normed, rows_x, row_sem.at[0], row_sem.at[1], x_side)
            to_c = send_to(normed, rows_c, row_sem.at[2], row_sem.at[3], c_side)
            to_x.start()
            to_c.start()
            own.start()
        for side in range(2):
            ring(step - 1, side).wait_recv()
            if step < size - 1:
                ring(step, side).start()
            across(step, side).start()
            settle_start(step, 0, side)
    for step in range(size):
        for side in range(2):
            across(step, side).wait_recv()
            settle_start(step, 1, side)
    to_x.wait_recv()
    relay = send_to(rows_x, rows_xc, row_sem.at[4], row_sem.at[5], c_side)
    relay.start()
    for step in range(half):
        for other_y in range(2):
            for side in range(2):
                local, remote = settle(step, other_y, side)
                local.wait()
                remote.wait()
    relay.wait()
    to_c.wait()
    to_x.wait_send()
    own.wait()
    keep.wait()
    over.wait_send()
    for copy in frames[1:]:
        copy.wait_send()
    for step in range(size):
        for side in range(2):
            across(step, side).wait_send()
            if step < size - 1:
                ring(step, side).wait_send()


def start_up(tokens, split, norm):
    size = lax.axis_size("z")
    groups, frames, model = tokens.shape
    rows, units = split.shape[1:]
    half = size // 2
    vmem = pl.BlockSpec(memory_space=pltpu.VMEM)
    dma = pltpu.SemaphoreType.DMA
    out = pl.pallas_call(
        functools.partial(start_kernel, size),
        in_specs=[vmem] * 3,
        out_specs=[ANYWHERE] * 6,
        out_shape=[like(tokens.shape)]
        + [like((groups * frames, model))] * PIECES
        + [like((half, 8 * rows, units))],
        scratch_shapes=[
            pltpu.VMEM((size, 2, 2, rows, units), jnp.bfloat16),
            pltpu.VMEM(tokens.shape, jnp.bfloat16),
            pltpu.VMEM((groups * frames, model), jnp.bfloat16),
            dma((groups,)),
            dma((groups,)),
            dma((2,)),
            dma((size - 1, 2)),
            dma((size - 1, 2)),
            dma((size, 2)),
            dma((size, 2)),
            dma((half, 2, 2)),
            dma((half, 2, 2)),
            dma((half, 2, 2)),
            dma((6,)),
            dma((3,)),
        ],
        compiler_params=pltpu.CompilerParams(
            collective_id=1, has_side_effects=True, vmem_limit_bytes=32 * 2**20
        ),
        cost_estimate=pl.CostEstimate(
            flops=10**7, bytes_accessed=200 * 2**20, transcendentals=0
        ),
        name="start_up",
    )(tokens, split, norm)
    return out[0].reshape(-1, model), out[1:5], out[5]


def end_kernel(
    size,
    far,
    near,
    part_own,
    part_c,
    part_x,
    part_xc,
    upstream,
    clip,
    norm,
    norm_in,
    grad_out,
    norm_out,
    unit_own,
    unit_x,
    y_held,
    folded,
    both,
    moved,
    ring_held,
    unit_held,
    core_held,
    x_moved,
    x_held,
    grads,
    grads_held,
    sums,
    sums_held,
    y_send,
    y_recv,
    c_send,
    c_recv,
    core_sem,
    x_sem,
    ring_send,
    ring_recv,
    clip_send,
    clip_recv,
    hop_send,
    hop_recv,
    unit_sem,
    out_sem,
):
    at_y, at_x, at_c, at_z = where_am_i()
    x_side = (at_y, 1 - at_x, at_c, at_z)
    y_side = (1 - at_y, at_x, at_c, at_z)
    c_side = (at_y, at_x, 1 - at_c, at_z)
    z_next = (at_y, at_x, at_c, (at_z + 1) % size)
    half = size // 2
    meet(size)

    def across(core, at, side):
        return send_to(
            far.at[core, at, side],
            y_held.at[core, at, side],
            y_send.at[core, at, side],
            y_recv.at[core, at, side],
            y_side,
        )

    places = [(at, side) for at in range(half) for side in range(2)]
    core_far = send_to(part_xc, core_held.at[1], core_sem.at[0], core_sem.at[1], c_side)
    core_near = send_to(part_c, core_held.at[0], core_sem.at[2], core_sem.at[3], c_side)
    core_far.start()
    for core in (1, 0):
        for at, side in places:
            across(core, at, side).start()
    core_near.start()
    frames = clip.shape[1]

    def rows_of(at):
        return pl.ds(pl.multiple_of(at * frames, frames), frames)

    core_far.wait_recv()

    def add_far(at, carry):
        here = rows_of(at)
        x_moved[here, :] = narrow(wide(part_x[here, :]) + wide(core_held[1, here, :]))
        return carry

    lax.fori_loop(0, clip.shape[0], add_far, 0)
    over = send_to(x_moved, x_held, x_sem.at[0], x_sem.at[1], x_side)
    over.start()

    def to_core(at, side):
        return send_to(
            folded.at[at, side],
            both.at[1, at, side],
            c_send.at[at, side],
            c_recv.at[at, side],
            c_side,
        )

    for at, side in places:
        across(1, at, side).wait_recv()
        folded[at, side] = narrow(wide(near[1, at, side]) + wide(y_held[1, at, side]))
        to_core(at, side).start()
    core_near.wait_recv()
    over.wait_recv()
    sums[...] = jnp.zeros_like(sums)
    sums[2:6, :] = norm_in[...]
    gain, bias = norm[0:1, :], norm[1:2, :]

    def one_block(at, carry):
        here = rows_of(at)
        change = wide(part_own[here, :]) + wide(core_held[0, here, :]) + wide(x_held[here, :])
        back, gain_g, bias_g = norm_gradient(change, wide(clip[at]), gain, bias)
        grads[at] = narrow(upstream[here, :] + back)
        sums[0:1, :] += gain_g
        sums[1:2, :] += bias_g
        return carry

    lax.fori_loop(0, clip.shape[0], one_block, 0)
    exchange = exchange_copies(grads, grads_held, size, clip_send, clip_recv)
    for copy in exchange:
        copy.start()
    hops = [c_side, x_side, y_side]
    for bit in (1, 2):
        low = at_z % 2
        other = (at_z + 1 - 2 * low) if bit == 1 else (at_z + 2) % size
        hops.append((at_y, at_x, at_c, other))

    def hop(number):
        source = sums if number == 0 else sums_held.at[1, number - 1]
        return send_to(
            source, sums_held.at[0, number], hop_send.at[number], hop_recv.at[number], hops[number]
        )

    def hop_next(number):
        hop(number).wait_recv()
        source = sums[...] if number == 0 else sums_held[1, number - 1]
        sums_held[1, number] = source + sums_held[0, number]
        if number + 1 < len(hops):
            hop(number + 1).start()

    hop(0).start()
    hop_next(0)
    for at, side in places:
        across(0, at, side).wait_recv()
        both[0, at, side] = narrow(wide(near[0, at, side]) + wide(y_held[0, at, side]))
    hop_next(1)
    for at, side in places:
        to_core(at, side).wait_recv()

    def chunk(step):
        return ((step // half) + at_c) % 2, step % half

    def ring(step, side):
        source = both.at[chunk(1) + (side,)] if step == 0 else moved.at[step - 1, side]
        return send_to(
            source,
            ring_held.at[step, side],
            ring_send.at[step, side],
            ring_recv.at[step, side],
            z_next,
        )

    for side in range(2):
        ring(0, side).start()
    hop_next(2)
    for step in range(1, size):
        which, at = chunk((step + 1) % size)
        for side in range(2):
            ring(step - 1, side).wait_recv()
            moved[step - 1, side] = narrow(
                wide(ring_held[step - 1, side]) + wide(both[which, at, side])
            )
            if step < size - 1:
                ring(step, side).start()
        if step < size - 1:
            hop_next(2 + step)
    last = send_to(moved.at[size - 2, 1], unit_held, unit_sem.at[0], unit_sem.at[1], x_side)
    last.start()
    for copy in exchange:
        if copy is exchange[0]:
            copy.wait()
        else:
            copy.wait_recv()
    outs = [
        pltpu.make_async_copy(grads_held, grad_out, out_sem.at[0]),
        pltpu.make_async_copy(moved.at[size - 2, 0], unit_own, out_sem.at[1]),
        pltpu.make_async_copy(sums_held.at[1, len(hops) - 1], norm_out, out_sem.at[2]),
    ]
    for copy in outs:
        copy.start()
    last.wait_recv()
    final = pltpu.make_async_copy(unit_held, unit_x, out_sem.at[3])
    final.start()
    for copy in outs:
        copy.wait()
    final.wait()
    last.wait_send()
    core_far.wait_send()
    core_near.wait_send()
    over.wait_send()
    for at, side in places:
        across(0, at, side).wait_send()
        across(1, at, side).wait_send()
        to_core(at, side).wait_send()
    for step in range(size - 1):
        for side in range(2):
            ring(step, side).wait_send()
    for copy in exchange[1:]:
        copy.wait_send()
    for number in range(len(hops)):
        hop(number).wait_send()


def end(far, near, parts, upstream, clip, norm, norm_in):
    size = lax.axis_size("z")
    half = size // 2
    groups, frames, model = clip.shape
    rows, units = far.shape[-2:]
    vmem = pl.BlockSpec(memory_space=pltpu.VMEM)
    dma = pltpu.SemaphoreType.DMA

    def buffer(*shape, dtype=jnp.bfloat16):
        return pltpu.VMEM(shape, dtype)

    return pl.pallas_call(
        functools.partial(end_kernel, size),
        in_specs=[vmem] * 10,
        out_specs=[ANYWHERE] * 4,
        out_shape=[
            like(clip.shape),
            like((8, model), jnp.float32),
            like((rows, units)),
            like((rows, units)),
        ],
        scratch_shapes=[
            buffer(2, half, 2, rows, units),
            buffer(half, 2, rows, units),
            buffer(2, half, 2, rows, units),
            buffer(size - 1, 2, rows, units),
            buffer(size - 1, 2, rows, units),
            buffer(rows, units),
            buffer(2, groups * frames, model),
            buffer(groups * frames, model),
            buffer(groups * frames, model),
            buffer(groups, frames, model),
            buffer(groups, frames, model),
            buffer(8, model, dtype=jnp.float32),
            buffer(2, 5, 8, model, dtype=jnp.float32),
            dma((2, half, 2)),
            dma((2, half, 2)),
            dma((half, 2)),
            dma((half, 2)),
            dma((4,)),
            dma((2,)),
            dma((size - 1, 2)),
            dma((size - 1, 2)),
            dma((groups,)),
            dma((groups,)),
            dma((5,)),
            dma((5,)),
            dma((2,)),
            dma((4,)),
        ],
        compiler_params=pltpu.CompilerParams(
            collective_id=2, has_side_effects=True, vmem_limit_bytes=56 * 2**20
        ),
        cost_estimate=pl.CostEstimate(
            flops=10**7, bytes_accessed=300 * 2**20, transcendentals=0
        ),
        name="end",
    )(far, near, *parts, upstream, clip, norm, norm_in)


def clip_body(
    tokens,
    memory,
    text_len,
    cotangent,
    gain_one,
    bias_one,
    gain_two,
    bias_two,
    gain_three,
    bias_three,
    w_query,
    w_key,
    w_value,
    w_out,
    c_query,
    c_key,
    c_value,
    c_out,
    w_up,
    w_down,
):
    at_y, at_x, at_c, at_z = (lax.axis_index(name) for name in ("y", "x", "c", "z"))
    ids = jnp.stack([at_y, at_x, at_c, at_z]).astype(jnp.int32)
    model = tokens.shape[-1]
    shard_rows, shard_width = w_query.shape
    slots = memory.shape[2]
    size = lax.axis_size("z")
    frame_block = tokens.shape[2]

    split = split_heads([w_query, w_key, w_value, w_out.T])
    norm_one = jnp.stack([gain_one, bias_one])
    clip_tokens, rows_one, attend_weights = start_up(
        tokens.reshape(-1, frame_block, model), split, norm_one
    )
    cross_pieces = gather_whole(jnp.concatenate([c_query, c_out.T], axis=1), clip_tokens)
    upstream = after(cotangent.reshape(-1, frame_block, model), clip_tokens)
    upstream = exchange_clips(upstream).reshape(-1, model)
    up_full = gather_units(w_up, clip_tokens)
    down_full = gather_units(w_down.T, clip_tokens)
    grad_rows3 = group_rows(upstream)

    at_f = block_of(at_y, at_x, at_c)
    text_flat = memory.reshape(-1, model)
    text_mine = lax.dynamic_slice_in_dim(text_flat, at_f * shard_rows, shard_rows, 1)
    text_shard = jnp.concatenate([c_key, c_value], axis=1)
    text_part = narrow(dot_nn(text_mine, text_shard)).reshape(2, -1, slots, 2 * shard_width)
    got = wide(pair_swap(take(text_part, 1 - at_y), "y"))
    text_part = narrow(wide(take(text_part, at_y)) + got)
    text_clip = text_part
    for distance in range(1, size):
        piece = ring_shift(take(text_part, lax.rem(at_z + distance, size)), distance)
        text_clip = place(text_clip, piece, lax.rem(at_z + size - distance, size))
    for name in ("x", "c"):
        text_clip = narrow(wide(text_clip) + wide(pair_swap(text_clip, name)))
    text_clip = text_clip.reshape(size, slots, 2, shard_width)
    keys_values = jnp.transpose(text_clip, (1, 2, 0, 3)).reshape(slots, -1)
    count = take(take(text_len, at_y), at_z).reshape(1)
    norms = jnp.stack([gain_two, bias_two, gain_three, bias_three])

    self_parts, qkv, mixed_one, log_total = attend_forward(ids, rows_one, attend_weights)
    after_self, rows_two, cross_q, mixed_two, after_cross, own_three = cross_forward(
        ids, count, clip_tokens, group_terms(self_parts), norms, keys_values, cross_pieces
    )
    rows_three = group_rows(own_three)

    feed_parts, back_parts, active, grad_hidden = feed(
        ids, rows_three, grad_rows3, up_full, down_full
    )
    back_terms = group_terms(back_parts)
    part_down = feed_grads(ids, grad_rows3, active)
    part_up = feed_grads(ids, rows_three, grad_hidden)
    fin_down, fin_up = sum_units(part_down), sum_units(part_up)
    feed_terms = group_terms(feed_parts)
    result = after_cross + wide(feed_terms[0]) + wide(feed_terms[1]) + wide(feed_terms[2])
    result = narrow(result)
    own_result = result
    result = exchange_clips(result.reshape(-1, frame_block, model)).reshape(tokens.shape)

    grad_one_rows, own_one, own_two, grad_cq, grad_text, norm_grads = cross_backward(
        ids,
        count,
        upstream,
        back_terms,
        norms,
        keys_values,
        after_self,
        after_cross,
        cross_q,
        cross_pieces,
    )
    grad_rows1 = group_rows(own_one)
    cross_keep, cross_send = cross_grads(ids, rows_two, grad_cq, own_two, mixed_two)
    fin_cross = sum_whole(cross_keep, cross_send)
    fin_cquery, fin_cout = fin_cross[:, :shard_width], fin_cross[:, shard_width:].T

    grad_text = grad_text.reshape(slots, 2, size, shard_width)
    grad_text = jnp.transpose(grad_text, (2, 0, 1, 3)).reshape(size, slots, 2 * shard_width)
    for name in ("x", "c"):
        grad_text = narrow(wide(grad_text) + wide(pair_swap(grad_text, name)))
    spread = grad_text
    for distance in range(1, size):
        piece = ring_shift(take(grad_text, lax.rem(at_z + distance, size)), distance)
        spread = place(spread, piece, lax.rem(at_z + size - distance, size))
    spread = ordered(at_y, spread, pair_swap(spread, "y")).reshape(-1, 2 * shard_width)
    fin_text = dot_tn(text_mine, spread)
    fin_ckey, fin_cvalue = fin_text[:, :shard_width], fin_text[:, shard_width:]
    grad_memory = narrow(dot_nt(spread, text_shard))
    bit = 1
    while bit < size:
        grad_memory = narrow(wide(grad_memory) + wide(ring_flip(grad_memory, bit)))
        bit *= 2
    for at, name in ((at_c, "c"), (at_x, "x"), (at_y, "y")):
        grad_memory = ordered(at, grad_memory, pair_swap(grad_memory, name))
    grad_memory = jnp.transpose(grad_memory.reshape(8, -1, shard_rows), (1, 0, 2))
    grad_memory = wide(grad_memory.reshape(memory.shape))

    self_back, grad_qkv = attend_backward(
        after(ids, cross_keep, part_up, part_down, own_result),
        grad_rows1,
        attend_weights,
        qkv,
        mixed_one,
        log_total,
    )
    far = attend_grads(ids, rows_one, grad_rows1, grad_qkv, mixed_one, 1)
    near = attend_grads(ids, rows_one, grad_rows1, grad_qkv, mixed_one, 0)
    input_grad, norm_grads, unit_own, unit_away = end(
        far,
        near,
        self_back,
        grad_one_rows,
        clip_tokens.reshape(-1, frame_block, model),
        norm_one,
        norm_grads,
    )
    input_grad = wide(input_grad).reshape(tokens.shape)
    fin_query, fin_key, fin_value, fin_out = join_heads(unit_own, unit_away)

    return (
        result,
        input_grad,
        grad_memory,
        norm_grads[0],
        norm_grads[1],
        norm_grads[2],
        norm_grads[3],
        norm_grads[4],
        norm_grads[5],
        fin_query,
        fin_key,
        fin_value,
        fin_out.T,
        fin_cquery,
        fin_ckey,
        fin_cvalue,
        fin_cout,
        fin_up,
        fin_down.T,
    )


def clip_groups(mesh):
    outer, inner = mesh.shape["fsdp"], mesh.shape["tp"]
    return (2, 2, 2, inner) if outer == 8 and inner == 4 else None


def solution(mesh):
    sizes = clip_groups(mesh)
    if sizes is None:
        rows, columns, program, used = "fsdp", "tp", body, mesh
    else:
        rows, columns, program = ("y", "x", "c"), "z", clip_body
        used = jax.sharding.Mesh(mesh.devices.reshape(sizes), ("y", "x", "c", "z"))
    both = ("fsdp", "tp") if sizes is None else ("y", "x", "c", "z")
    frames = P(None, None, both, None)
    tall, wide = P(rows, columns), P(columns, rows)
    weights = (tall, tall, tall, wide, tall, tall, tall, wide, tall, wide)
    return jax.shard_map(
        program,
        mesh=used,
        in_specs=(frames, P(), P(), frames) + (P(),) * 6 + weights,
        out_specs=(frames, frames, P()) + (P(),) * 6 + weights,
        check_vma=False,
    )
```

```python
import functools
import math

import jax
import jax.numpy as jnp
from jax import lax
from jax.experimental import pallas as pl
from jax.experimental.pallas import tpu as pltpu
from jax.sharding import PartitionSpec as P

HD = 64
MICRO = 2


EPSILON = 1e-05
PRECISE = lax.Precision.HIGHEST
MASKED = -1e30


def layer_norm(values, gain_vec, bias_vec):
    center = values - jnp.mean(values, axis=-1, keepdims=True)
    inverse = lax.rsqrt(jnp.mean(center * center, axis=-1, keepdims=True) + EPSILON)
    scaled = center * inverse
    return (scaled * gain_vec + bias_vec, scaled, inverse)


def norm_back(upstream, scaled, inverse, gain_vec):
    weighted = upstream * gain_vec
    result = inverse * (
        weighted
        - jnp.mean(weighted, axis=-1, keepdims=True)
        - scaled * jnp.mean(weighted * scaled, axis=-1, keepdims=True)
    )
    return (result, jnp.sum(upstream * scaled, axis=(0, 1)), jnp.sum(upstream, axis=(0, 1)))


def spread_rows(values):
    return lax.all_gather(values, "tp", axis=1, tiled=True)


def spread_grads(values):
    return lax.all_gather(values, "tp", axis=1, tiled=True)


def fold_rows(values):
    return lax.psum_scatter(values, "tp", scatter_dimension=1, tiled=True)


def fold_grads(values):
    return lax.psum_scatter(values, "tp", scatter_dimension=1, tiled=True)


def project(left_side, right_side):
    return jnp.einsum("cfd,de->cfe", left_side, right_side, preferred_element_type=jnp.float32)


def project_back(left_side, right_side):
    return jnp.einsum("cfe,de->cfd", left_side, right_side, preferred_element_type=jnp.float32)


def weight_grad(left_side, right_side):
    return jnp.einsum("cfd,cfe->de", left_side, right_side, preferred_element_type=jnp.float32)


def masked_scores(queries, key_rows, allowed):
    factor = 1.0 / math.sqrt(queries.shape[-1])
    scores = (
        jnp.einsum("cqhe,ckhe->chqk", queries, key_rows, preferred_element_type=jnp.float32)
        * factor
    )
    return jnp.where(allowed, scores, MASKED)


def attention_forward(queries, key_rows, value_rows, allowed):
    scores = masked_scores(queries, key_rows, allowed)
    highest = jnp.max(scores, axis=-1, keepdims=True)
    log_total = highest + jnp.log(jnp.sum(jnp.exp(scores - highest), axis=-1, keepdims=True))
    weights = jnp.exp(scores - log_total).astype(jnp.bfloat16)
    mixed = jnp.einsum("chqk,ckhe->cqhe", weights, value_rows, preferred_element_type=jnp.float32)
    return (mixed, log_total)


def score_grads(queries, key_rows, value_rows, allowed, log_total, grad_mixed):
    weights = jnp.exp(masked_scores(queries, key_rows, allowed) - log_total)
    grad_weights = jnp.einsum(
        "cqhe,ckhe->chqk", grad_mixed, value_rows, preferred_element_type=jnp.float32
    )
    row_total = jnp.sum(grad_weights * weights, axis=-1, keepdims=True)
    grad_scores = (weights * (grad_weights - row_total)).astype(jnp.bfloat16)
    return (weights, grad_scores, row_total)


def attention_backward(queries, key_rows, value_rows, allowed, log_total, grad_mixed):
    factor = 1.0 / math.sqrt(queries.shape[-1])
    weights, grad_scores, row_total = score_grads(
        queries, key_rows, value_rows, allowed, log_total, grad_mixed
    )
    grad_queries = (
        jnp.einsum("chqk,ckhe->cqhe", grad_scores, key_rows, preferred_element_type=jnp.float32)
        * factor
    )
    grad_keys = (
        jnp.einsum("chqk,cqhe->ckhe", grad_scores, queries, preferred_element_type=jnp.float32)
        * factor
    )
    grad_values = jnp.einsum(
        "chqk,cqhe->ckhe",
        weights.astype(jnp.bfloat16),
        grad_mixed,
        preferred_element_type=jnp.float32,
    )
    return (grad_queries, grad_keys, grad_values, row_total)


def body(
    tokens,
    memory,
    text_len,
    cotangent,
    gain_one,
    bias_one,
    gain_two,
    bias_two,
    gain_three,
    bias_three,
    w_query,
    w_key,
    w_value,
    w_out,
    c_query,
    c_key,
    c_value,
    c_out,
    w_up,
    w_down,
):
    clips = tokens.shape[1]
    shard_frames = tokens.shape[2] * lax.axis_size("tp")
    text_slots = memory.shape[2]
    local_width = w_query.shape[1]
    local_heads = local_width // HD
    query_pos = lax.axis_index("fsdp") * shard_frames + jnp.arange(shard_frames)
    key_pos = jnp.arange(shard_frames * lax.axis_size("fsdp"))
    causal = (key_pos[None, :] <= query_pos[:, None])[None, None]
    shards = (w_query, w_key, w_value, c_query, c_key, c_value, w_up, w_out, c_out, w_down)
    head_shape = (clips, shard_frames, local_heads, HD)
    text_shape = (clips, text_slots, local_heads, HD)
    outputs = []
    input_grads = []
    text_grads = []
    norm_totals = None
    weight_total = None
    for micro in range(MICRO):
        gathered = (
            lax.all_gather(shards[0], "fsdp", axis=0, tiled=True),
            lax.all_gather(shards[1], "fsdp", axis=0, tiled=True),
            lax.all_gather(shards[2], "fsdp", axis=0, tiled=True),
            lax.all_gather(shards[3], "fsdp", axis=0, tiled=True),
            lax.all_gather(shards[4], "fsdp", axis=0, tiled=True),
            lax.all_gather(shards[5], "fsdp", axis=0, tiled=True),
            lax.all_gather(shards[6], "fsdp", axis=0, tiled=True),
            lax.all_gather(shards[7], "fsdp", axis=1, tiled=True),
            lax.all_gather(shards[8], "fsdp", axis=1, tiled=True),
            lax.all_gather(shards[9], "fsdp", axis=1, tiled=True),
        )
        (
            query_full,
            key_full,
            value_full,
            cross_query,
            cross_key,
            cross_value,
            up_full,
            out_full,
            cross_out,
            down_full,
        ) = gathered
        frames = tokens[micro].astype(jnp.float32)
        text_rows = memory[micro]
        counts = text_len[micro]
        normed_one, scaled_one, inverse_one = layer_norm(frames, gain_one, bias_one)
        rows_one = spread_rows(normed_one.astype(jnp.bfloat16))
        queries = project(rows_one, query_full).astype(jnp.bfloat16).reshape(head_shape)
        key_local = project(rows_one, key_full).astype(jnp.bfloat16)
        value_local = project(rows_one, value_full).astype(jnp.bfloat16)
        key_all, value_all = (
            lax.all_gather(key_local, "fsdp", axis=1, tiled=True),
            lax.all_gather(value_local, "fsdp", axis=1, tiled=True),
        )
        key_all = key_all.reshape(clips, -1, local_heads, HD)
        value_all = value_all.reshape(clips, -1, local_heads, HD)
        mixed_one, total_one = attention_forward(queries, key_all, value_all, causal)
        mixed_one = mixed_one.astype(jnp.bfloat16).reshape(clips, shard_frames, local_width)
        after_self = frames + fold_rows(project(mixed_one, out_full))
        normed_two, scaled_two, inverse_two = layer_norm(after_self, gain_two, bias_two)
        rows_two = spread_rows(normed_two.astype(jnp.bfloat16))
        cross_q = project(rows_two, cross_query).astype(jnp.bfloat16).reshape(head_shape)
        cross_k = project(text_rows, cross_key).astype(jnp.bfloat16).reshape(text_shape)
        cross_v = project(text_rows, cross_value).astype(jnp.bfloat16).reshape(text_shape)
        visible = (jnp.arange(text_slots)[None, :] < counts[:, None])[:, None, None, :]
        mixed_two, total_two = attention_forward(cross_q, cross_k, cross_v, visible)
        mixed_two = mixed_two.astype(jnp.bfloat16).reshape(clips, shard_frames, local_width)
        after_cross = after_self + fold_rows(project(mixed_two, cross_out))
        normed_three, scaled_three, inverse_three = layer_norm(after_cross, gain_three, bias_three)
        rows_three = spread_rows(normed_three.astype(jnp.bfloat16))
        hidden = project(rows_three, up_full)
        active = jax.nn.gelu(hidden).astype(jnp.bfloat16)
        result = after_cross + fold_rows(project(active, down_full))
        outputs.append(result.astype(jnp.bfloat16))
        gathered = (
            lax.all_gather(shards[0], "fsdp", axis=0, tiled=True),
            lax.all_gather(shards[1], "fsdp", axis=0, tiled=True),
            lax.all_gather(shards[2], "fsdp", axis=0, tiled=True),
            lax.all_gather(shards[3], "fsdp", axis=0, tiled=True),
            lax.all_gather(shards[4], "fsdp", axis=0, tiled=True),
            lax.all_gather(shards[5], "fsdp", axis=0, tiled=True),
            lax.all_gather(shards[6], "fsdp", axis=0, tiled=True),
            lax.all_gather(shards[7], "fsdp", axis=1, tiled=True),
            lax.all_gather(shards[8], "fsdp", axis=1, tiled=True),
            lax.all_gather(shards[9], "fsdp", axis=1, tiled=True),
        )
        (
            query_full,
            key_full,
            value_full,
            cross_query,
            cross_key,
            cross_value,
            up_full,
            out_full,
            cross_out,
            down_full,
        ) = gathered
        upstream = cotangent[micro].astype(jnp.float32)
        grad_rows = spread_grads(upstream.astype(jnp.bfloat16))
        grad_down = weight_grad(active, grad_rows)
        grad_active = project_back(grad_rows, down_full)
        _, gelu_pull = jax.vjp(jax.nn.gelu, hidden)
        grad_hidden = gelu_pull(grad_active)[0].astype(jnp.bfloat16)
        grad_up = weight_grad(rows_three, grad_hidden)
        grad_three = fold_grads(project_back(grad_hidden, up_full))
        back_three, gain_g3, bias_g3 = norm_back(
            grad_three, scaled_three, inverse_three, gain_three
        )
        upstream = upstream + back_three
        grad_rows = spread_grads(upstream.astype(jnp.bfloat16))
        grad_cout = weight_grad(mixed_two, grad_rows)
        grad_mixed = project_back(grad_rows, cross_out).astype(jnp.bfloat16).reshape(head_shape)
        grad_cq, grad_ck, grad_cv, _ = attention_backward(
            cross_q, cross_k, cross_v, visible, total_two, grad_mixed
        )
        grad_cq = grad_cq.astype(jnp.bfloat16).reshape(clips, shard_frames, local_width)
        grad_ck = grad_ck.reshape(clips, text_slots, local_width)
        grad_cv = grad_cv.reshape(clips, text_slots, local_width)
        grad_cquery = weight_grad(rows_two, grad_cq)
        text_wide = text_rows.astype(jnp.float32)
        grad_ckey = jnp.einsum("cmd,cme->de", text_wide, grad_ck, precision=PRECISE)
        grad_cvalue = jnp.einsum("cmd,cme->de", text_wide, grad_cv, precision=PRECISE)
        text_grads.append(
            jnp.einsum("cme,de->cmd", grad_ck, cross_key.astype(jnp.float32), precision=PRECISE)
            + jnp.einsum("cme,de->cmd", grad_cv, cross_value.astype(jnp.float32), precision=PRECISE)
        )
        grad_two = fold_grads(project_back(grad_cq, cross_query))
        back_two, gain_g2, bias_g2 = norm_back(grad_two, scaled_two, inverse_two, gain_two)
        upstream = upstream + back_two
        grad_rows = spread_grads(upstream.astype(jnp.bfloat16))
        grad_out = weight_grad(mixed_one, grad_rows)
        grad_mixed = project_back(grad_rows, out_full).astype(jnp.bfloat16).reshape(head_shape)
        grad_q, grad_kall, grad_vall, _ = attention_backward(
            queries, key_all, value_all, causal, total_one, grad_mixed
        )
        grad_kloc, grad_vloc = (
            lax.psum_scatter(
                grad_kall.reshape(clips, -1, local_width).astype(jnp.bfloat16),
                "fsdp",
                scatter_dimension=1,
                tiled=True,
            ).astype(jnp.float32),
            lax.psum_scatter(
                grad_vall.reshape(clips, -1, local_width).astype(jnp.bfloat16),
                "fsdp",
                scatter_dimension=1,
                tiled=True,
            ).astype(jnp.float32),
        )
        grad_q = grad_q.astype(jnp.bfloat16).reshape(clips, shard_frames, local_width)
        grad_kloc = grad_kloc.astype(jnp.bfloat16)
        grad_vloc = grad_vloc.astype(jnp.bfloat16)
        grad_query = weight_grad(rows_one, grad_q)
        grad_key = weight_grad(rows_one, grad_kloc)
        grad_value = weight_grad(rows_one, grad_vloc)
        grad_one = fold_grads(
            project_back(grad_q, query_full)
            + project_back(grad_kloc, key_full)
            + project_back(grad_vloc, value_full)
        )
        back_one, gain_g1, bias_g1 = norm_back(grad_one, scaled_one, inverse_one, gain_one)
        input_grads.append(upstream + back_one)
        norm_parts = (gain_g1, bias_g1, gain_g2, bias_g2, gain_g3, bias_g3)
        norm_totals = norm_parts if micro == 0 else jax.tree.map(jnp.add, norm_totals, norm_parts)
        micro_grads = (
            grad_query,
            grad_key,
            grad_value,
            grad_cquery,
            grad_ckey,
            grad_cvalue,
            grad_up,
            grad_out,
            grad_cout,
            grad_down,
        )
        weight_total = (
            micro_grads if micro == 0 else jax.tree.map(jnp.add, weight_total, micro_grads)
        )
    weight_total = (
        lax.psum_scatter(
            weight_total[0].astype(jnp.bfloat16), "fsdp", scatter_dimension=0, tiled=True
        ).astype(jnp.float32),
        lax.psum_scatter(
            weight_total[1].astype(jnp.bfloat16), "fsdp", scatter_dimension=0, tiled=True
        ).astype(jnp.float32),
        lax.psum_scatter(
            weight_total[2].astype(jnp.bfloat16), "fsdp", scatter_dimension=0, tiled=True
        ).astype(jnp.float32),
        lax.psum_scatter(
            weight_total[3].astype(jnp.bfloat16), "fsdp", scatter_dimension=0, tiled=True
        ).astype(jnp.float32),
        lax.psum_scatter(
            weight_total[4].astype(jnp.bfloat16), "fsdp", scatter_dimension=0, tiled=True
        ).astype(jnp.float32),
        lax.psum_scatter(
            weight_total[5].astype(jnp.bfloat16), "fsdp", scatter_dimension=0, tiled=True
        ).astype(jnp.float32),
        lax.psum_scatter(
            weight_total[6].astype(jnp.bfloat16), "fsdp", scatter_dimension=0, tiled=True
        ).astype(jnp.float32),
        lax.psum_scatter(
            weight_total[7].astype(jnp.bfloat16), "fsdp", scatter_dimension=1, tiled=True
        ).astype(jnp.float32),
        lax.psum_scatter(
            weight_total[8].astype(jnp.bfloat16), "fsdp", scatter_dimension=1, tiled=True
        ).astype(jnp.float32),
        lax.psum_scatter(
            weight_total[9].astype(jnp.bfloat16), "fsdp", scatter_dimension=1, tiled=True
        ).astype(jnp.float32),
    )
    summed = lax.psum(
        (
            jnp.stack(text_grads),
            norm_totals[0],
            norm_totals[1],
            norm_totals[2],
            norm_totals[3],
            norm_totals[4],
            norm_totals[5],
        ),
        ("fsdp", "tp"),
    )
    (
        fin_query,
        fin_key,
        fin_value,
        fin_cquery,
        fin_ckey,
        fin_cvalue,
        fin_up,
        fin_out,
        fin_cout,
        fin_down,
    ) = weight_total
    return (
        jnp.stack(outputs),
        jnp.stack(input_grads),
        summed[0],
        summed[1],
        summed[2],
        summed[3],
        summed[4],
        summed[5],
        summed[6],
        fin_query,
        fin_key,
        fin_value,
        fin_out,
        fin_cquery,
        fin_ckey,
        fin_cvalue,
        fin_cout,
        fin_up,
        fin_down,
    )


BLOCK = 256
SCALE = 1.0 / math.sqrt(HD)
PIECES = 4


def pair_swap(values, axis_name):
    return lax.ppermute(values, axis_name, [(0, 1), (1, 0)])


def ring_shift(values, distance):
    size = lax.axis_size("z")
    return lax.ppermute(values, "z", [(i, (i + distance) % size) for i in range(size)])


def ring_flip(values, bit):
    size = lax.axis_size("z")
    return lax.ppermute(values, "z", [(i, i ^ bit) for i in range(size)])


def take(values, index, axis=0):
    return lax.dynamic_index_in_dim(values, index, axis, keepdims=False)


def place(values, piece, index, axis=0):
    return lax.dynamic_update_index_in_dim(values, piece, index, axis)


def ordered(index, own, other):
    return jnp.where(index == 0, jnp.stack([own, other]), jnp.stack([other, own]))


def wide(values):
    return values.astype(jnp.float32)


def narrow(values):
    return values.astype(jnp.bfloat16)


def exchange_clips(values):
    return lax.all_to_all(values, ("y", "z"), 0, 0, tiled=True)


def group_rows(own):
    across = pair_swap(own, "x")
    return [own, pair_swap(own, "c"), across, pair_swap(across, "c")]


def group_terms(parts):
    far = wide(parts[2]) + wide(pair_swap(parts[3], "c"))
    return [parts[0], pair_swap(parts[1], "c"), pair_swap(narrow(far), "x")]


def everywhere(values):
    for name in ("c", "x", "y"):
        values = values + pair_swap(values, name)
    bit = 1
    while bit < lax.axis_size("z"):
        values = values + ring_flip(values, bit)
        bit *= 2
    return values


def after(values, *others):
    return lax.optimization_barrier((values, others))[0]


def split_heads(shards):
    rows, units = shards[0].shape
    split = jnp.stack([shard.reshape(rows, 2, units // 2) for shard in shards], axis=1)
    return jnp.transpose(split, (2, 0, 1, 3)).reshape(2, rows, -1)


def join_heads(own, away):
    halves = wide(ordered(lax.axis_index("x"), own, away))
    rows, width = own.shape
    halves = halves.reshape(2, rows, 4, width // 4)
    return [jnp.concatenate([halves[0, :, i], halves[1, :, i]], axis=1) for i in range(4)]


def gather_units(shards):
    at_x, at_c = lax.axis_index("x"), lax.axis_index("c")
    rows, units = shards[0].shape
    split = jnp.stack([shard.reshape(rows, 2, 2, units // 4) for shard in shards])
    split = jnp.transpose(split, (2, 3, 0, 1, 4))
    mine = take(split, at_x)
    other = pair_swap(take(split, 1 - at_x), "x")
    pair = jnp.stack([mine, other], axis=1)
    pair = jnp.stack([take(pair, at_c), pair_swap(take(pair, 1 - at_c), "c")], axis=1)
    own = pair.reshape((1, PIECES) + pair.shape[2:])
    return lax.all_gather(own, ("y", "z"), axis=0, tiled=True)


def scatter_units(grad):
    grad = grad.reshape((-1,) + grad.shape[2:])
    return lax.psum_scatter(grad, ("y", "z"), scatter_dimension=0, tiled=True)[0]


def join_units(total):
    at_x, at_c = lax.axis_index("x"), lax.axis_index("c")
    away = pair_swap(total[2:], "x")
    pair = ordered(at_x, total[:2], away)
    whole = ordered(at_c, pair[:, 0], pair_swap(pair[:, 1], "c"))
    whole = jnp.transpose(wide(whole), (2, 1, 0, 3))
    return whole.reshape(whole.shape[0], -1)


def sum_plane(keep, send, gate):
    got = pair_swap(send, "c")
    away = narrow(wide(keep[1]) + wide(got[1]))
    near = narrow(wide(keep[0]) + wide(got[0]))
    return near, pair_swap(after(away, gate), "x")


def sum_plane_rest(near, got):
    away = narrow(wide(near[1]) + wide(got[1]))
    near = narrow(wide(near[0]) + wide(got[0]))
    return narrow(wide(near) + wide(pair_swap(away, "y")))


def dot_nt(left, right):
    return lax.dot_general(left, right, (((1,), (1,)), ((), ())), preferred_element_type=jnp.float32)


def dot_nn(left, right):
    return lax.dot_general(left, right, (((1,), (0,)), ((), ())), preferred_element_type=jnp.float32)


def dot_tn(left, right):
    return lax.dot_general(left, right, (((0,), (0,)), ((), ())), preferred_element_type=jnp.float32)


def whole_spec(array):
    return pl.BlockSpec(array.shape, lambda *_: (0,) * len(array.shape))


ANYWHERE = pl.BlockSpec(memory_space=pl.ANY)
SCALARS = pl.BlockSpec(memory_space=pltpu.SMEM)


def like(shape, dtype=jnp.bfloat16):
    return jax.ShapeDtypeStruct(shape, dtype)


def diagonal_mask(size):
    row = lax.broadcasted_iota(jnp.int32, (size, size), 0)
    column = lax.broadcasted_iota(jnp.int32, (size, size), 1)
    return column <= row


def block_of(at_y, at_x, at_c):
    return (at_y * 2 + at_x) * 2 + at_c


def natural_rows(ids, piece, upper, rows):
    at_x, at_c = ids[1], ids[2]
    member = (at_x ^ (piece // 2)) * 2 + (at_c ^ (piece % 2))
    return pl.ds(pl.multiple_of((upper * PIECES + member) * rows, rows), rows)


def attend_forward_kernel(ids, *refs):
    rows_in, weights = refs[0:4], refs[4]
    parts, qkv, mixed_out, log_out, mixed = refs[5:9], refs[9], refs[10], refs[11], refs[12]
    halves, frames, width = qkv.shape
    third = width // 3
    rows = rows_in[0].shape[0] // 2
    for at in range(halves):
        for piece in range(PIECES):
            out = narrow(dot_nn(rows_in[piece][...], weights[at, :, :width]))
            for upper in range(2):
                qkv[at, natural_rows(ids, piece, upper, rows), :] = out[upper * rows : (upper + 1) * rows]
    mask = diagonal_mask(BLOCK)
    log_out[...] = jnp.zeros_like(log_out)
    lane = lax.broadcasted_iota(jnp.int32, (BLOCK, log_out.shape[1]), 1)

    def half_heads(at, carry):
        for head in range(third // HD):
            q_lanes, k_lanes, v_lanes = (
                slice(i * third + head * HD, i * third + (head + 1) * HD) for i in range(3)
            )
            for start in range(0, frames, BLOCK):
                block = slice(start, start + BLOCK)
                q = qkv[at, block, q_lanes] * jnp.bfloat16(SCALE)
                near = jnp.where(mask, dot_nt(q, qkv[at, block, k_lanes]), MASKED)
                top = jnp.max(near, axis=-1, keepdims=True)
                if start:
                    past = dot_nt(q, qkv[at, 0:start, k_lanes])
                    top = jnp.maximum(top, jnp.max(past, axis=-1, keepdims=True))
                near = jnp.exp(near - top)
                total = jnp.sum(near, axis=-1, keepdims=True)
                out = dot_nn(narrow(near), qkv[at, block, v_lanes])
                if start:
                    past = jnp.exp(past - top)
                    total = total + jnp.sum(past, axis=-1, keepdims=True)
                    out = out + dot_nn(narrow(past), qkv[at, 0:start, v_lanes])
                mixed[at, block, head * HD : (head + 1) * HD] = narrow(out / total)
                log_total = top + jnp.log(total)
                log_out[block, :] = jnp.where(
                    lane == at * (third // HD) + head, log_total, log_out[block, :]
                )
        return carry

    lax.fori_loop(0, halves, half_heads, 0)
    for piece in range(PIECES):
        for upper in range(2):
            here = natural_rows(ids, piece, upper, rows)
            there = slice(upper * rows, (upper + 1) * rows)
            out = None
            for at in range(halves):
                own = mixed[at, here, :]
                mixed_out[at, piece, there, :] = own
                term = dot_nt(own, weights[at, :, width:])
                out = term if out is None else out + term
            parts[piece][there, :] = narrow(out)


def attend_backward_kernel(ids, *refs):
    rows_in, weights = refs[0:4], refs[4]
    qkv, mixed_in, log_in = refs[5], refs[6], refs[7]
    parts, grad_out = refs[8:12], refs[12]
    grads, totals, back, dk_sum, dv_sum = refs[13:18]
    halves, frames, width = qkv.shape
    third = width // 3
    heads = third // HD
    rows = rows_in[0].shape[0] // 2
    for at in range(halves):
        for piece in range(PIECES):
            out = narrow(dot_nn(rows_in[piece][...], weights[at, :, width:]))
            product = wide(out) * wide(mixed_in[at, piece])
            lane = lax.broadcasted_iota(jnp.int32, (2 * rows, totals.shape[2]), 1)
            sums = jnp.zeros((2 * rows, totals.shape[2]), jnp.float32)
            for head in range(heads):
                one = jnp.sum(product[:, head * HD : (head + 1) * HD], axis=-1, keepdims=True)
                sums = jnp.where(lane == head, one, sums)
            for upper in range(2):
                here = natural_rows(ids, piece, upper, rows)
                there = slice(upper * rows, (upper + 1) * rows)
                grads[at, here, :] = out[there]
                totals[at, here, :] = sums[there]
    mask = diagonal_mask(BLOCK)

    def half_heads(at, carry):
        dk_sum[...] = jnp.zeros_like(dk_sum)
        dv_sum[...] = jnp.zeros_like(dv_sum)
        for head in range(heads):
            q_lanes, k_lanes, v_lanes = (
                slice(i * third + head * HD, i * third + (head + 1) * HD) for i in range(3)
            )
            o_lanes = slice(head * HD, (head + 1) * HD)
            log_lane = lax.broadcasted_iota(jnp.int32, (BLOCK, log_in.shape[1]), 1)
            for start in range(0, frames, BLOCK):
                block = slice(start, start + BLOCK)
                q = qkv[at, block, q_lanes] * jnp.bfloat16(SCALE)
                grad = grads[at, block, o_lanes]
                q_turned = narrow(wide(q).T)
                grad_turned = narrow(wide(grad).T)
                log_total = jnp.sum(
                    jnp.where(log_lane == at * heads + head, log_in[block, :], 0.0),
                    axis=-1,
                    keepdims=True,
                )
                row_total = totals[at, block, head : head + 1]
                dq = None
                for columns in (block, slice(0, start)):
                    if columns.stop == 0:
                        continue
                    keys = qkv[at, columns, k_lanes]
                    weight = jnp.exp(dot_nt(q, keys) - log_total)
                    if columns is block:
                        weight = jnp.where(mask, weight, 0.0)
                    grad_weight = dot_nt(grad, qkv[at, columns, v_lanes])
                    scores = narrow(weight * (grad_weight - row_total))
                    part = dot_nn(scores, keys)
                    dq = part if dq is None else dq + part
                    dk_sum[o_lanes, columns] += dot_nn(q_turned, scores)
                    dv_sum[o_lanes, columns] += dot_nn(grad_turned, narrow(weight))
                back[at, block, q_lanes] = narrow(dq * SCALE)
        for start in range(0, frames, BLOCK):
            block = slice(start, start + BLOCK)
            back[at, block, third : 2 * third] = narrow(dk_sum[:, block].T)
            back[at, block, 2 * third :] = narrow(dv_sum[:, block].T)
        return carry

    lax.fori_loop(0, halves, half_heads, 0)
    for piece in range(PIECES):
        for at in range(halves):
            for upper in range(2):
                there = slice(upper * rows, (upper + 1) * rows)
                grad_out[at, piece, there, :] = back[at, natural_rows(ids, piece, upper, rows), :]
        out = None
        for at in range(halves):
            term = dot_nt(grad_out[at, piece], weights[at, :, :width])
            out = term if out is None else out + term
        parts[piece][...] = narrow(out)


def attend_forward(ids, rows_in, weights):
    rows, model = rows_in[0].shape
    halves, _, units = weights.shape
    width = units // 4
    frames = PIECES * rows
    outs = [like((rows, model))] * PIECES + [
        like((halves, frames, 3 * width)),
        like((halves, PIECES, rows, width)),
        like((frames, 128), jnp.float32),
    ]
    out = pl.pallas_call(
        attend_forward_kernel,
        in_specs=[SCALARS] + [pl.BlockSpec(memory_space=pltpu.VMEM)] * (PIECES + 1),
        out_specs=[pl.BlockSpec(memory_space=pltpu.VMEM)] * len(outs),
        out_shape=outs,
        scratch_shapes=[
            pltpu.VMEM((halves, frames, width), jnp.bfloat16),
        ],
        compiler_params=pltpu.CompilerParams(vmem_limit_bytes=56 * 2**20),
        cost_estimate=pl.CostEstimate(
            flops=30 * 10**9, bytes_accessed=24 * 2**20, transcendentals=0
        ),
        name="attend_forward",
    )(ids, *rows_in, weights)
    return out[:4], out[4], out[5], out[6]


def attend_backward(ids, rows_in, weights, qkv, mixed, log_total):
    rows, model = rows_in[0].shape
    halves, _, units = weights.shape
    frames, width = qkv.shape[1], qkv.shape[2] // 3
    outs = [like((rows, model))] * PIECES + [like((halves, PIECES, rows, 3 * width))]
    vmem = pl.BlockSpec(memory_space=pltpu.VMEM)
    out = pl.pallas_call(
        attend_backward_kernel,
        in_specs=[SCALARS] + [vmem] * (PIECES + 4),
        out_specs=[vmem] * len(outs),
        out_shape=outs,
        scratch_shapes=[
            pltpu.VMEM((halves, frames, width), jnp.bfloat16),
            pltpu.VMEM((halves, frames, 128), jnp.float32),
            pltpu.VMEM((halves, frames, 3 * width), jnp.bfloat16),
            pltpu.VMEM((width, frames), jnp.float32),
            pltpu.VMEM((width, frames), jnp.float32),
        ],
        compiler_params=pltpu.CompilerParams(vmem_limit_bytes=58 * 2**20),
        cost_estimate=pl.CostEstimate(
            flops=50 * 10**9, bytes_accessed=24 * 2**20, transcendentals=0
        ),
        name="attend_backward",
    )(ids, *rows_in, weights, qkv, mixed, log_total)
    return out[:4], out[4]


def attend_grads_kernel(ids, *refs):
    normed, grads = refs[0:4], refs[4:8]
    grad_qkv, mixed, out = refs[8:11]
    halves, _, _, width = grad_qkv.shape
    rows = out.shape[-2]
    at_c = ids[2]
    for at in range(halves):
        left = right = None
        for piece in range(PIECES):
            one = dot_tn(normed[piece][...], grad_qkv[at, piece])
            two = dot_tn(grads[piece][...], mixed[at, piece])
            left = one if left is None else left + one
            right = two if right is None else right + two
        for core in range(2):
            block = slice(core * rows, (core + 1) * rows)
            out[at_c ^ core, at, 0, :, :width] = narrow(left[block])
            out[at_c ^ core, at, 0, :, width:] = narrow(right[block])


def attend_grads(ids, normed, grads, grad_qkv, mixed, other_y):
    rows, model = normed[0].shape
    halves, units = mixed.shape[0], 4 * mixed.shape[-1]
    strip = model // 4
    column = pl.BlockSpec((rows, strip), lambda i, ids: (0, (ids[0] ^ other_y) * 2 + i))
    return pl.pallas_call(
        attend_grads_kernel,
        grid_spec=pltpu.PrefetchScalarGridSpec(
            num_scalar_prefetch=1,
            grid=(2,),
            in_specs=[column] * 8 + [whole_spec(grad_qkv), whole_spec(mixed)],
            out_specs=pl.BlockSpec(
                (2, halves, 1, strip // 2, units), lambda i, ids: (0, 0, i ^ ids[1], 0, 0)
            ),
        ),
        out_shape=like((2, halves, 2, strip // 2, units)),
        compiler_params=pltpu.CompilerParams(vmem_limit_bytes=40 * 2**20),
        cost_estimate=pl.CostEstimate(
            flops=6 * 10**9, bytes_accessed=12 * 2**20, transcendentals=0
        ),
        name="attend_grads",
    )(ids, *normed, *grads, grad_qkv, mixed)


def gelu_both(values):
    factor = math.sqrt(2.0 / math.pi)
    square = values * values
    bent = jnp.tanh(factor * values * (1.0 + 0.044715 * square))
    slope = 0.5 * (1.0 + bent) + 0.5 * values * (1.0 - bent * bent) * factor * (
        1.0 + 3.0 * 0.044715 * square
    )
    return 0.5 * values * (1.0 + bent), slope


def feed_kernel(ids, *refs):
    rows_in, grads_in, units_in = refs[0:4], refs[4:8], refs[8]
    result_out, back_out, active_out, hidden_out = refs[9:13], refs[13:17], refs[17], refs[18]
    rows_all, grads_all, up, down, result, back, active, hidden, w_sem, in_sem, out_sem = refs[19:]
    at_x, at_c = ids[1], ids[2]
    rows, model = rows_in[0].shape
    shard_rows, width = units_in.shape[-2:]
    groups = units_in.shape[0] // 2
    copies = []
    for which, target in enumerate((up, down)):
        for other_y in range(2):
            for at_z in range(groups):
                for piece in range(PIECES):
                    block = block_of(other_y, at_x ^ (piece // 2), at_c ^ (piece % 2))
                    place_rows = pl.ds(pl.multiple_of(block * shard_rows, shard_rows), shard_rows)
                    lanes = slice((at_z % 2) * width, (at_z % 2 + 1) * width)
                    copies.append(
                        pltpu.make_async_copy(
                            units_in.at[other_y * groups + at_z, piece, which],
                            target.at[at_z // 2, place_rows, lanes],
                            w_sem.at[len(copies)],
                        )
                    )
    for piece in range(PIECES):
        copies.append(
            pltpu.make_async_copy(rows_in[piece], rows_all.at[piece], in_sem.at[2 * piece])
        )
        copies.append(
            pltpu.make_async_copy(grads_in[piece], grads_all.at[piece], in_sem.at[2 * piece + 1])
        )
    for copy in copies:
        copy.start()
    for copy in copies:
        copy.wait()
    blocks = groups // 2

    def outputs(piece, slot):
        return [
            pltpu.make_async_copy(source.at[slot], target, out_sem.at[slot, i])
            for i, (source, target) in enumerate(
                (
                    (result, result_out[piece]),
                    (back, back_out[piece]),
                    (active, active_out.at[piece]),
                    (hidden, hidden_out.at[piece]),
                )
            )
        ]

    for piece in range(PIECES):
        slot = piece % 2
        if piece >= 2:
            for copy in outputs(piece - 2, slot):
                copy.wait()

        def one_block(at, carry):
            own = rows_all[piece]
            value, slope = gelu_both(dot_nn(own, up[at]))
            value = narrow(value)
            change = narrow(dot_nn(grads_all[piece], down[at]) * slope)
            lanes = pl.ds(pl.multiple_of(at * 2 * width, 2 * width), 2 * width)
            active[slot, :, lanes] = value
            hidden[slot, :, lanes] = change
            return carry

        lax.fori_loop(0, blocks, one_block, 0)

        def one_result(at, carry):
            here = pl.ds(pl.multiple_of(at * 2 * width, 2 * width), 2 * width)
            first = second = None
            for part in range(blocks):
                lanes = slice(part * 2 * width, (part + 1) * 2 * width)
                one = dot_nt(active[slot, :, lanes], down[part, here, :])
                two = dot_nt(hidden[slot, :, lanes], up[part, here, :])
                first = one if first is None else first + one
                second = two if second is None else second + two
            result[slot, :, here] = narrow(first)
            back[slot, :, here] = narrow(second)
            return carry

        lax.fori_loop(0, model // (2 * width), one_result, 0)
        for copy in outputs(piece, slot):
            copy.start()
    for piece in (PIECES - 2, PIECES - 1):
        for copy in outputs(piece, piece % 2):
            copy.wait()


def feed(ids, rows_in, grads_in, both):
    rows, model = rows_in[0].shape
    units = both.shape[0] // 2 * both.shape[-1]
    outs = [like((rows, model))] * 8 + [like((PIECES, rows, units))] * 2
    blocks = both.shape[0] // 4
    weight = pltpu.VMEM((blocks, model, 2 * both.shape[-1]), jnp.bfloat16)
    out = pl.pallas_call(
        feed_kernel,
        in_specs=[SCALARS] + [ANYWHERE] * 9,
        out_specs=[ANYWHERE] * 10,
        out_shape=outs,
        scratch_shapes=[
            pltpu.VMEM((PIECES, rows, model), jnp.bfloat16),
            pltpu.VMEM((PIECES, rows, model), jnp.bfloat16),
            weight,
            weight,
            pltpu.VMEM((2, rows, model), jnp.bfloat16),
            pltpu.VMEM((2, rows, model), jnp.bfloat16),
            pltpu.VMEM((2, rows, units), jnp.bfloat16),
            pltpu.VMEM((2, rows, units), jnp.bfloat16),
            pltpu.SemaphoreType.DMA((2 * both.shape[0] * PIECES,)),
            pltpu.SemaphoreType.DMA((2 * PIECES,)),
            pltpu.SemaphoreType.DMA((2, 4)),
        ],
        compiler_params=pltpu.CompilerParams(vmem_limit_bytes=56 * 2**20),
        cost_estimate=pl.CostEstimate(
            flops=8 * PIECES * rows * model * units, bytes_accessed=36 * 2**20, transcendentals=0
        ),
        name="feed_forward",
    )(ids, *rows_in, *grads_in, both)
    return out[0:4], out[4:8], out[8], out[9]


def feed_grads_kernel(ids, *refs):
    left, right, out = refs[0:4], refs[4], refs[5]
    rows, width = out.shape[-2:]
    at_c = ids[2]
    for at_z in range(out.shape[1]):
        total = None
        for piece in range(PIECES):
            one = dot_tn(left[piece][...], right[piece, :, at_z * width : (at_z + 1) * width])
            total = one if total is None else total + one
        for core in range(2):
            out[0, at_z, 0, at_c ^ core] = narrow(total[core * rows : (core + 1) * rows])


def feed_grads(ids, left, right):
    rows, model = left[0].shape
    units = right.shape[-1]
    groups = lax.axis_size("z")
    strip = model // 4
    shape = (2, groups, 2, 2, strip // 2, units // groups)
    out = pl.pallas_call(
        feed_grads_kernel,
        grid_spec=pltpu.PrefetchScalarGridSpec(
            num_scalar_prefetch=1,
            grid=(4,),
            in_specs=[pl.BlockSpec((rows, strip), lambda i, ids: (0, i))] * 4 + [whole_spec(right)],
            out_specs=pl.BlockSpec(
                (1, groups, 1, 2, strip // 2, units // groups),
                lambda i, ids: (i // 2, 0, (i % 2) ^ ids[1], 0, 0, 0),
            ),
        ),
        out_shape=like(shape),
        compiler_params=pltpu.CompilerParams(vmem_limit_bytes=40 * 2**20),
        cost_estimate=pl.CostEstimate(
            flops=2 * PIECES * rows * model * units, bytes_accessed=16 * 2**20, transcendentals=0
        ),
        name="feed_grads",
    )(ids, *left, right)
    return out.reshape(2, groups, PIECES, strip // 2, units // groups)


def block_pair(values):
    low = lax.broadcasted_iota(jnp.int32, values.shape, 1) < HD
    zero = jnp.zeros_like(values)
    return jnp.concatenate([jnp.where(low, values, zero), jnp.where(low, zero, values)], axis=0)


def by_half(low, values, reduce, empty):
    first = reduce(jnp.where(low, values, empty), axis=-1, keepdims=True)
    second = reduce(jnp.where(low, empty, values), axis=-1, keepdims=True)
    return jnp.where(low, first, second)


def cross_weights(count, queries, keys):
    slots = keys.shape[0] // 2
    scores = dot_nt(queries, keys)
    lane = lax.broadcasted_iota(jnp.int32, scores.shape, 1)
    low = lane < slots
    scores = jnp.where(jnp.where(low, lane, lane - slots) < count, scores, MASKED)
    raised = jnp.exp(scores - by_half(low, scores, jnp.max, MASKED))
    return raised / by_half(low, raised, jnp.sum, 0.0), low


def cross_copies(ids, pieces, weights, sem):
    rows = pieces[0].shape[-2]
    copies = []
    for index, piece in enumerate(pieces):
        block = block_of(ids[0] ^ (index % 2), ids[1] ^ (index // 2 % 2), ids[2] ^ (index // 4))
        for distance in range(piece.shape[0]):
            at_z = (ids[3] + piece.shape[0] - distance) % piece.shape[0]
            target = weights.at[at_z, pl.ds(pl.multiple_of(block * rows, rows), rows)]
            copies.append(pltpu.make_async_copy(piece.at[distance], target, sem.at[len(copies)]))
    return copies


def lanes_of(at, size):
    return pl.ds(pl.multiple_of(at * size, size), size)


def cross_forward_kernel(ids, count, *refs):
    tokens, terms, norms, keys_values, pieces = refs[0], refs[1:4], refs[4], refs[5], refs[6:14]
    self_out, normed_out, queries, mixed, cross_out, rows_out = refs[14:20]
    weights, sem = refs[20:22]
    copies = cross_copies(ids, pieces, weights, sem)
    for copy in copies:
        copy.start()
    after_self = wide(tokens[...])
    for term in terms:
        after_self = after_self + wide(term[...])
    self_out[...] = after_self
    normed = narrow(layer_norm(after_self, norms[0:1, :], norms[1:2, :])[0])
    normed_out[...] = normed
    for copy in copies:
        copy.wait()
    width = weights.shape[2] // 2
    model = tokens.shape[1]
    for at in range(weights.shape[0]):
        out = dot_nn(normed_out[...], weights[at, :, :width])
        queries[:, at * width : (at + 1) * width] = narrow(out)

    def one_pair(at, carry):
        lanes = lanes_of(at, 2 * HD)
        query = queries[:, lanes] * jnp.bfloat16(SCALE)
        keys = block_pair(keys_values[:, lanes])
        values = block_pair(keys_values[:, lanes_of(at + model // (2 * HD), 2 * HD)])
        weight, _ = cross_weights(count[0], query, keys)
        mixed[:, lanes] = narrow(dot_nn(narrow(weight), values))
        return carry

    lax.fori_loop(0, model // (2 * HD), one_pair, 0)
    after_cross = self_out[...]
    for at in range(weights.shape[0]):
        after_cross = after_cross + dot_nt(
            mixed[:, at * width : (at + 1) * width], weights[at, :, width:]
        )
    cross_out[...] = after_cross
    rows_out[...] = narrow(layer_norm(after_cross, norms[2:3, :], norms[3:4, :])[0])


def cross_forward(ids, count, tokens, terms, norms, keys_values, pieces):
    rows, model = tokens.shape
    outs = [
        like((rows, model), jnp.float32),
        like((rows, model)),
        like((rows, model)),
        like((rows, model)),
        like((rows, model), jnp.float32),
        like((rows, model)),
    ]
    vmem = pl.BlockSpec(memory_space=pltpu.VMEM)
    size, shard_rows, width = pieces[0].shape
    return pl.pallas_call(
        cross_forward_kernel,
        in_specs=[SCALARS] * 2 + [vmem] * 6 + [ANYWHERE] * 8,
        out_specs=[vmem] * len(outs),
        out_shape=outs,
        scratch_shapes=[
            pltpu.VMEM((size, 8 * shard_rows, width), jnp.bfloat16),
            pltpu.SemaphoreType.DMA((8 * size,)),
        ],
        compiler_params=pltpu.CompilerParams(vmem_limit_bytes=48 * 2**20),
        cost_estimate=pl.CostEstimate(
            flops=12 * 10**9, bytes_accessed=24 * 2**20, transcendentals=0
        ),
        name="cross_forward",
    )(ids, count, tokens, *terms, norms, keys_values, *pieces)


def norm_gradient(upstream, values, gain_vec, bias_vec):
    _, scaled, inverse = layer_norm(values, gain_vec, bias_vec)
    weighted = upstream * gain_vec
    result = inverse * (
        weighted
        - jnp.mean(weighted, axis=-1, keepdims=True)
        - scaled * jnp.mean(weighted * scaled, axis=-1, keepdims=True)
    )
    return (
        result,
        jnp.sum(upstream * scaled, axis=0, keepdims=True),
        jnp.sum(upstream, axis=0, keepdims=True),
    )


def cross_backward_kernel(ids, count, *refs):
    upstream, terms, norms, keys_values = refs[0], refs[1:4], refs[4], refs[5]
    self_in, cross_in, queries, pieces = refs[6], refs[7], refs[8], refs[9:17]
    grad_out, first_out, second_out, dq_out, dkv_out, norm_out = refs[17:23]
    weights, grads, sem = refs[23:26]
    copies = cross_copies(ids, pieces, weights, sem)
    for copy in copies:
        copy.start()
    grad_three = wide(terms[0][...]) + wide(terms[1][...]) + wide(terms[2][...])
    back, gain_g, bias_g = norm_gradient(
        grad_three, cross_in[...], norms[2:3, :], norms[3:4, :]
    )
    norm_out[2:3, :] = gain_g
    norm_out[3:4, :] = bias_g
    grad_two = wide(upstream[...]) + back
    grad_out[...] = grad_two
    second_out[...] = narrow(grad_two)
    for copy in copies:
        copy.wait()
    width = weights.shape[2] // 2
    model = upstream.shape[1]
    slots = keys_values.shape[0]
    for at in range(weights.shape[0]):
        out = dot_nn(second_out[...], weights[at, :, width:])
        grads[:, at * width : (at + 1) * width] = narrow(out)
    dims_low = lax.broadcasted_iota(jnp.int32, (slots, 2 * HD), 1) < HD

    def one_pair(at, carry):
        lanes = lanes_of(at, 2 * HD)
        value_lanes = lanes_of(at + model // (2 * HD), 2 * HD)
        query = queries[:, lanes] * jnp.bfloat16(SCALE)
        keys = block_pair(keys_values[:, lanes])
        weight, low = cross_weights(count[0], query, keys)
        grad = grads[:, lanes]
        grad_weight = dot_nt(grad, block_pair(keys_values[:, value_lanes]))
        scores = weight * (grad_weight - by_half(low, grad_weight * weight, jnp.sum, 0.0))
        scores = narrow(scores)
        dq_out[:, lanes] = narrow(dot_nn(scores, keys) * SCALE)
        dk = dot_tn(scores, query)
        strips = width // (2 * HD)
        low_lanes = lanes_of(at % strips, 2 * HD)
        dkv_out[at // strips, :, low_lanes] = narrow(jnp.where(dims_low, dk[:slots], dk[slots:]))
        dv = dot_tn(narrow(weight), grad)
        high_lanes = lanes_of(at % strips + strips, 2 * HD)
        dkv_out[at // strips, :, high_lanes] = narrow(jnp.where(dims_low, dv[:slots], dv[slots:]))
        return carry

    lax.fori_loop(0, model // (2 * HD), one_pair, 0)
    grad_two_rows = None
    for at in range(weights.shape[0]):
        term = dot_nt(dq_out[:, at * width : (at + 1) * width], weights[at, :, :width])
        grad_two_rows = term if grad_two_rows is None else grad_two_rows + term
    back, gain_g, bias_g = norm_gradient(grad_two_rows, self_in[...], norms[0:1, :], norms[1:2, :])
    norm_out[0:1, :] = gain_g
    norm_out[1:2, :] = bias_g
    grad_one = grad_out[...] + back
    grad_out[...] = grad_one
    first_out[...] = narrow(grad_one)


def cross_backward(
    ids, count, upstream, terms, norms, keys_values, after_self, after_cross, queries, pieces
):
    rows, model = upstream.shape
    slots = keys_values.shape[0]
    outs = [
        like((rows, model), jnp.float32),
        like((rows, model)),
        like((rows, model)),
        like((rows, model)),
        like((pieces[0].shape[0], slots, 2 * model // pieces[0].shape[0])),
        like((4, model), jnp.float32),
    ]
    vmem = pl.BlockSpec(memory_space=pltpu.VMEM)
    size, shard_rows, width = pieces[0].shape
    return pl.pallas_call(
        cross_backward_kernel,
        in_specs=[SCALARS] * 2 + [vmem] * 9 + [ANYWHERE] * 8,
        out_specs=[vmem] * len(outs),
        out_shape=outs,
        scratch_shapes=[
            pltpu.VMEM((size, 8 * shard_rows, width), jnp.bfloat16),
            pltpu.VMEM((rows, model), jnp.bfloat16),
            pltpu.SemaphoreType.DMA((8 * size,)),
        ],
        compiler_params=pltpu.CompilerParams(vmem_limit_bytes=56 * 2**20),
        cost_estimate=pl.CostEstimate(
            flops=16 * 10**9, bytes_accessed=28 * 2**20, transcendentals=0
        ),
        name="cross_backward",
    )(
        ids,
        count,
        upstream,
        *terms,
        norms,
        keys_values,
        after_self,
        after_cross,
        queries,
        *pieces,
    )


def cross_grads_kernel(ids, normed, grad_queries, grads, mixed, keep, send):
    size, rows, width = keep.shape[2], keep.shape[3], keep.shape[4] // 2
    first = ids[2] == 0
    for at in range(size):
        lanes = slice(at * width, (at + 1) * width)
        distance = (ids[3] + size - at) % size
        for part, (left, right) in enumerate(((normed, grad_queries), (grads, mixed))):
            out = narrow(dot_tn(left[...], right[:, lanes]))
            there = slice(part * width, (part + 1) * width)
            keep[0, 0, distance, :, there] = jnp.where(first, out[:rows], out[rows:])
            send[0, 0, distance, :, there] = jnp.where(first, out[rows:], out[:rows])


def cross_grads(ids, normed, grad_queries, grads, mixed):
    rows, model = normed.shape
    size = lax.axis_size("z")
    strip = model // 4
    column = pl.BlockSpec((rows, strip), lambda i, ids: (0, i))
    shape = (2, 2, size, strip // 2, 2 * (model // size))
    out = pl.BlockSpec(
        (1, 1) + shape[2:], lambda i, ids: ((i % 2) ^ ids[1], (i // 2) ^ ids[0], 0, 0, 0)
    )
    return pl.pallas_call(
        cross_grads_kernel,
        grid_spec=pltpu.PrefetchScalarGridSpec(
            num_scalar_prefetch=1,
            grid=(4,),
            in_specs=[column, whole_spec(grad_queries), column, whole_spec(mixed)],
            out_specs=[out, out],
        ),
        out_shape=[like(shape), like(shape)],
        compiler_params=pltpu.CompilerParams(vmem_limit_bytes=40 * 2**20),
        cost_estimate=pl.CostEstimate(
            flops=4 * rows * model * model, bytes_accessed=14 * 2**20, transcendentals=0
        ),
        name="cross_grads",
    )(ids, normed, grad_queries, grads, mixed)


MESH = pl.DeviceIdType.MESH


def where_am_i():
    return tuple(lax.axis_index(name) for name in ("y", "x", "c", "z"))


def send_to(source, target, send_sem, recv_sem, device):
    return pltpu.make_async_remote_copy(
        src_ref=source,
        dst_ref=target,
        send_sem=send_sem,
        recv_sem=recv_sem,
        device_id=device,
        device_id_type=MESH,
    )


def groups_around(size):
    at_y, at_x, at_c, at_z = where_am_i()
    return [
        ((at_y + step // size) % 2, at_x, at_c, (at_z + step % size) % size)
        for step in range(2 * size)
    ]


def meet(size):
    at_y, at_x, at_c, at_z = where_am_i()
    others = groups_around(size)[1:]
    others += [(at_y, 1 - at_x, at_c, at_z), (at_y, at_x, 1 - at_c, at_z)]
    barrier = pltpu.get_barrier_semaphore()
    for other in others:
        pl.semaphore_signal(barrier, inc=1, device_id=other, device_id_type=MESH)
    pl.semaphore_wait(barrier, len(others))


def exchange_copies(source, target, size, send_sem, recv_sem):
    at_y, _, _, at_z = where_am_i()
    here = at_y * size + at_z
    copies = []
    for step, group in enumerate(groups_around(size)):
        there = group[0] * size + group[3]
        if step == 0:
            copies.append(pltpu.make_async_copy(source.at[there], target.at[here], recv_sem.at[0]))
        else:
            copies.append(
                send_to(
                    source.at[there], target.at[here], send_sem.at[step], recv_sem.at[step], group
                )
            )
    return copies


def block_rows(at_y, at_x, at_c, rows):
    return pl.ds(pl.multiple_of(((at_y * 2 + at_x) * 2 + at_c) * rows, rows), rows)


def start_kernel(
    size,
    tokens,
    split,
    norm,
    cross,
    clip_out,
    rows_own,
    rows_c,
    rows_x,
    rows_xc,
    weights,
    cross_near_out,
    cross_x_out,
    cross_near,
    cross_x,
    held,
    clip,
    normed,
    clip_send,
    clip_recv,
    x_sem,
    ring_send,
    ring_recv,
    y_send,
    y_recv,
    c_send,
    c_recv,
    c_local,
    row_sem,
    out_sem,
    cross_ring_sem,
    cross_x_sem,
):
    at_y, at_x, at_c, at_z = where_am_i()
    rows = split.shape[1]
    half = size // 2
    x_side = (at_y, 1 - at_x, at_c, at_z)
    y_side = (1 - at_y, at_x, at_c, at_z)
    c_side = (at_y, at_x, 1 - at_c, at_z)
    z_next = (at_y, at_x, at_c, (at_z + 1) % size)
    meet(size)
    frames = exchange_copies(tokens, clip, size, clip_send, clip_recv)
    for copy in frames:
        copy.start()
    first = pltpu.make_async_copy(split.at[at_x], held.at[0, 0, 0], out_sem.at[0])
    first.start()
    over = send_to(split.at[1 - at_x], held.at[0, 0, 1], x_sem.at[0], x_sem.at[1], x_side)
    over.start()

    def ring(step, side):
        return send_to(
            held.at[step, 0, side],
            held.at[step + 1, 0, side],
            ring_send.at[step, side],
            ring_recv.at[step, side],
            z_next,
        )

    def across(step, side):
        return send_to(
            held.at[step, 0, side],
            held.at[step, 1, side],
            y_send.at[step, side],
            y_recv.at[step, side],
            y_side,
        )

    def cross_send(step):
        source = cross_near.at[step]
        copies = [
            send_to(
                source, cross_x.at[step], cross_x_sem.at[0, step], cross_x_sem.at[1, step], x_side
            )
        ]
        if step < size - 1:
            copies.append(
                send_to(
                    source,
                    cross_near.at[step + 1],
                    cross_ring_sem.at[0, step],
                    cross_ring_sem.at[1, step],
                    z_next,
                )
            )
        return copies

    def settle(step, other_y, side):
        target = weights.at[
            step % half, block_rows((at_y + other_y) % 2, (at_x + side) % 2, at_c, rows)
        ]
        source = held.at[step, other_y, side]
        slot = (step % half, other_y, side)
        local = pltpu.make_async_copy(source, target, c_local.at[slot])
        remote = send_to(source, target, c_send.at[slot], c_recv.at[slot], c_side)
        return local, remote

    def settle_start(step, other_y, side):
        local, remote = settle(step, other_y, side)

        @pl.when(at_c == step // half)
        def _():
            local.start()

        @pl.when(at_c != step // half)
        def _():
            remote.start()

    cross_own = pltpu.make_async_copy(cross, cross_near.at[0], out_sem.at[3])
    cross_own.start()
    for side in range(2):
        if side == 0:
            first.wait()
        else:
            over.wait_recv()
        ring(0, side).start()
        across(0, side).start()
        settle_start(0, 0, side)
    cross_own.wait()

    def ring_step(step):
        for side in range(2):
            ring(step - 1, side).wait_recv()
            if step < size - 1:
                ring(step, side).start()
            across(step, side).start()
            settle_start(step, 0, side)

    def cross_step(step):
        if step:
            cross_send(step - 1)[1].wait_recv()
        for copy in cross_send(step):
            copy.start()

    ring_step(1)
    for copy in frames:
        if copy is frames[0]:
            copy.wait()
        else:
            copy.wait_recv()
    keep = pltpu.make_async_copy(clip, clip_out, out_sem.at[1])
    keep.start()
    gain, bias = norm[0:1, :], norm[1:2, :]

    def one_block(at, carry):
        here = pl.ds(pl.multiple_of(at * clip.shape[1], clip.shape[1]), clip.shape[1])
        normed[here, :] = narrow(layer_norm(wide(clip[at]), gain, bias)[0])
        return carry

    lax.fori_loop(0, clip.shape[0], one_block, 0)
    own = pltpu.make_async_copy(normed, rows_own, out_sem.at[2])
    to_x = send_to(normed, rows_x, row_sem.at[0], row_sem.at[1], x_side)
    to_c = send_to(normed, rows_c, row_sem.at[2], row_sem.at[3], c_side)
    to_x.start()
    to_c.start()
    own.start()
    ring_step(2)
    ring_step(3)
    cross_step(0)
    for step in range(size):
        for side in range(2):
            across(step, side).wait_recv()
            settle_start(step, 1, side)
        if step:
            cross_step(step)
    to_x.wait_recv()
    relay = send_to(rows_x, rows_xc, row_sem.at[4], row_sem.at[5], c_side)
    relay.start()
    for step in range(size):
        copies = cross_send(step)
        copies[0].wait()
        if step < size - 1:
            copies[1].wait_send()
    cross_outs = [
        pltpu.make_async_copy(cross_near, cross_near_out, out_sem.at[3]),
        pltpu.make_async_copy(cross_x, cross_x_out, out_sem.at[4]),
    ]
    for copy in cross_outs:
        copy.start()
    for copy in cross_outs:
        copy.wait()
    for step in range(half):
        for other_y in range(2):
            for side in range(2):
                local, remote = settle(step, other_y, side)
                local.wait()
                remote.wait()
    relay.wait()
    to_c.wait()
    to_x.wait_send()
    own.wait()
    keep.wait()
    over.wait_send()
    for copy in frames[1:]:
        copy.wait_send()
    for step in range(size):
        for side in range(2):
            across(step, side).wait_send()
            if step < size - 1:
                ring(step, side).wait_send()


def start_up(tokens, split, norm, cross):
    size = lax.axis_size("z")
    groups, frames, model = tokens.shape
    rows, units = split.shape[1:]
    half = size // 2
    vmem = pl.BlockSpec(memory_space=pltpu.VMEM)
    dma = pltpu.SemaphoreType.DMA
    out = pl.pallas_call(
        functools.partial(start_kernel, size),
        in_specs=[vmem] * 4,
        out_specs=[ANYWHERE] * 8,
        out_shape=[like(tokens.shape)]
        + [like((groups * frames, model))] * PIECES
        + [like((half, 8 * rows, units))]
        + [like((size,) + cross.shape)] * 2,
        scratch_shapes=[
            pltpu.VMEM((size,) + cross.shape, jnp.bfloat16),
            pltpu.VMEM((size,) + cross.shape, jnp.bfloat16),
            pltpu.VMEM((size, 2, 2, rows, units), jnp.bfloat16),
            pltpu.VMEM(tokens.shape, jnp.bfloat16),
            pltpu.VMEM((groups * frames, model), jnp.bfloat16),
            dma((groups,)),
            dma((groups,)),
            dma((2,)),
            dma((size - 1, 2)),
            dma((size - 1, 2)),
            dma((size, 2)),
            dma((size, 2)),
            dma((half, 2, 2)),
            dma((half, 2, 2)),
            dma((half, 2, 2)),
            dma((6,)),
            dma((5,)),
            dma((2, size - 1)),
            dma((2, size)),
        ],
        compiler_params=pltpu.CompilerParams(
            collective_id=1, has_side_effects=True, vmem_limit_bytes=32 * 2**20
        ),
        cost_estimate=pl.CostEstimate(
            flops=10**7, bytes_accessed=200 * 2**20, transcendentals=0
        ),
        name="start_up",
    )(tokens, split, norm, cross)
    return out[0].reshape(-1, model), out[1:5], out[5], out[6:8]


def middle_kernel(
    size,
    part_own,
    part_c,
    part_x,
    part_xc,
    near,
    side,
    text,
    cot,
    term_c,
    term_x,
    near_y,
    side_y,
    near_c,
    side_c,
    near_yc,
    side_yc,
    text_out,
    cot_c,
    cot_x,
    cot_xc,
    text_parts,
    far_held,
    far_sum,
    text_held,
    text_sum,
    core_sem,
    x_sem,
    y_sem,
    c_sem,
    text_sem,
    out_sem,
    text_send,
    text_recv,
    cot_sem,
):
    at_y, at_x, at_c, at_z = where_am_i()
    x_side = (at_y, 1 - at_x, at_c, at_z)
    y_side = (1 - at_y, at_x, at_c, at_z)
    c_side = (at_y, at_x, 1 - at_c, at_z)
    meet(size)
    exchange = exchange_copies(text, text_parts, size, text_send, text_recv)

    def swap(source, target, sem, at, device):
        return send_to(source, target, sem.at[0, at], sem.at[1, at], device)

    core_far = swap(part_xc, far_held, core_sem, 0, c_side)
    core_near = swap(part_c, term_c, core_sem, 1, c_side)
    y_near = swap(near, near_y, y_sem, 0, y_side)
    y_side_copy = swap(side, side_y, y_sem, 1, y_side)
    text_c = swap(text_sum.at[0], text_held.at[0], text_sem, 0, c_side)
    text_x = swap(text_sum.at[1], text_held.at[1], text_sem, 1, x_side)
    cots = [
        swap(cot, cot_c, cot_sem, 0, c_side),
        swap(cot, cot_x, cot_sem, 1, x_side),
        swap(cot_x, cot_xc, cot_sem, 2, c_side),
    ]
    core_far.start()
    for copy in exchange:
        copy.start()
    y_near.start()
    core_far.wait_recv()
    rows = 48

    def add_far(at, carry):
        here = pl.ds(pl.multiple_of(at * rows, rows), rows)
        far_sum[here, :] = narrow(wide(part_x[here, :]) + wide(far_held[here, :]))
        return carry

    lax.fori_loop(0, part_x.shape[0] // rows, add_far, 0)
    over = swap(far_sum, term_x, x_sem, 0, x_side)
    over.start()
    core_near.start()
    y_side_copy.start()
    pieces_c = [swap(near, near_c, c_sem, 0, c_side), swap(side, side_c, c_sem, 1, c_side)]
    for copy in pieces_c:
        copy.start()
    cots[0].start()
    for copy in exchange:
        if copy is exchange[0]:
            copy.wait()
        else:
            copy.wait_recv()
    text_sum[0] = narrow(wide(text_parts[:size]) + wide(text_parts[size:]))
    text_c.start()
    text_c.wait_recv()
    text_sum[1] = narrow(wide(text_sum[0]) + wide(text_held[0]))
    text_x.start()
    over.wait_recv()
    cots[1].start()
    y_near.wait_recv()
    more = [swap(near_y, near_yc, c_sem, 2, c_side)]
    more[0].start()
    text_x.wait_recv()
    text_sum[2] = narrow(wide(text_sum[1]) + wide(text_held[1]))
    last = pltpu.make_async_copy(text_sum.at[2], text_out, out_sem.at[0])
    last.start()
    y_side_copy.wait_recv()
    more.append(swap(side_y, side_yc, c_sem, 3, c_side))
    more[1].start()
    cots[1].wait_recv()
    cots[2].start()
    last.wait()
    for copy in pieces_c + more:
        copy.wait()
    core_near.wait()
    over.wait_send()
    cots[0].wait()
    cots[1].wait_send()
    cots[2].wait()
    for copy in exchange[1:]:
        copy.wait_send()
    for copy in (core_far, y_near, y_side_copy, text_c, text_x):
        copy.wait_send()


def middle(parts, near, side, text, cot):
    size = lax.axis_size("z")
    vmem = pl.BlockSpec(memory_space=pltpu.VMEM)
    dma = pltpu.SemaphoreType.DMA
    rows = like(parts[0].shape)
    piece = like(near.shape)
    out = pl.pallas_call(
        functools.partial(middle_kernel, size),
        in_specs=[vmem] * 8,
        out_specs=[ANYWHERE] * 12,
        out_shape=[rows, rows] + [piece] * 6 + [like((size,) + text.shape[1:])] + [rows] * 3,
        scratch_shapes=[
            pltpu.VMEM(text.shape, jnp.bfloat16),
            pltpu.VMEM(rows.shape, jnp.bfloat16),
            pltpu.VMEM(rows.shape, jnp.bfloat16),
            pltpu.VMEM((2, size) + text.shape[1:], jnp.bfloat16),
            pltpu.VMEM((3, size) + text.shape[1:], jnp.bfloat16),
            dma((2, 2)),
            dma((2, 1)),
            dma((2, 2)),
            dma((2, 4)),
            dma((2, 2)),
            dma((1,)),
            dma((2 * size,)),
            dma((2 * size,)),
            dma((2, 3)),
        ],
        compiler_params=pltpu.CompilerParams(
            collective_id=3, has_side_effects=True, vmem_limit_bytes=40 * 2**20
        ),
        cost_estimate=pl.CostEstimate(
            flops=10**7, bytes_accessed=100 * 2**20, transcendentals=0
        ),
        name="middle",
    )(*parts, near, side, text, cot)
    near_y, side_y, near_c, side_c, near_yc, side_yc = out[2:8]
    pieces = [near, near_y, side, side_y, near_c, near_yc, side_c, side_yc]
    return [parts[0], out[0], out[1]], pieces, out[8], [cot] + list(out[9:])


def end_kernel(
    size,
    far,
    near,
    part_own,
    part_c,
    part_x,
    part_xc,
    upstream,
    clip,
    norm,
    norm_in,
    cross,
    text,
    text_rows,
    text_weights,
    grad_out,
    norm_out,
    unit_own,
    unit_x,
    cross_out,
    text_out,
    memory_out,
    y_held,
    folded,
    both,
    moved,
    ring_held,
    unit_held,
    core_held,
    x_moved,
    x_held,
    grads,
    grads_held,
    sums,
    sums_held,
    y_send,
    y_recv,
    c_send,
    c_recv,
    core_sem,
    x_sem,
    ring_send,
    ring_recv,
    clip_send,
    clip_recv,
    hop_send,
    hop_recv,
    unit_sem,
    out_sem,
    cross_held,
    cross_moved,
    cross_final,
    cross_sem,
    text_held,
    text_sum,
    text_sem,
    text_final,
    memory_part,
    memory_held,
    memory_all,
    memory_sem,
    all_send,
    all_recv,
):
    at_y, at_x, at_c, at_z = where_am_i()
    x_side = (at_y, 1 - at_x, at_c, at_z)
    y_side = (1 - at_y, at_x, at_c, at_z)
    c_side = (at_y, at_x, 1 - at_c, at_z)
    z_next = (at_y, at_x, at_c, (at_z + 1) % size)
    half = size // 2
    meet(size)

    def across(core, at, side):
        return send_to(
            far.at[core, at, side],
            y_held.at[core, at, side],
            y_send.at[core, at, side],
            y_recv.at[core, at, side],
            y_side,
        )

    places = [(at, side) for at in range(half) for side in range(2)]
    core_far = send_to(part_xc, core_held.at[1], core_sem.at[0], core_sem.at[1], c_side)
    core_near = send_to(part_c, core_held.at[0], core_sem.at[2], core_sem.at[3], c_side)
    z_sides = []
    for bit in (1, 2):
        low = at_z % 2
        other = (at_z + 1 - 2 * low) if bit == 1 else (at_z + 2) % size
        z_sides.append((at_y, at_x, at_c, other))

    def cross_ring(step):
        return send_to(
            cross.at[1] if step == 0 else cross_moved.at[step - 1],
            cross_held.at[step],
            cross_sem.at[0, step],
            cross_sem.at[1, step],
            z_next,
        )

    def cross_next(step):
        cross_ring(step - 1).wait_recv()
        total = wide(cross_held[step - 1]) + wide(cross[(step + 1) % size])
        if step < size - 1:
            cross_moved[step - 1] = narrow(total)
            cross_ring(step).start()
        else:
            cross_final[...] = total

    text_c = send_to(text, text_held.at[0], text_sem.at[0], text_sem.at[1], c_side)
    text_x = send_to(text_sum.at[0], text_held.at[1], text_sem.at[2], text_sem.at[3], x_side)

    def memory_hop(number):
        return send_to(
            memory_part.at[number],
            memory_held.at[number],
            memory_sem.at[0, number],
            memory_sem.at[1, number],
            z_sides[number],
        )

    def block_at(near_y, near_x, near_c):
        return (((at_y + near_y) % 2) * 2 + (at_x + near_x) % 2) * 2 + (at_c + near_c) % 2

    def memory_copies(stage):
        if stage == 0:
            blocks, device = [block_at(0, 0, 0)], y_side
        elif stage == 1:
            blocks, device = [block_at(i, 0, 0) for i in range(2)], x_side
        else:
            blocks, device = [block_at(i // 2, i % 2, 0) for i in range(4)], c_side
        return [
            send_to(
                memory_all.at[block],
                memory_all.at[block],
                all_send.at[stage, i],
                all_recv.at[stage, i],
                device,
            )
            for i, block in enumerate(blocks)
        ]

    def text_step(step):
        if step == 0:
            text_c.wait_recv()
            text_sum[0] = narrow(wide(text[...]) + wide(text_held[0]))
            text_x.start()
        elif step == 2:
            text_x.wait_recv()
            text_sum[1] = narrow(wide(text_sum[0]) + wide(text_held[1]))
            whole = text_sum[1].reshape(-1, text.shape[2])
            text_final[...] = dot_tn(text_rows[...], whole)
            memory_part[0] = narrow(dot_nt(text_weights[...], whole))
            memory_hop(0).start()
        elif step == 3:
            memory_hop(0).wait_recv()
            memory_part[1] = narrow(wide(memory_part[0]) + wide(memory_held[0]))
            memory_hop(1).start()
        elif step == 4:
            memory_hop(1).wait_recv()
            memory_all[block_at(0, 0, 0)] = narrow(wide(memory_part[1]) + wide(memory_held[1]))
            memory_copies(0)[0].start()
        elif step < 7:
            for copy in memory_copies(step - 5):
                copy.wait_recv()
            for copy in memory_copies(step - 4):
                copy.start()
        else:
            for copy in memory_copies(2):
                copy.wait_recv()

    def to_core(at, side):
        return send_to(
            folded.at[at, side],
            both.at[1, at, side],
            c_send.at[at, side],
            c_recv.at[at, side],
            c_side,
        )

    def fold(at, side):
        across(1, at, side).wait_recv()
        folded[at, side] = narrow(wide(near[1, at, side]) + wide(y_held[1, at, side]))
        to_core(at, side).start()
        across(0, at, side).wait_recv()
        both[0, at, side] = narrow(wide(near[0, at, side]) + wide(y_held[0, at, side]))
        to_core(at, side).wait_recv()

    def chunk(step):
        return ((step // half) + at_c) % 2, step % half

    def ring(step, side):
        source = both.at[chunk(1) + (side,)] if step == 0 else moved.at[step - 1, side]
        return send_to(
            source,
            ring_held.at[step, side],
            ring_send.at[step, side],
            ring_recv.at[step, side],
            z_next,
        )

    def ring_next(step, side):
        which, at = chunk((step + 1) % size)
        ring(step - 1, side).wait_recv()
        moved[step - 1, side] = narrow(
            wide(ring_held[step - 1, side]) + wide(both[which, at, side])
        )
        if step < size - 1:
            ring(step, side).start()

    core_far.start()
    def across_start(side):
        for at in range(half - 1, -1, -1):
            for core in (1, 0):
                across(core, at, side).start()

    across_start(1)
    across_start(0)
    cross_ring(0).start()
    core_near.start()
    frames = clip.shape[1]

    def rows_of(at):
        return pl.ds(pl.multiple_of(at * frames, frames), frames)

    core_far.wait_recv()

    def add_far(at, carry):
        here = rows_of(at)
        x_moved[here, :] = narrow(wide(part_x[here, :]) + wide(core_held[1, here, :]))
        return carry

    lax.fori_loop(0, clip.shape[0], add_far, 0)
    over = send_to(x_moved, x_held, x_sem.at[0], x_sem.at[1], x_side)
    over.start()
    text_c.start()
    fold(1, 1)
    ring(0, 1).start()
    cross_next(1)
    fold(0, 1)
    ring_next(1, 1)
    cross_next(2)
    text_step(0)
    fold(1, 0)
    ring(0, 0).start()
    ring_next(2, 1)
    cross_next(3)
    core_near.wait_recv()
    over.wait_recv()
    sums[...] = jnp.zeros_like(sums)
    sums[2:6, :] = norm_in[...]
    gain, bias = norm[0:1, :], norm[1:2, :]

    def one_block(at, carry):
        here = rows_of(at)
        change = wide(part_own[here, :]) + wide(core_held[0, here, :]) + wide(x_held[here, :])
        back, gain_g, bias_g = norm_gradient(change, wide(clip[at]), gain, bias)
        grads[at] = narrow(upstream[here, :] + back)
        sums[0:1, :] += gain_g
        sums[1:2, :] += bias_g
        return carry

    lax.fori_loop(0, clip.shape[0], one_block, 0)
    exchange = exchange_copies(grads, grads_held, size, clip_send, clip_recv)
    for copy in exchange:
        copy.start()
    hops = [c_side, x_side, y_side] + z_sides

    def hop(number):
        source = sums if number == 0 else sums_held.at[1, number - 1]
        return send_to(
            source, sums_held.at[0, number], hop_send.at[number], hop_recv.at[number], hops[number]
        )

    def hop_next(number):
        hop(number).wait_recv()
        source = sums[...] if number == 0 else sums_held[1, number - 1]
        sums_held[1, number] = source + sums_held[0, number]
        if number + 1 < len(hops):
            hop(number + 1).start()

    hop(0).start()
    ring_next(3, 1)
    last = send_to(moved.at[size - 2, 1], unit_held, unit_sem.at[0], unit_sem.at[1], x_side)
    last.start()
    text_step(2)
    fold(0, 0)
    text_step(3)
    ring_next(1, 0)
    text_step(4)
    hop_next(0)
    hop_next(1)
    text_step(5)
    ring_next(2, 0)
    hop_next(2)
    text_step(6)
    ring_next(3, 0)
    hop_next(3)
    text_step(7)
    hop_next(4)
    for copy in exchange:
        if copy is exchange[0]:
            copy.wait()
        else:
            copy.wait_recv()
    outs = [
        pltpu.make_async_copy(grads_held, grad_out, out_sem.at[0]),
        pltpu.make_async_copy(moved.at[size - 2, 0], unit_own, out_sem.at[1]),
        pltpu.make_async_copy(sums_held.at[1, len(hops) - 1], norm_out, out_sem.at[2]),
        pltpu.make_async_copy(cross_final, cross_out, out_sem.at[4]),
        pltpu.make_async_copy(text_final, text_out, out_sem.at[5]),
        pltpu.make_async_copy(memory_all, memory_out, out_sem.at[6]),
    ]
    for copy in outs:
        copy.start()
    last.wait_recv()
    final = pltpu.make_async_copy(unit_held, unit_x, out_sem.at[3])
    final.start()
    for copy in outs:
        copy.wait()
    final.wait()
    last.wait_send()
    core_far.wait_send()
    core_near.wait_send()
    over.wait_send()
    for at, side in places:
        across(0, at, side).wait_send()
        across(1, at, side).wait_send()
        to_core(at, side).wait_send()
    for step in range(size - 1):
        for side in range(2):
            ring(step, side).wait_send()
    for copy in exchange[1:]:
        copy.wait_send()
    for number in range(len(hops)):
        hop(number).wait_send()
    for step in range(size - 1):
        cross_ring(step).wait_send()
    text_c.wait_send()
    text_x.wait_send()
    for number in range(2):
        memory_hop(number).wait_send()
    for stage in range(3):
        for copy in memory_copies(stage):
            copy.wait_send()


def end(far, near, parts, upstream, clip, norm, norm_in, cross, text, text_rows, text_weights):
    size = lax.axis_size("z")
    half = size // 2
    groups, frames, model = clip.shape
    rows, units = far.shape[-2:]
    vmem = pl.BlockSpec(memory_space=pltpu.VMEM)
    dma = pltpu.SemaphoreType.DMA

    def buffer(*shape, dtype=jnp.bfloat16):
        return pltpu.VMEM(shape, dtype)

    return pl.pallas_call(
        functools.partial(end_kernel, size),
        in_specs=[vmem] * 14,
        out_specs=[ANYWHERE] * 7,
        out_shape=[
            like(clip.shape),
            like((8, model), jnp.float32),
            like((rows, units)),
            like((rows, units)),
            like(cross.shape[1:], jnp.float32),
            like((text_rows.shape[1], text.shape[2]), jnp.float32),
            like((8, text_weights.shape[0], text_rows.shape[0])),
        ],
        scratch_shapes=[
            buffer(2, half, 2, rows, units),
            buffer(half, 2, rows, units),
            buffer(2, half, 2, rows, units),
            buffer(size - 1, 2, rows, units),
            buffer(size - 1, 2, rows, units),
            buffer(rows, units),
            buffer(2, groups * frames, model),
            buffer(groups * frames, model),
            buffer(groups * frames, model),
            buffer(groups, frames, model),
            buffer(groups, frames, model),
            buffer(8, model, dtype=jnp.float32),
            buffer(2, 5, 8, model, dtype=jnp.float32),
            dma((2, half, 2)),
            dma((2, half, 2)),
            dma((half, 2)),
            dma((half, 2)),
            dma((4,)),
            dma((2,)),
            dma((size - 1, 2)),
            dma((size - 1, 2)),
            dma((groups,)),
            dma((groups,)),
            dma((5,)),
            dma((5,)),
            dma((2,)),
            dma((7,)),
            buffer(size - 1, *cross.shape[1:]),
            buffer(size - 2, *cross.shape[1:]),
            buffer(*cross.shape[1:], dtype=jnp.float32),
            dma((2, size - 1)),
            buffer(2, *text.shape),
            buffer(2, *text.shape),
            dma((4,)),
            buffer(text_rows.shape[1], text.shape[2], dtype=jnp.float32),
            buffer(2, text_weights.shape[0], text_rows.shape[0]),
            buffer(2, text_weights.shape[0], text_rows.shape[0]),
            buffer(8, text_weights.shape[0], text_rows.shape[0]),
            dma((2, 2)),
            dma((3, 4)),
            dma((3, 4)),
        ],
        compiler_params=pltpu.CompilerParams(
            collective_id=2, has_side_effects=True, vmem_limit_bytes=56 * 2**20
        ),
        cost_estimate=pl.CostEstimate(
            flops=10**7, bytes_accessed=300 * 2**20, transcendentals=0
        ),
        name="end",
    )(
        far,
        near,
        *parts,
        upstream,
        clip,
        norm,
        norm_in,
        cross,
        text,
        text_rows,
        text_weights,
    )


def clip_body(
    tokens,
    memory,
    text_len,
    cotangent,
    gain_one,
    bias_one,
    gain_two,
    bias_two,
    gain_three,
    bias_three,
    w_query,
    w_key,
    w_value,
    w_out,
    c_query,
    c_key,
    c_value,
    c_out,
    w_up,
    w_down,
):
    at_y, at_x, at_c, at_z = (lax.axis_index(name) for name in ("y", "x", "c", "z"))
    ids = jnp.stack([at_y, at_x, at_c, at_z]).astype(jnp.int32)
    model = tokens.shape[-1]
    shard_rows, shard_width = w_query.shape
    slots = memory.shape[2]
    size = lax.axis_size("z")
    frame_block = tokens.shape[2]

    both = gather_units([w_up, w_down.T])
    split = split_heads([w_query, w_key, w_value, w_out.T])
    norm_one = jnp.stack([gain_one, bias_one])
    at_f = block_of(at_y, at_x, at_c)
    text_mine = lax.dynamic_slice_in_dim(
        memory.reshape(-1, model), at_f * shard_rows, shard_rows, 1
    )
    text_shard = jnp.concatenate([c_key, c_value], axis=1)
    text_part = narrow(dot_nn(text_mine, text_shard)).reshape(-1, slots, 2 * shard_width)
    clip_tokens, rows_one, attend_weights, cross_pieces = start_up(
        tokens.reshape(-1, frame_block, model),
        split,
        norm_one,
        jnp.concatenate([c_query, c_out.T], axis=1),
    )
    near, side = cross_pieces
    upstream = after(cotangent.reshape(-1, frame_block, model), clip_tokens)
    upstream = exchange_clips(upstream).reshape(-1, model)
    count = take(take(text_len, at_y), at_z).reshape(1)
    norms = jnp.stack([gain_two, bias_two, gain_three, bias_three])

    self_parts, qkv, mixed_one, log_total = attend_forward(ids, rows_one, attend_weights)
    self_terms, cross_pieces, text_clip, grad_rows3 = middle(
        self_parts, near, side, text_part, upstream
    )
    text_clip = text_clip.reshape(size, slots, 2, shard_width)
    keys_values = jnp.transpose(text_clip, (1, 2, 0, 3)).reshape(slots, -1)
    after_self, rows_two, cross_q, mixed_two, after_cross, own_three = cross_forward(
        ids, count, clip_tokens, self_terms, norms, keys_values, cross_pieces
    )
    rows_three = group_rows(own_three)

    feed_parts, back_parts, active, grad_hidden = feed(
        ids, rows_three, grad_rows3, both
    )
    back_terms = group_terms(back_parts)
    part_down = feed_grads(ids, grad_rows3, active)
    part_up = feed_grads(ids, rows_three, grad_hidden)
    sum_down, sum_up = scatter_units(part_down), scatter_units(part_up)
    grad_one_rows, own_one, own_two, grad_cq, grad_text, norm_grads = cross_backward(
        ids,
        count,
        upstream,
        back_terms,
        norms,
        keys_values,
        after_self,
        after_cross,
        cross_q,
        cross_pieces,
    )
    grad_rows1 = group_rows(own_one)
    cross_keep, cross_send = cross_grads(ids, rows_two, grad_cq, own_two, mixed_two)
    cross_sum = sum_plane(cross_keep, cross_send, grad_rows1)
    grad_text = exchange_clips(jnp.concatenate([grad_text, grad_text]))

    feed_terms = group_terms(after(feed_parts, grad_rows1))
    self_back, grad_qkv = attend_backward(
        after(ids, cross_keep, part_up, part_down),
        grad_rows1,
        attend_weights,
        qkv,
        mixed_one,
        log_total,
    )
    feed_terms = after(feed_terms, self_back)
    result = after_cross + wide(feed_terms[0]) + wide(feed_terms[1]) + wide(feed_terms[2])
    result = narrow(result)
    result = after(result.reshape(-1, frame_block, model), grad_text)
    result = exchange_clips(result).reshape(tokens.shape)

    cross_part = sum_plane_rest(*after(cross_sum, self_back))
    far = attend_grads(ids, rows_one, grad_rows1, grad_qkv, mixed_one, 1)
    near = attend_grads(ids, rows_one, grad_rows1, grad_qkv, mixed_one, 0)
    input_grad, norm_grads, unit_own, unit_away, fin_cross, fin_text, grad_memory = end(
        after(far, result),
        near,
        self_back,
        grad_one_rows,
        clip_tokens.reshape(-1, frame_block, model),
        norm_one,
        norm_grads,
        cross_part,
        grad_text,
        text_mine,
        text_shard,
    )
    fin_down = join_units(after(sum_down, input_grad)).T
    fin_up = join_units(after(sum_up, input_grad))
    fin_cquery, fin_cout = fin_cross[:, :shard_width], fin_cross[:, shard_width:].T
    fin_ckey, fin_cvalue = fin_text[:, :shard_width], fin_text[:, shard_width:]
    grad_memory = wide(grad_memory.reshape(model, -1).T).reshape(memory.shape)
    input_grad = wide(input_grad).reshape(tokens.shape)
    fin_query, fin_key, fin_value, fin_out = join_heads(unit_own, unit_away)

    return (
        result,
        input_grad,
        grad_memory,
        norm_grads[0],
        norm_grads[1],
        norm_grads[2],
        norm_grads[3],
        norm_grads[4],
        norm_grads[5],
        fin_query,
        fin_key,
        fin_value,
        fin_out.T,
        fin_cquery,
        fin_ckey,
        fin_cvalue,
        fin_cout,
        fin_up,
        fin_down,
    )


def clip_groups(mesh):
    outer, inner = mesh.shape["fsdp"], mesh.shape["tp"]
    return (2, 2, 2, inner) if outer == 8 and inner == 4 else None


def solution(mesh):
    sizes = clip_groups(mesh)
    if sizes is None:
        rows, columns, program, used = "fsdp", "tp", body, mesh
    else:
        rows, columns, program = ("y", "x", "c"), "z", clip_body
        used = jax.sharding.Mesh(mesh.devices.reshape(sizes), ("y", "x", "c", "z"))
    both = ("fsdp", "tp") if sizes is None else ("y", "x", "c", "z")
    frames = P(None, None, both, None)
    tall, wide = P(rows, columns), P(columns, rows)
    weights = (tall, tall, tall, wide, tall, tall, tall, wide, tall, wide)
    return jax.shard_map(
        program,
        mesh=used,
        in_specs=(frames, P(), P(), frames) + (P(),) * 6 + weights,
        out_specs=(frames, frames, P()) + (P(),) * 6 + weights,
        check_vma=False,
    )
```

```python
import functools
import math

import jax
import jax.numpy as jnp
from jax import lax
from jax.experimental import pallas as pl
from jax.experimental.pallas import tpu as pltpu
from jax.sharding import PartitionSpec as P

HD = 64
MICRO = 2


EPSILON = 1e-05
PRECISE = lax.Precision.HIGHEST
MASKED = -1e30


def layer_norm(values, gain_vec, bias_vec):
    center = values - jnp.mean(values, axis=-1, keepdims=True)
    inverse = lax.rsqrt(jnp.mean(center * center, axis=-1, keepdims=True) + EPSILON)
    scaled = center * inverse
    return (scaled * gain_vec + bias_vec, scaled, inverse)


def norm_back(upstream, scaled, inverse, gain_vec):
    weighted = upstream * gain_vec
    result = inverse * (
        weighted
        - jnp.mean(weighted, axis=-1, keepdims=True)
        - scaled * jnp.mean(weighted * scaled, axis=-1, keepdims=True)
    )
    return (result, jnp.sum(upstream * scaled, axis=(0, 1)), jnp.sum(upstream, axis=(0, 1)))


def spread_rows(values):
    return lax.all_gather(values, "tp", axis=1, tiled=True)


def spread_grads(values):
    return lax.all_gather(values, "tp", axis=1, tiled=True)


def fold_rows(values):
    return lax.psum_scatter(values, "tp", scatter_dimension=1, tiled=True)


def fold_grads(values):
    return lax.psum_scatter(values, "tp", scatter_dimension=1, tiled=True)


def project(left_side, right_side):
    return jnp.einsum("cfd,de->cfe", left_side, right_side, preferred_element_type=jnp.float32)


def project_back(left_side, right_side):
    return jnp.einsum("cfe,de->cfd", left_side, right_side, preferred_element_type=jnp.float32)


def weight_grad(left_side, right_side):
    return jnp.einsum("cfd,cfe->de", left_side, right_side, preferred_element_type=jnp.float32)


def masked_scores(queries, key_rows, allowed):
    factor = 1.0 / math.sqrt(queries.shape[-1])
    scores = (
        jnp.einsum("cqhe,ckhe->chqk", queries, key_rows, preferred_element_type=jnp.float32)
        * factor
    )
    return jnp.where(allowed, scores, MASKED)


def attention_forward(queries, key_rows, value_rows, allowed):
    scores = masked_scores(queries, key_rows, allowed)
    highest = jnp.max(scores, axis=-1, keepdims=True)
    log_total = highest + jnp.log(jnp.sum(jnp.exp(scores - highest), axis=-1, keepdims=True))
    weights = jnp.exp(scores - log_total).astype(jnp.bfloat16)
    mixed = jnp.einsum("chqk,ckhe->cqhe", weights, value_rows, preferred_element_type=jnp.float32)
    return (mixed, log_total)


def score_grads(queries, key_rows, value_rows, allowed, log_total, grad_mixed):
    weights = jnp.exp(masked_scores(queries, key_rows, allowed) - log_total)
    grad_weights = jnp.einsum(
        "cqhe,ckhe->chqk", grad_mixed, value_rows, preferred_element_type=jnp.float32
    )
    row_total = jnp.sum(grad_weights * weights, axis=-1, keepdims=True)
    grad_scores = (weights * (grad_weights - row_total)).astype(jnp.bfloat16)
    return (weights, grad_scores, row_total)


def attention_backward(queries, key_rows, value_rows, allowed, log_total, grad_mixed):
    factor = 1.0 / math.sqrt(queries.shape[-1])
    weights, grad_scores, row_total = score_grads(
        queries, key_rows, value_rows, allowed, log_total, grad_mixed
    )
    grad_queries = (
        jnp.einsum("chqk,ckhe->cqhe", grad_scores, key_rows, preferred_element_type=jnp.float32)
        * factor
    )
    grad_keys = (
        jnp.einsum("chqk,cqhe->ckhe", grad_scores, queries, preferred_element_type=jnp.float32)
        * factor
    )
    grad_values = jnp.einsum(
        "chqk,cqhe->ckhe",
        weights.astype(jnp.bfloat16),
        grad_mixed,
        preferred_element_type=jnp.float32,
    )
    return (grad_queries, grad_keys, grad_values, row_total)


def body(
    tokens,
    memory,
    text_len,
    cotangent,
    gain_one,
    bias_one,
    gain_two,
    bias_two,
    gain_three,
    bias_three,
    w_query,
    w_key,
    w_value,
    w_out,
    c_query,
    c_key,
    c_value,
    c_out,
    w_up,
    w_down,
):
    clips = tokens.shape[1]
    shard_frames = tokens.shape[2] * lax.axis_size("tp")
    text_slots = memory.shape[2]
    local_width = w_query.shape[1]
    local_heads = local_width // HD
    query_pos = lax.axis_index("fsdp") * shard_frames + jnp.arange(shard_frames)
    key_pos = jnp.arange(shard_frames * lax.axis_size("fsdp"))
    causal = (key_pos[None, :] <= query_pos[:, None])[None, None]
    shards = (w_query, w_key, w_value, c_query, c_key, c_value, w_up, w_out, c_out, w_down)
    head_shape = (clips, shard_frames, local_heads, HD)
    text_shape = (clips, text_slots, local_heads, HD)
    outputs = []
    input_grads = []
    text_grads = []
    norm_totals = None
    weight_total = None
    for micro in range(MICRO):
        gathered = (
            lax.all_gather(shards[0], "fsdp", axis=0, tiled=True),
            lax.all_gather(shards[1], "fsdp", axis=0, tiled=True),
            lax.all_gather(shards[2], "fsdp", axis=0, tiled=True),
            lax.all_gather(shards[3], "fsdp", axis=0, tiled=True),
            lax.all_gather(shards[4], "fsdp", axis=0, tiled=True),
            lax.all_gather(shards[5], "fsdp", axis=0, tiled=True),
            lax.all_gather(shards[6], "fsdp", axis=0, tiled=True),
            lax.all_gather(shards[7], "fsdp", axis=1, tiled=True),
            lax.all_gather(shards[8], "fsdp", axis=1, tiled=True),
            lax.all_gather(shards[9], "fsdp", axis=1, tiled=True),
        )
        (
            query_full,
            key_full,
            value_full,
            cross_query,
            cross_key,
            cross_value,
            up_full,
            out_full,
            cross_out,
            down_full,
        ) = gathered
        frames = tokens[micro].astype(jnp.float32)
        text_rows = memory[micro]
        counts = text_len[micro]
        normed_one, scaled_one, inverse_one = layer_norm(frames, gain_one, bias_one)
        rows_one = spread_rows(normed_one.astype(jnp.bfloat16))
        queries = project(rows_one, query_full).astype(jnp.bfloat16).reshape(head_shape)
        key_local = project(rows_one, key_full).astype(jnp.bfloat16)
        value_local = project(rows_one, value_full).astype(jnp.bfloat16)
        key_all, value_all = (
            lax.all_gather(key_local, "fsdp", axis=1, tiled=True),
            lax.all_gather(value_local, "fsdp", axis=1, tiled=True),
        )
        key_all = key_all.reshape(clips, -1, local_heads, HD)
        value_all = value_all.reshape(clips, -1, local_heads, HD)
        mixed_one, total_one = attention_forward(queries, key_all, value_all, causal)
        mixed_one = mixed_one.astype(jnp.bfloat16).reshape(clips, shard_frames, local_width)
        after_self = frames + fold_rows(project(mixed_one, out_full))
        normed_two, scaled_two, inverse_two = layer_norm(after_self, gain_two, bias_two)
        rows_two = spread_rows(normed_two.astype(jnp.bfloat16))
        cross_q = project(rows_two, cross_query).astype(jnp.bfloat16).reshape(head_shape)
        cross_k = project(text_rows, cross_key).astype(jnp.bfloat16).reshape(text_shape)
        cross_v = project(text_rows, cross_value).astype(jnp.bfloat16).reshape(text_shape)
        visible = (jnp.arange(text_slots)[None, :] < counts[:, None])[:, None, None, :]
        mixed_two, total_two = attention_forward(cross_q, cross_k, cross_v, visible)
        mixed_two = mixed_two.astype(jnp.bfloat16).reshape(clips, shard_frames, local_width)
        after_cross = after_self + fold_rows(project(mixed_two, cross_out))
        normed_three, scaled_three, inverse_three = layer_norm(after_cross, gain_three, bias_three)
        rows_three = spread_rows(normed_three.astype(jnp.bfloat16))
        hidden = project(rows_three, up_full)
        active = jax.nn.gelu(hidden).astype(jnp.bfloat16)
        result = after_cross + fold_rows(project(active, down_full))
        outputs.append(result.astype(jnp.bfloat16))
        gathered = (
            lax.all_gather(shards[0], "fsdp", axis=0, tiled=True),
            lax.all_gather(shards[1], "fsdp", axis=0, tiled=True),
            lax.all_gather(shards[2], "fsdp", axis=0, tiled=True),
            lax.all_gather(shards[3], "fsdp", axis=0, tiled=True),
            lax.all_gather(shards[4], "fsdp", axis=0, tiled=True),
            lax.all_gather(shards[5], "fsdp", axis=0, tiled=True),
            lax.all_gather(shards[6], "fsdp", axis=0, tiled=True),
            lax.all_gather(shards[7], "fsdp", axis=1, tiled=True),
            lax.all_gather(shards[8], "fsdp", axis=1, tiled=True),
            lax.all_gather(shards[9], "fsdp", axis=1, tiled=True),
        )
        (
            query_full,
            key_full,
            value_full,
            cross_query,
            cross_key,
            cross_value,
            up_full,
            out_full,
            cross_out,
            down_full,
        ) = gathered
        upstream = cotangent[micro].astype(jnp.float32)
        grad_rows = spread_grads(upstream.astype(jnp.bfloat16))
        grad_down = weight_grad(active, grad_rows)
        grad_active = project_back(grad_rows, down_full)
        _, gelu_pull = jax.vjp(jax.nn.gelu, hidden)
        grad_hidden = gelu_pull(grad_active)[0].astype(jnp.bfloat16)
        grad_up = weight_grad(rows_three, grad_hidden)
        grad_three = fold_grads(project_back(grad_hidden, up_full))
        back_three, gain_g3, bias_g3 = norm_back(
            grad_three, scaled_three, inverse_three, gain_three
        )
        upstream = upstream + back_three
        grad_rows = spread_grads(upstream.astype(jnp.bfloat16))
        grad_cout = weight_grad(mixed_two, grad_rows)
        grad_mixed = project_back(grad_rows, cross_out).astype(jnp.bfloat16).reshape(head_shape)
        grad_cq, grad_ck, grad_cv, _ = attention_backward(
            cross_q, cross_k, cross_v, visible, total_two, grad_mixed
        )
        grad_cq = grad_cq.astype(jnp.bfloat16).reshape(clips, shard_frames, local_width)
        grad_ck = grad_ck.reshape(clips, text_slots, local_width)
        grad_cv = grad_cv.reshape(clips, text_slots, local_width)
        grad_cquery = weight_grad(rows_two, grad_cq)
        text_wide = text_rows.astype(jnp.float32)
        grad_ckey = jnp.einsum("cmd,cme->de", text_wide, grad_ck, precision=PRECISE)
        grad_cvalue = jnp.einsum("cmd,cme->de", text_wide, grad_cv, precision=PRECISE)
        text_grads.append(
            jnp.einsum("cme,de->cmd", grad_ck, cross_key.astype(jnp.float32), precision=PRECISE)
            + jnp.einsum("cme,de->cmd", grad_cv, cross_value.astype(jnp.float32), precision=PRECISE)
        )
        grad_two = fold_grads(project_back(grad_cq, cross_query))
        back_two, gain_g2, bias_g2 = norm_back(grad_two, scaled_two, inverse_two, gain_two)
        upstream = upstream + back_two
        grad_rows = spread_grads(upstream.astype(jnp.bfloat16))
        grad_out = weight_grad(mixed_one, grad_rows)
        grad_mixed = project_back(grad_rows, out_full).astype(jnp.bfloat16).reshape(head_shape)
        grad_q, grad_kall, grad_vall, _ = attention_backward(
            queries, key_all, value_all, causal, total_one, grad_mixed
        )
        grad_kloc, grad_vloc = (
            lax.psum_scatter(
                grad_kall.reshape(clips, -1, local_width).astype(jnp.bfloat16),
                "fsdp",
                scatter_dimension=1,
                tiled=True,
            ).astype(jnp.float32),
            lax.psum_scatter(
                grad_vall.reshape(clips, -1, local_width).astype(jnp.bfloat16),
                "fsdp",
                scatter_dimension=1,
                tiled=True,
            ).astype(jnp.float32),
        )
        grad_q = grad_q.astype(jnp.bfloat16).reshape(clips, shard_frames, local_width)
        grad_kloc = grad_kloc.astype(jnp.bfloat16)
        grad_vloc = grad_vloc.astype(jnp.bfloat16)
        grad_query = weight_grad(rows_one, grad_q)
        grad_key = weight_grad(rows_one, grad_kloc)
        grad_value = weight_grad(rows_one, grad_vloc)
        grad_one = fold_grads(
            project_back(grad_q, query_full)
            + project_back(grad_kloc, key_full)
            + project_back(grad_vloc, value_full)
        )
        back_one, gain_g1, bias_g1 = norm_back(grad_one, scaled_one, inverse_one, gain_one)
        input_grads.append(upstream + back_one)
        norm_parts = (gain_g1, bias_g1, gain_g2, bias_g2, gain_g3, bias_g3)
        norm_totals = norm_parts if micro == 0 else jax.tree.map(jnp.add, norm_totals, norm_parts)
        micro_grads = (
            grad_query,
            grad_key,
            grad_value,
            grad_cquery,
            grad_ckey,
            grad_cvalue,
            grad_up,
            grad_out,
            grad_cout,
            grad_down,
        )
        weight_total = (
            micro_grads if micro == 0 else jax.tree.map(jnp.add, weight_total, micro_grads)
        )
    weight_total = (
        lax.psum_scatter(
            weight_total[0].astype(jnp.bfloat16), "fsdp", scatter_dimension=0, tiled=True
        ).astype(jnp.float32),
        lax.psum_scatter(
            weight_total[1].astype(jnp.bfloat16), "fsdp", scatter_dimension=0, tiled=True
        ).astype(jnp.float32),
        lax.psum_scatter(
            weight_total[2].astype(jnp.bfloat16), "fsdp", scatter_dimension=0, tiled=True
        ).astype(jnp.float32),
        lax.psum_scatter(
            weight_total[3].astype(jnp.bfloat16), "fsdp", scatter_dimension=0, tiled=True
        ).astype(jnp.float32),
        lax.psum_scatter(
            weight_total[4].astype(jnp.bfloat16), "fsdp", scatter_dimension=0, tiled=True
        ).astype(jnp.float32),
        lax.psum_scatter(
            weight_total[5].astype(jnp.bfloat16), "fsdp", scatter_dimension=0, tiled=True
        ).astype(jnp.float32),
        lax.psum_scatter(
            weight_total[6].astype(jnp.bfloat16), "fsdp", scatter_dimension=0, tiled=True
        ).astype(jnp.float32),
        lax.psum_scatter(
            weight_total[7].astype(jnp.bfloat16), "fsdp", scatter_dimension=1, tiled=True
        ).astype(jnp.float32),
        lax.psum_scatter(
            weight_total[8].astype(jnp.bfloat16), "fsdp", scatter_dimension=1, tiled=True
        ).astype(jnp.float32),
        lax.psum_scatter(
            weight_total[9].astype(jnp.bfloat16), "fsdp", scatter_dimension=1, tiled=True
        ).astype(jnp.float32),
    )
    summed = lax.psum(
        (
            jnp.stack(text_grads),
            norm_totals[0],
            norm_totals[1],
            norm_totals[2],
            norm_totals[3],
            norm_totals[4],
            norm_totals[5],
        ),
        ("fsdp", "tp"),
    )
    (
        fin_query,
        fin_key,
        fin_value,
        fin_cquery,
        fin_ckey,
        fin_cvalue,
        fin_up,
        fin_out,
        fin_cout,
        fin_down,
    ) = weight_total
    return (
        jnp.stack(outputs),
        jnp.stack(input_grads),
        summed[0],
        summed[1],
        summed[2],
        summed[3],
        summed[4],
        summed[5],
        summed[6],
        fin_query,
        fin_key,
        fin_value,
        fin_out,
        fin_cquery,
        fin_ckey,
        fin_cvalue,
        fin_cout,
        fin_up,
        fin_down,
    )


BLOCK = 256
SCALE = 1.0 / math.sqrt(HD)
PIECES = 4


def pair_swap(values, axis_name):
    return lax.ppermute(values, axis_name, [(0, 1), (1, 0)])


def ring_shift(values, distance):
    size = lax.axis_size("z")
    return lax.ppermute(values, "z", [(i, (i + distance) % size) for i in range(size)])


def ring_flip(values, bit):
    size = lax.axis_size("z")
    return lax.ppermute(values, "z", [(i, i ^ bit) for i in range(size)])


def take(values, index, axis=0):
    return lax.dynamic_index_in_dim(values, index, axis, keepdims=False)


def place(values, piece, index, axis=0):
    return lax.dynamic_update_index_in_dim(values, piece, index, axis)


def ordered(index, own, other):
    return jnp.where(index == 0, jnp.stack([own, other]), jnp.stack([other, own]))


def wide(values):
    return values.astype(jnp.float32)


def narrow(values):
    return values.astype(jnp.bfloat16)


def exchange_clips(values):
    return lax.all_to_all(values, ("y", "z"), 0, 0, tiled=True)


def group_rows(own):
    across = pair_swap(own, "x")
    return [own, pair_swap(own, "c"), across, pair_swap(across, "c")]


def far_sum(parts):
    return narrow(wide(parts[2]) + wide(pair_swap(parts[3], "c")))


def group_terms(parts, far):
    return [parts[0], pair_swap(parts[1], "c"), pair_swap(far, "x")]


def everywhere(values):
    for name in ("c", "x", "y"):
        values = values + pair_swap(values, name)
    bit = 1
    while bit < lax.axis_size("z"):
        values = values + ring_flip(values, bit)
        bit *= 2
    return values


def after(values, *others):
    return lax.optimization_barrier((values, others))[0]


def split_heads(shards):
    rows, units = shards[0].shape
    split = jnp.stack([shard.reshape(rows, 2, units // 2) for shard in shards], axis=1)
    return jnp.transpose(split, (2, 0, 1, 3)).reshape(2, rows, -1)


def join_heads(own, away):
    halves = wide(ordered(lax.axis_index("x"), own, away))
    rows, width = own.shape
    halves = halves.reshape(2, rows, 4, width // 4)
    return [jnp.concatenate([halves[0, :, i], halves[1, :, i]], axis=1) for i in range(4)]


def gather_units(shards):
    at_x, at_c = lax.axis_index("x"), lax.axis_index("c")
    rows, units = shards[0].shape
    split = jnp.stack([shard.reshape(rows, 2, 2, units // 4) for shard in shards])
    split = jnp.transpose(split, (2, 3, 0, 1, 4))
    mine = take(split, at_x)
    other = pair_swap(take(split, 1 - at_x), "x")
    pair = jnp.stack([mine, other], axis=1)
    pair = jnp.stack([take(pair, at_c), pair_swap(take(pair, 1 - at_c), "c")], axis=1)
    own = pair.reshape((1, PIECES) + pair.shape[2:])
    return lax.all_gather(own, ("y", "z"), axis=0, tiled=True)


def scatter_units(grad):
    grad = grad.reshape((-1,) + grad.shape[2:])
    return lax.psum_scatter(grad, ("y", "z"), scatter_dimension=0, tiled=True)[0]


def join_units(total):
    at_x, at_c = lax.axis_index("x"), lax.axis_index("c")
    away = pair_swap(total[2:], "x")
    pair = ordered(at_x, total[:2], away)
    whole = ordered(at_c, pair[:, 0], pair_swap(pair[:, 1], "c"))
    whole = jnp.transpose(wide(whole), (2, 1, 0, 3))
    return whole.reshape(whole.shape[0], -1)


def sum_plane(keep, send):
    got = pair_swap(send, "c")
    away = narrow(wide(keep[1]) + wide(got[1]))
    near = narrow(wide(keep[0]) + wide(got[0]))
    return near, away


def sum_plane_rest(near, got):
    away = narrow(wide(near[1]) + wide(got[1]))
    near = narrow(wide(near[0]) + wide(got[0]))
    return narrow(wide(near) + wide(pair_swap(away, "y")))


def dot_nt(left, right):
    return lax.dot_general(left, right, (((1,), (1,)), ((), ())), preferred_element_type=jnp.float32)


def dot_nn(left, right):
    return lax.dot_general(left, right, (((1,), (0,)), ((), ())), preferred_element_type=jnp.float32)


def dot_tn(left, right):
    return lax.dot_general(left, right, (((0,), (0,)), ((), ())), preferred_element_type=jnp.float32)


def whole_spec(array):
    return pl.BlockSpec(array.shape, lambda *_: (0,) * len(array.shape))


ANYWHERE = pl.BlockSpec(memory_space=pl.ANY)
SCALARS = pl.BlockSpec(memory_space=pltpu.SMEM)


def like(shape, dtype=jnp.bfloat16):
    return jax.ShapeDtypeStruct(shape, dtype)


def diagonal_mask(size):
    row = lax.broadcasted_iota(jnp.int32, (size, size), 0)
    column = lax.broadcasted_iota(jnp.int32, (size, size), 1)
    return column <= row


def block_of(at_y, at_x, at_c):
    return (at_y * 2 + at_x) * 2 + at_c


def natural_rows(ids, piece, upper, rows):
    at_x, at_c = ids[1], ids[2]
    member = (at_x ^ (piece // 2)) * 2 + (at_c ^ (piece % 2))
    return pl.ds(pl.multiple_of((upper * PIECES + member) * rows, rows), rows)


def attend_forward_kernel(ids, *refs):
    rows_in, weights = refs[0:4], refs[4]
    parts, qkv, mixed_out, log_out, mixed = refs[5:9], refs[9], refs[10], refs[11], refs[12]
    halves, frames, width = qkv.shape
    third = width // 3
    rows = rows_in[0].shape[0] // 2
    for at in range(halves):
        for piece in range(PIECES):
            out = narrow(dot_nn(rows_in[piece][...], weights[at, :, :width]))
            for upper in range(2):
                qkv[at, natural_rows(ids, piece, upper, rows), :] = out[upper * rows : (upper + 1) * rows]
    mask = diagonal_mask(BLOCK)
    log_out[...] = jnp.zeros_like(log_out)
    lane = lax.broadcasted_iota(jnp.int32, (BLOCK, log_out.shape[1]), 1)

    def half_heads(at, carry):
        for head in range(third // HD):
            q_lanes, k_lanes, v_lanes = (
                slice(i * third + head * HD, i * third + (head + 1) * HD) for i in range(3)
            )
            for start in range(0, frames, BLOCK):
                block = slice(start, start + BLOCK)
                q = qkv[at, block, q_lanes] * jnp.bfloat16(SCALE)
                near = jnp.where(mask, dot_nt(q, qkv[at, block, k_lanes]), MASKED)
                top = jnp.max(near, axis=-1, keepdims=True)
                if start:
                    past = dot_nt(q, qkv[at, 0:start, k_lanes])
                    top = jnp.maximum(top, jnp.max(past, axis=-1, keepdims=True))
                near = jnp.exp(near - top)
                total = jnp.sum(near, axis=-1, keepdims=True)
                out = dot_nn(narrow(near), qkv[at, block, v_lanes])
                if start:
                    past = jnp.exp(past - top)
                    total = total + jnp.sum(past, axis=-1, keepdims=True)
                    out = out + dot_nn(narrow(past), qkv[at, 0:start, v_lanes])
                mixed[at, block, head * HD : (head + 1) * HD] = narrow(out / total)
                log_total = top + jnp.log(total)
                log_out[block, :] = jnp.where(
                    lane == at * (third // HD) + head, log_total, log_out[block, :]
                )
        return carry

    lax.fori_loop(0, halves, half_heads, 0)
    for piece in range(PIECES):
        for upper in range(2):
            here = natural_rows(ids, piece, upper, rows)
            there = slice(upper * rows, (upper + 1) * rows)
            out = None
            for at in range(halves):
                own = mixed[at, here, :]
                mixed_out[at, piece, there, :] = own
                term = dot_nt(own, weights[at, :, width:])
                out = term if out is None else out + term
            parts[piece][there, :] = narrow(out)


def attend_backward_kernel(ids, *refs):
    rows_in, weights = refs[0:4], refs[4]
    qkv, mixed_in, log_in = refs[5], refs[6], refs[7]
    parts, grad_out = refs[8:12], refs[12]
    grads, totals, back, dk_sum, dv_sum = refs[13:18]
    halves, frames, width = qkv.shape
    third = width // 3
    heads = third // HD
    rows = rows_in[0].shape[0] // 2
    for at in range(halves):
        for piece in range(PIECES):
            out = narrow(dot_nn(rows_in[piece][...], weights[at, :, width:]))
            product = wide(out) * wide(mixed_in[at, piece])
            lane = lax.broadcasted_iota(jnp.int32, (2 * rows, totals.shape[2]), 1)
            sums = jnp.zeros((2 * rows, totals.shape[2]), jnp.float32)
            for head in range(heads):
                one = jnp.sum(product[:, head * HD : (head + 1) * HD], axis=-1, keepdims=True)
                sums = jnp.where(lane == head, one, sums)
            for upper in range(2):
                here = natural_rows(ids, piece, upper, rows)
                there = slice(upper * rows, (upper + 1) * rows)
                grads[at, here, :] = out[there]
                totals[at, here, :] = sums[there]
    mask = diagonal_mask(BLOCK)

    def half_heads(at, carry):
        dk_sum[...] = jnp.zeros_like(dk_sum)
        dv_sum[...] = jnp.zeros_like(dv_sum)
        for head in range(heads):
            q_lanes, k_lanes, v_lanes = (
                slice(i * third + head * HD, i * third + (head + 1) * HD) for i in range(3)
            )
            o_lanes = slice(head * HD, (head + 1) * HD)
            log_lane = lax.broadcasted_iota(jnp.int32, (BLOCK, log_in.shape[1]), 1)
            for start in range(0, frames, BLOCK):
                block = slice(start, start + BLOCK)
                q = qkv[at, block, q_lanes] * jnp.bfloat16(SCALE)
                grad = grads[at, block, o_lanes]
                q_turned = narrow(wide(q).T)
                grad_turned = narrow(wide(grad).T)
                log_total = jnp.sum(
                    jnp.where(log_lane == at * heads + head, log_in[block, :], 0.0),
                    axis=-1,
                    keepdims=True,
                )
                row_total = totals[at, block, head : head + 1]
                dq = None
                for columns in (block, slice(0, start)):
                    if columns.stop == 0:
                        continue
                    keys = qkv[at, columns, k_lanes]
                    weight = jnp.exp(dot_nt(q, keys) - log_total)
                    if columns is block:
                        weight = jnp.where(mask, weight, 0.0)
                    grad_weight = dot_nt(grad, qkv[at, columns, v_lanes])
                    scores = narrow(weight * (grad_weight - row_total))
                    part = dot_nn(scores, keys)
                    dq = part if dq is None else dq + part
                    dk_sum[o_lanes, columns] += dot_nn(q_turned, scores)
                    dv_sum[o_lanes, columns] += dot_nn(grad_turned, narrow(weight))
                back[at, block, q_lanes] = narrow(dq * SCALE)
        for start in range(0, frames, BLOCK):
            block = slice(start, start + BLOCK)
            back[at, block, third : 2 * third] = narrow(dk_sum[:, block].T)
            back[at, block, 2 * third :] = narrow(dv_sum[:, block].T)
        return carry

    lax.fori_loop(0, halves, half_heads, 0)
    for piece in range(PIECES):
        for at in range(halves):
            for upper in range(2):
                there = slice(upper * rows, (upper + 1) * rows)
                grad_out[at, piece, there, :] = back[at, natural_rows(ids, piece, upper, rows), :]
        out = None
        for at in range(halves):
            term = dot_nt(grad_out[at, piece], weights[at, :, :width])
            out = term if out is None else out + term
        parts[piece][...] = narrow(out)


def attend_forward(ids, rows_in, weights):
    rows, model = rows_in[0].shape
    halves, _, units = weights.shape
    width = units // 4
    frames = PIECES * rows
    outs = [like((rows, model))] * PIECES + [
        like((halves, frames, 3 * width)),
        like((halves, PIECES, rows, width)),
        like((frames, 128), jnp.float32),
    ]
    out = pl.pallas_call(
        attend_forward_kernel,
        in_specs=[SCALARS] + [pl.BlockSpec(memory_space=pltpu.VMEM)] * (PIECES + 1),
        out_specs=[pl.BlockSpec(memory_space=pltpu.VMEM)] * len(outs),
        out_shape=outs,
        scratch_shapes=[
            pltpu.VMEM((halves, frames, width), jnp.bfloat16),
        ],
        compiler_params=pltpu.CompilerParams(vmem_limit_bytes=56 * 2**20),
        cost_estimate=pl.CostEstimate(
            flops=30 * 10**9, bytes_accessed=24 * 2**20, transcendentals=0
        ),
        name="attend_forward",
    )(ids, *rows_in, weights)
    return out[:4], out[4], out[5], out[6]


def attend_backward(ids, rows_in, weights, qkv, mixed, log_total):
    rows, model = rows_in[0].shape
    halves, _, units = weights.shape
    frames, width = qkv.shape[1], qkv.shape[2] // 3
    outs = [like((rows, model))] * PIECES + [like((halves, PIECES, rows, 3 * width))]
    vmem = pl.BlockSpec(memory_space=pltpu.VMEM)
    out = pl.pallas_call(
        attend_backward_kernel,
        in_specs=[SCALARS] + [vmem] * (PIECES + 4),
        out_specs=[vmem] * len(outs),
        out_shape=outs,
        scratch_shapes=[
            pltpu.VMEM((halves, frames, width), jnp.bfloat16),
            pltpu.VMEM((halves, frames, 128), jnp.float32),
            pltpu.VMEM((halves, frames, 3 * width), jnp.bfloat16),
            pltpu.VMEM((width, frames), jnp.float32),
            pltpu.VMEM((width, frames), jnp.float32),
        ],
        compiler_params=pltpu.CompilerParams(vmem_limit_bytes=58 * 2**20),
        cost_estimate=pl.CostEstimate(
            flops=50 * 10**9, bytes_accessed=24 * 2**20, transcendentals=0
        ),
        name="attend_backward",
    )(ids, *rows_in, weights, qkv, mixed, log_total)
    return out[:4], out[4]


def attend_grads_kernel(ids, *refs):
    normed, grads = refs[0:4], refs[4:8]
    grad_qkv, mixed, out = refs[8:11]
    halves, _, _, width = grad_qkv.shape
    rows = out.shape[-2]
    at_c = ids[2]
    for at in range(halves):
        left = right = None
        for piece in range(PIECES):
            one = dot_tn(normed[piece][...], grad_qkv[at, piece])
            two = dot_tn(grads[piece][...], mixed[at, piece])
            left = one if left is None else left + one
            right = two if right is None else right + two
        for core in range(2):
            block = slice(core * rows, (core + 1) * rows)
            out[at_c ^ core, at, 0, :, :width] = narrow(left[block])
            out[at_c ^ core, at, 0, :, width:] = narrow(right[block])


def attend_grads(ids, normed, grads, grad_qkv, mixed, other_y):
    rows, model = normed[0].shape
    halves, units = mixed.shape[0], 4 * mixed.shape[-1]
    strip = model // 4
    column = pl.BlockSpec((rows, strip), lambda i, ids: (0, (ids[0] ^ other_y) * 2 + i))
    return pl.pallas_call(
        attend_grads_kernel,
        grid_spec=pltpu.PrefetchScalarGridSpec(
            num_scalar_prefetch=1,
            grid=(2,),
            in_specs=[column] * 8 + [whole_spec(grad_qkv), whole_spec(mixed)],
            out_specs=pl.BlockSpec(
                (2, halves, 1, strip // 2, units), lambda i, ids: (0, 0, i ^ ids[1], 0, 0)
            ),
        ),
        out_shape=like((2, halves, 2, strip // 2, units)),
        compiler_params=pltpu.CompilerParams(vmem_limit_bytes=40 * 2**20),
        cost_estimate=pl.CostEstimate(
            flops=6 * 10**9, bytes_accessed=12 * 2**20, transcendentals=0
        ),
        name="attend_grads",
    )(ids, *normed, *grads, grad_qkv, mixed)


def gelu_both(values):
    factor = math.sqrt(2.0 / math.pi)
    square = values * values
    bent = jnp.tanh(factor * values * (1.0 + 0.044715 * square))
    slope = 0.5 * (1.0 + bent) + 0.5 * values * (1.0 - bent * bent) * factor * (
        1.0 + 3.0 * 0.044715 * square
    )
    return 0.5 * values * (1.0 + bent), slope


def feed_kernel(ids, *refs):
    rows_in, grads_in, units_in = refs[0:4], refs[4:8], refs[8]
    result_out, back_out, active_out, hidden_out = refs[9:13], refs[13:17], refs[17], refs[18]
    rows_all, grads_all, up, down, result, back, active, hidden, w_sem, in_sem, out_sem = refs[19:]
    at_x, at_c = ids[1], ids[2]
    rows, model = rows_in[0].shape
    shard_rows, width = units_in.shape[-2:]
    groups = units_in.shape[0] // 2
    copies = []
    for which, target in enumerate((up, down)):
        for other_y in range(2):
            for at_z in range(groups):
                for piece in range(PIECES):
                    block = block_of(other_y, at_x ^ (piece // 2), at_c ^ (piece % 2))
                    place_rows = pl.ds(pl.multiple_of(block * shard_rows, shard_rows), shard_rows)
                    lanes = slice((at_z % 2) * width, (at_z % 2 + 1) * width)
                    copies.append(
                        pltpu.make_async_copy(
                            units_in.at[other_y * groups + at_z, piece, which],
                            target.at[at_z // 2, place_rows, lanes],
                            w_sem.at[len(copies)],
                        )
                    )
    for piece in range(PIECES):
        copies.append(
            pltpu.make_async_copy(rows_in[piece], rows_all.at[piece], in_sem.at[2 * piece])
        )
        copies.append(
            pltpu.make_async_copy(grads_in[piece], grads_all.at[piece], in_sem.at[2 * piece + 1])
        )
    for copy in copies:
        copy.start()
    for copy in copies:
        copy.wait()
    blocks = groups // 2

    def outputs(piece, slot):
        return [
            pltpu.make_async_copy(source.at[slot], target, out_sem.at[slot, i])
            for i, (source, target) in enumerate(
                (
                    (result, result_out[piece]),
                    (back, back_out[piece]),
                    (active, active_out.at[piece]),
                    (hidden, hidden_out.at[piece]),
                )
            )
        ]

    for piece in range(PIECES):
        slot = piece % 2
        if piece >= 2:
            for copy in outputs(piece - 2, slot):
                copy.wait()

        def one_block(at, carry):
            own = rows_all[piece]
            value, slope = gelu_both(dot_nn(own, up[at]))
            value = narrow(value)
            change = narrow(dot_nn(grads_all[piece], down[at]) * slope)
            lanes = pl.ds(pl.multiple_of(at * 2 * width, 2 * width), 2 * width)
            active[slot, :, lanes] = value
            hidden[slot, :, lanes] = change
            return carry

        lax.fori_loop(0, blocks, one_block, 0)

        def one_result(at, carry):
            here = pl.ds(pl.multiple_of(at * 2 * width, 2 * width), 2 * width)
            first = second = None
            for part in range(blocks):
                lanes = slice(part * 2 * width, (part + 1) * 2 * width)
                one = dot_nt(active[slot, :, lanes], down[part, here, :])
                two = dot_nt(hidden[slot, :, lanes], up[part, here, :])
                first = one if first is None else first + one
                second = two if second is None else second + two
            result[slot, :, here] = narrow(first)
            back[slot, :, here] = narrow(second)
            return carry

        lax.fori_loop(0, model // (2 * width), one_result, 0)
        for copy in outputs(piece, slot):
            copy.start()
    for piece in (PIECES - 2, PIECES - 1):
        for copy in outputs(piece, piece % 2):
            copy.wait()


def feed(ids, rows_in, grads_in, both):
    rows, model = rows_in[0].shape
    units = both.shape[0] // 2 * both.shape[-1]
    outs = [like((rows, model))] * 8 + [like((PIECES, rows, units))] * 2
    blocks = both.shape[0] // 4
    weight = pltpu.VMEM((blocks, model, 2 * both.shape[-1]), jnp.bfloat16)
    out = pl.pallas_call(
        feed_kernel,
        in_specs=[SCALARS] + [ANYWHERE] * 9,
        out_specs=[ANYWHERE] * 10,
        out_shape=outs,
        scratch_shapes=[
            pltpu.VMEM((PIECES, rows, model), jnp.bfloat16),
            pltpu.VMEM((PIECES, rows, model), jnp.bfloat16),
            weight,
            weight,
            pltpu.VMEM((2, rows, model), jnp.bfloat16),
            pltpu.VMEM((2, rows, model), jnp.bfloat16),
            pltpu.VMEM((2, rows, units), jnp.bfloat16),
            pltpu.VMEM((2, rows, units), jnp.bfloat16),
            pltpu.SemaphoreType.DMA((2 * both.shape[0] * PIECES,)),
            pltpu.SemaphoreType.DMA((2 * PIECES,)),
            pltpu.SemaphoreType.DMA((2, 4)),
        ],
        compiler_params=pltpu.CompilerParams(vmem_limit_bytes=56 * 2**20),
        cost_estimate=pl.CostEstimate(
            flops=8 * PIECES * rows * model * units, bytes_accessed=36 * 2**20, transcendentals=0
        ),
        name="feed_forward",
    )(ids, *rows_in, *grads_in, both)
    return out[0:4], out[4:8], out[8], out[9]


def feed_grads_kernel(ids, *refs):
    left, right, out = refs[0:4], refs[4], refs[5]
    rows, width = out.shape[-2:]
    at_c = ids[2]
    for at_z in range(out.shape[1]):
        total = None
        for piece in range(PIECES):
            one = dot_tn(left[piece][...], right[piece, :, at_z * width : (at_z + 1) * width])
            total = one if total is None else total + one
        for core in range(2):
            out[0, at_z, 0, at_c ^ core] = narrow(total[core * rows : (core + 1) * rows])


def feed_grads(ids, left, right):
    rows, model = left[0].shape
    units = right.shape[-1]
    groups = lax.axis_size("z")
    strip = model // 4
    shape = (2, groups, 2, 2, strip // 2, units // groups)
    out = pl.pallas_call(
        feed_grads_kernel,
        grid_spec=pltpu.PrefetchScalarGridSpec(
            num_scalar_prefetch=1,
            grid=(4,),
            in_specs=[pl.BlockSpec((rows, strip), lambda i, ids: (0, i))] * 4 + [whole_spec(right)],
            out_specs=pl.BlockSpec(
                (1, groups, 1, 2, strip // 2, units // groups),
                lambda i, ids: (i // 2, 0, (i % 2) ^ ids[1], 0, 0, 0),
            ),
        ),
        out_shape=like(shape),
        compiler_params=pltpu.CompilerParams(vmem_limit_bytes=40 * 2**20),
        cost_estimate=pl.CostEstimate(
            flops=2 * PIECES * rows * model * units, bytes_accessed=16 * 2**20, transcendentals=0
        ),
        name="feed_grads",
    )(ids, *left, right)
    return out.reshape(2, groups, PIECES, strip // 2, units // groups)


def block_pair(values):
    low = lax.broadcasted_iota(jnp.int32, values.shape, 1) < HD
    zero = jnp.zeros_like(values)
    return jnp.concatenate([jnp.where(low, values, zero), jnp.where(low, zero, values)], axis=0)


def by_half(low, values, reduce, empty):
    first = reduce(jnp.where(low, values, empty), axis=-1, keepdims=True)
    second = reduce(jnp.where(low, empty, values), axis=-1, keepdims=True)
    return jnp.where(low, first, second)


def cross_weights(count, queries, keys):
    slots = keys.shape[0] // 2
    scores = dot_nt(queries, keys)
    lane = lax.broadcasted_iota(jnp.int32, scores.shape, 1)
    low = lane < slots
    scores = jnp.where(jnp.where(low, lane, lane - slots) < count, scores, MASKED)
    raised = jnp.exp(scores - by_half(low, scores, jnp.max, MASKED))
    return raised / by_half(low, raised, jnp.sum, 0.0), low


def cross_copies(ids, pieces, weights, sem):
    rows = pieces[0].shape[-2]
    copies = []
    for index, piece in enumerate(pieces):
        block = block_of(ids[0] ^ (index % 2), ids[1] ^ (index // 2 % 2), ids[2] ^ (index // 4))
        for distance in range(piece.shape[0]):
            at_z = (ids[3] + piece.shape[0] - distance) % piece.shape[0]
            target = weights.at[at_z, pl.ds(pl.multiple_of(block * rows, rows), rows)]
            copies.append(pltpu.make_async_copy(piece.at[distance], target, sem.at[len(copies)]))
    return copies


def lanes_of(at, size):
    return pl.ds(pl.multiple_of(at * size, size), size)


def cross_forward_kernel(ids, count, *refs):
    tokens, terms, norms, keys_values, pieces = refs[0], refs[1:4], refs[4], refs[5], refs[6:14]
    self_out, normed_out, queries, mixed, cross_out, rows_out = refs[14:20]
    weights, sem = refs[20:22]
    copies = cross_copies(ids, pieces, weights, sem)
    for copy in copies:
        copy.start()
    after_self = wide(tokens[...])
    for term in terms:
        after_self = after_self + wide(term[...])
    self_out[...] = after_self
    normed = narrow(layer_norm(after_self, norms[0:1, :], norms[1:2, :])[0])
    normed_out[...] = normed
    for copy in copies:
        copy.wait()
    width = weights.shape[2] // 2
    model = tokens.shape[1]
    for at in range(weights.shape[0]):
        out = dot_nn(normed_out[...], weights[at, :, :width])
        queries[:, at * width : (at + 1) * width] = narrow(out)

    def one_pair(at, carry):
        lanes = lanes_of(at, 2 * HD)
        query = queries[:, lanes] * jnp.bfloat16(SCALE)
        keys = block_pair(keys_values[:, lanes])
        values = block_pair(keys_values[:, lanes_of(at + model // (2 * HD), 2 * HD)])
        weight, _ = cross_weights(count[0], query, keys)
        mixed[:, lanes] = narrow(dot_nn(narrow(weight), values))
        return carry

    lax.fori_loop(0, model // (2 * HD), one_pair, 0)
    after_cross = self_out[...]
    for at in range(weights.shape[0]):
        after_cross = after_cross + dot_nt(
            mixed[:, at * width : (at + 1) * width], weights[at, :, width:]
        )
    cross_out[...] = after_cross
    rows_out[...] = narrow(layer_norm(after_cross, norms[2:3, :], norms[3:4, :])[0])


def cross_forward(ids, count, tokens, terms, norms, keys_values, pieces):
    rows, model = tokens.shape
    outs = [
        like((rows, model), jnp.float32),
        like((rows, model)),
        like((rows, model)),
        like((rows, model)),
        like((rows, model), jnp.float32),
        like((rows, model)),
    ]
    vmem = pl.BlockSpec(memory_space=pltpu.VMEM)
    size, shard_rows, width = pieces[0].shape
    return pl.pallas_call(
        cross_forward_kernel,
        in_specs=[SCALARS] * 2 + [vmem] * 6 + [ANYWHERE] * 8,
        out_specs=[vmem] * len(outs),
        out_shape=outs,
        scratch_shapes=[
            pltpu.VMEM((size, 8 * shard_rows, width), jnp.bfloat16),
            pltpu.SemaphoreType.DMA((8 * size,)),
        ],
        compiler_params=pltpu.CompilerParams(vmem_limit_bytes=48 * 2**20),
        cost_estimate=pl.CostEstimate(
            flops=12 * 10**9, bytes_accessed=24 * 2**20, transcendentals=0
        ),
        name="cross_forward",
    )(ids, count, tokens, *terms, norms, keys_values, *pieces)


def norm_gradient(upstream, values, gain_vec, bias_vec):
    _, scaled, inverse = layer_norm(values, gain_vec, bias_vec)
    weighted = upstream * gain_vec
    result = inverse * (
        weighted
        - jnp.mean(weighted, axis=-1, keepdims=True)
        - scaled * jnp.mean(weighted * scaled, axis=-1, keepdims=True)
    )
    return (
        result,
        jnp.sum(upstream * scaled, axis=0, keepdims=True),
        jnp.sum(upstream, axis=0, keepdims=True),
    )


def cross_backward_kernel(ids, count, *refs):
    upstream, terms, norms, keys_values = refs[0], refs[1:4], refs[4], refs[5]
    self_in, cross_in, queries, pieces = refs[6], refs[7], refs[8], refs[9:17]
    grad_out, first_out, second_out, dq_out, dkv_out, norm_out = refs[17:23]
    weights, grads, sem = refs[23:26]
    copies = cross_copies(ids, pieces, weights, sem)
    for copy in copies:
        copy.start()
    grad_three = wide(terms[0][...]) + wide(terms[1][...]) + wide(terms[2][...])
    back, gain_g, bias_g = norm_gradient(
        grad_three, cross_in[...], norms[2:3, :], norms[3:4, :]
    )
    norm_out[2:3, :] = gain_g
    norm_out[3:4, :] = bias_g
    grad_two = wide(upstream[...]) + back
    grad_out[...] = grad_two
    second_out[...] = narrow(grad_two)
    for copy in copies:
        copy.wait()
    width = weights.shape[2] // 2
    model = upstream.shape[1]
    slots = keys_values.shape[0]
    for at in range(weights.shape[0]):
        out = dot_nn(second_out[...], weights[at, :, width:])
        grads[:, at * width : (at + 1) * width] = narrow(out)
    dims_low = lax.broadcasted_iota(jnp.int32, (slots, 2 * HD), 1) < HD

    def one_pair(at, carry):
        lanes = lanes_of(at, 2 * HD)
        value_lanes = lanes_of(at + model // (2 * HD), 2 * HD)
        query = queries[:, lanes] * jnp.bfloat16(SCALE)
        keys = block_pair(keys_values[:, lanes])
        weight, low = cross_weights(count[0], query, keys)
        grad = grads[:, lanes]
        grad_weight = dot_nt(grad, block_pair(keys_values[:, value_lanes]))
        scores = weight * (grad_weight - by_half(low, grad_weight * weight, jnp.sum, 0.0))
        scores = narrow(scores)
        dq_out[:, lanes] = narrow(dot_nn(scores, keys) * SCALE)
        dk = dot_tn(scores, query)
        strips = width // (2 * HD)
        low_lanes = lanes_of(at % strips, 2 * HD)
        dkv_out[at // strips, :, low_lanes] = narrow(jnp.where(dims_low, dk[:slots], dk[slots:]))
        dv = dot_tn(narrow(weight), grad)
        high_lanes = lanes_of(at % strips + strips, 2 * HD)
        dkv_out[at // strips, :, high_lanes] = narrow(jnp.where(dims_low, dv[:slots], dv[slots:]))
        return carry

    lax.fori_loop(0, model // (2 * HD), one_pair, 0)
    grad_two_rows = None
    for at in range(weights.shape[0]):
        term = dot_nt(dq_out[:, at * width : (at + 1) * width], weights[at, :, :width])
        grad_two_rows = term if grad_two_rows is None else grad_two_rows + term
    back, gain_g, bias_g = norm_gradient(grad_two_rows, self_in[...], norms[0:1, :], norms[1:2, :])
    norm_out[0:1, :] = gain_g
    norm_out[1:2, :] = bias_g
    grad_one = grad_out[...] + back
    grad_out[...] = grad_one
    first_out[...] = narrow(grad_one)


def cross_backward(
    ids, count, upstream, terms, norms, keys_values, after_self, after_cross, queries, pieces
):
    rows, model = upstream.shape
    slots = keys_values.shape[0]
    outs = [
        like((rows, model), jnp.float32),
        like((rows, model)),
        like((rows, model)),
        like((rows, model)),
        like((pieces[0].shape[0], slots, 2 * model // pieces[0].shape[0])),
        like((4, model), jnp.float32),
    ]
    vmem = pl.BlockSpec(memory_space=pltpu.VMEM)
    size, shard_rows, width = pieces[0].shape
    return pl.pallas_call(
        cross_backward_kernel,
        in_specs=[SCALARS] * 2 + [vmem] * 9 + [ANYWHERE] * 8,
        out_specs=[vmem] * len(outs),
        out_shape=outs,
        scratch_shapes=[
            pltpu.VMEM((size, 8 * shard_rows, width), jnp.bfloat16),
            pltpu.VMEM((rows, model), jnp.bfloat16),
            pltpu.SemaphoreType.DMA((8 * size,)),
        ],
        compiler_params=pltpu.CompilerParams(vmem_limit_bytes=56 * 2**20),
        cost_estimate=pl.CostEstimate(
            flops=16 * 10**9, bytes_accessed=28 * 2**20, transcendentals=0
        ),
        name="cross_backward",
    )(
        ids,
        count,
        upstream,
        *terms,
        norms,
        keys_values,
        after_self,
        after_cross,
        queries,
        *pieces,
    )


def cross_grads_kernel(ids, normed, grad_queries, grads, mixed, keep, send):
    size, rows, width = keep.shape[2], keep.shape[3], keep.shape[4] // 2
    first = ids[2] == 0
    for at in range(size):
        lanes = slice(at * width, (at + 1) * width)
        distance = (ids[3] + size - at) % size
        for part, (left, right) in enumerate(((normed, grad_queries), (grads, mixed))):
            out = narrow(dot_tn(left[...], right[:, lanes]))
            there = slice(part * width, (part + 1) * width)
            keep[0, 0, distance, :, there] = jnp.where(first, out[:rows], out[rows:])
            send[0, 0, distance, :, there] = jnp.where(first, out[rows:], out[:rows])


def cross_grads(ids, normed, grad_queries, grads, mixed):
    rows, model = normed.shape
    size = lax.axis_size("z")
    strip = model // 4
    column = pl.BlockSpec((rows, strip), lambda i, ids: (0, i))
    shape = (2, 2, size, strip // 2, 2 * (model // size))
    out = pl.BlockSpec(
        (1, 1) + shape[2:], lambda i, ids: ((i % 2) ^ ids[1], (i // 2) ^ ids[0], 0, 0, 0)
    )
    return pl.pallas_call(
        cross_grads_kernel,
        grid_spec=pltpu.PrefetchScalarGridSpec(
            num_scalar_prefetch=1,
            grid=(4,),
            in_specs=[column, whole_spec(grad_queries), column, whole_spec(mixed)],
            out_specs=[out, out],
        ),
        out_shape=[like(shape), like(shape)],
        compiler_params=pltpu.CompilerParams(vmem_limit_bytes=40 * 2**20),
        cost_estimate=pl.CostEstimate(
            flops=4 * rows * model * model, bytes_accessed=14 * 2**20, transcendentals=0
        ),
        name="cross_grads",
    )(ids, normed, grad_queries, grads, mixed)


MESH = pl.DeviceIdType.MESH


def where_am_i():
    return tuple(lax.axis_index(name) for name in ("y", "x", "c", "z"))


def send_to(source, target, send_sem, recv_sem, device):
    return pltpu.make_async_remote_copy(
        src_ref=source,
        dst_ref=target,
        send_sem=send_sem,
        recv_sem=recv_sem,
        device_id=device,
        device_id_type=MESH,
    )


def groups_around(size):
    at_y, at_x, at_c, at_z = where_am_i()
    return [
        ((at_y + step // size) % 2, at_x, at_c, (at_z + step % size) % size)
        for step in range(2 * size)
    ]


def meet(size):
    at_y, at_x, at_c, at_z = where_am_i()
    others = groups_around(size)[1:]
    others += [(at_y, 1 - at_x, at_c, at_z), (at_y, at_x, 1 - at_c, at_z)]
    barrier = pltpu.get_barrier_semaphore()
    for other in others:
        pl.semaphore_signal(barrier, inc=1, device_id=other, device_id_type=MESH)
    pl.semaphore_wait(barrier, len(others))


def exchange_copies(source, target, size, send_sem, recv_sem):
    at_y, _, _, at_z = where_am_i()
    here = at_y * size + at_z
    copies = []
    for step, group in enumerate(groups_around(size)):
        there = group[0] * size + group[3]
        if step == 0:
            copies.append(pltpu.make_async_copy(source.at[there], target.at[here], recv_sem.at[0]))
        else:
            copies.append(
                send_to(
                    source.at[there], target.at[here], send_sem.at[step], recv_sem.at[step], group
                )
            )
    return copies


def block_rows(at_y, at_x, at_c, rows):
    return pl.ds(pl.multiple_of(((at_y * 2 + at_x) * 2 + at_c) * rows, rows), rows)


def start_kernel(
    size,
    tokens,
    split,
    norm,
    cross,
    clip_out,
    rows_own,
    rows_c,
    rows_x,
    rows_xc,
    weights,
    cross_near_out,
    cross_x_out,
    cross_near,
    cross_x,
    held,
    clip,
    normed,
    clip_send,
    clip_recv,
    x_sem,
    ring_send,
    ring_recv,
    y_send,
    y_recv,
    c_send,
    c_recv,
    c_local,
    row_sem,
    out_sem,
    cross_ring_sem,
    cross_x_sem,
):
    at_y, at_x, at_c, at_z = where_am_i()
    rows = split.shape[1]
    half = size // 2
    x_side = (at_y, 1 - at_x, at_c, at_z)
    y_side = (1 - at_y, at_x, at_c, at_z)
    c_side = (at_y, at_x, 1 - at_c, at_z)
    z_next = (at_y, at_x, at_c, (at_z + 1) % size)
    meet(size)
    frames = exchange_copies(tokens, clip, size, clip_send, clip_recv)
    for copy in frames:
        copy.start()
    first = pltpu.make_async_copy(split.at[at_x], held.at[0, 0, 0], out_sem.at[0])
    first.start()
    over = send_to(split.at[1 - at_x], held.at[0, 0, 1], x_sem.at[0], x_sem.at[1], x_side)
    over.start()

    def ring(step, side):
        return send_to(
            held.at[step, 0, side],
            held.at[step + 1, 0, side],
            ring_send.at[step, side],
            ring_recv.at[step, side],
            z_next,
        )

    def across(step, side):
        return send_to(
            held.at[step, 0, side],
            held.at[step, 1, side],
            y_send.at[step, side],
            y_recv.at[step, side],
            y_side,
        )

    def cross_send(step):
        source = cross_near.at[step]
        copies = [
            send_to(
                source, cross_x.at[step], cross_x_sem.at[0, step], cross_x_sem.at[1, step], x_side
            )
        ]
        if step < size - 1:
            copies.append(
                send_to(
                    source,
                    cross_near.at[step + 1],
                    cross_ring_sem.at[0, step],
                    cross_ring_sem.at[1, step],
                    z_next,
                )
            )
        return copies

    def settle(step, other_y, side):
        target = weights.at[
            step % half, block_rows((at_y + other_y) % 2, (at_x + side) % 2, at_c, rows)
        ]
        source = held.at[step, other_y, side]
        slot = (step % half, other_y, side)
        local = pltpu.make_async_copy(source, target, c_local.at[slot])
        remote = send_to(source, target, c_send.at[slot], c_recv.at[slot], c_side)
        return local, remote

    def settle_start(step, other_y, side):
        local, remote = settle(step, other_y, side)

        @pl.when(at_c == step // half)
        def _():
            local.start()

        @pl.when(at_c != step // half)
        def _():
            remote.start()

    cross_own = pltpu.make_async_copy(cross, cross_near.at[0], out_sem.at[3])
    cross_own.start()
    for side in range(2):
        if side == 0:
            first.wait()
        else:
            over.wait_recv()
        ring(0, side).start()
        across(0, side).start()
        settle_start(0, 0, side)
    cross_own.wait()

    def ring_step(step):
        for side in range(2):
            ring(step - 1, side).wait_recv()
            if step < size - 1:
                ring(step, side).start()
            across(step, side).start()
            settle_start(step, 0, side)

    def cross_step(step):
        if step:
            cross_send(step - 1)[1].wait_recv()
        for copy in cross_send(step):
            copy.start()

    ring_step(1)
    for copy in frames:
        if copy is frames[0]:
            copy.wait()
        else:
            copy.wait_recv()
    keep = pltpu.make_async_copy(clip, clip_out, out_sem.at[1])
    keep.start()
    gain, bias = norm[0:1, :], norm[1:2, :]

    def one_block(at, carry):
        here = pl.ds(pl.multiple_of(at * clip.shape[1], clip.shape[1]), clip.shape[1])
        normed[here, :] = narrow(layer_norm(wide(clip[at]), gain, bias)[0])
        return carry

    lax.fori_loop(0, clip.shape[0], one_block, 0)
    own = pltpu.make_async_copy(normed, rows_own, out_sem.at[2])
    to_x = send_to(normed, rows_x, row_sem.at[0], row_sem.at[1], x_side)
    to_c = send_to(normed, rows_c, row_sem.at[2], row_sem.at[3], c_side)
    to_x.start()
    to_c.start()
    own.start()
    ring_step(2)
    ring_step(3)
    cross_step(0)
    for step in range(size):
        for side in range(2):
            across(step, side).wait_recv()
            settle_start(step, 1, side)
        if step:
            cross_step(step)
    to_x.wait_recv()
    relay = send_to(rows_x, rows_xc, row_sem.at[4], row_sem.at[5], c_side)
    relay.start()
    for step in range(size):
        copies = cross_send(step)
        copies[0].wait()
        if step < size - 1:
            copies[1].wait_send()
    cross_outs = [
        pltpu.make_async_copy(cross_near, cross_near_out, out_sem.at[3]),
        pltpu.make_async_copy(cross_x, cross_x_out, out_sem.at[4]),
    ]
    for copy in cross_outs:
        copy.start()
    for copy in cross_outs:
        copy.wait()
    for step in range(half):
        for other_y in range(2):
            for side in range(2):
                local, remote = settle(step, other_y, side)
                local.wait()
                remote.wait()
    relay.wait()
    to_c.wait()
    to_x.wait_send()
    own.wait()
    keep.wait()
    over.wait_send()
    for copy in frames[1:]:
        copy.wait_send()
    for step in range(size):
        for side in range(2):
            across(step, side).wait_send()
            if step < size - 1:
                ring(step, side).wait_send()


def start_up(tokens, split, norm, cross):
    size = lax.axis_size("z")
    groups, frames, model = tokens.shape
    rows, units = split.shape[1:]
    half = size // 2
    vmem = pl.BlockSpec(memory_space=pltpu.VMEM)
    dma = pltpu.SemaphoreType.DMA
    out = pl.pallas_call(
        functools.partial(start_kernel, size),
        in_specs=[vmem] * 4,
        out_specs=[ANYWHERE] * 8,
        out_shape=[like(tokens.shape)]
        + [like((groups * frames, model))] * PIECES
        + [like((half, 8 * rows, units))]
        + [like((size,) + cross.shape)] * 2,
        scratch_shapes=[
            pltpu.VMEM((size,) + cross.shape, jnp.bfloat16),
            pltpu.VMEM((size,) + cross.shape, jnp.bfloat16),
            pltpu.VMEM((size, 2, 2, rows, units), jnp.bfloat16),
            pltpu.VMEM(tokens.shape, jnp.bfloat16),
            pltpu.VMEM((groups * frames, model), jnp.bfloat16),
            dma((groups,)),
            dma((groups,)),
            dma((2,)),
            dma((size - 1, 2)),
            dma((size - 1, 2)),
            dma((size, 2)),
            dma((size, 2)),
            dma((half, 2, 2)),
            dma((half, 2, 2)),
            dma((half, 2, 2)),
            dma((6,)),
            dma((5,)),
            dma((2, size - 1)),
            dma((2, size)),
        ],
        compiler_params=pltpu.CompilerParams(
            collective_id=1, has_side_effects=True, vmem_limit_bytes=32 * 2**20
        ),
        cost_estimate=pl.CostEstimate(
            flops=10**7, bytes_accessed=200 * 2**20, transcendentals=0
        ),
        name="start_up",
    )(tokens, split, norm, cross)
    return out[0].reshape(-1, model), out[1:5], out[5], out[6:8]


def middle_kernel(
    size,
    part_own,
    part_c,
    part_x,
    part_xc,
    near,
    side,
    text,
    cot,
    term_c,
    term_x,
    near_y,
    side_y,
    near_c,
    side_c,
    near_yc,
    side_yc,
    text_out,
    cot_c,
    cot_x,
    cot_xc,
    text_parts,
    far_held,
    far_sum,
    text_held,
    text_sum,
    core_sem,
    x_sem,
    y_sem,
    c_sem,
    text_sem,
    out_sem,
    text_send,
    text_recv,
    cot_sem,
):
    at_y, at_x, at_c, at_z = where_am_i()
    x_side = (at_y, 1 - at_x, at_c, at_z)
    y_side = (1 - at_y, at_x, at_c, at_z)
    c_side = (at_y, at_x, 1 - at_c, at_z)
    meet(size)
    exchange = exchange_copies(text, text_parts, size, text_send, text_recv)

    def swap(source, target, sem, at, device):
        return send_to(source, target, sem.at[0, at], sem.at[1, at], device)

    core_far = swap(part_xc, far_held, core_sem, 0, c_side)
    core_near = swap(part_c, term_c, core_sem, 1, c_side)
    y_near = swap(near, near_y, y_sem, 0, y_side)
    y_side_copy = swap(side, side_y, y_sem, 1, y_side)
    text_c = swap(text_sum.at[0], text_held.at[0], text_sem, 0, c_side)
    text_x = swap(text_sum.at[1], text_held.at[1], text_sem, 1, x_side)
    cots = [
        swap(cot, cot_c, cot_sem, 0, c_side),
        swap(cot, cot_x, cot_sem, 1, x_side),
        swap(cot_x, cot_xc, cot_sem, 2, c_side),
    ]
    core_far.start()
    for copy in exchange:
        copy.start()
    y_near.start()
    core_far.wait_recv()
    rows = 48

    def add_far(at, carry):
        here = pl.ds(pl.multiple_of(at * rows, rows), rows)
        far_sum[here, :] = narrow(wide(part_x[here, :]) + wide(far_held[here, :]))
        return carry

    lax.fori_loop(0, part_x.shape[0] // rows, add_far, 0)
    over = swap(far_sum, term_x, x_sem, 0, x_side)
    over.start()
    core_near.start()
    y_side_copy.start()
    pieces_c = [swap(near, near_c, c_sem, 0, c_side), swap(side, side_c, c_sem, 1, c_side)]
    for copy in pieces_c:
        copy.start()
    cots[0].start()
    for copy in exchange:
        if copy is exchange[0]:
            copy.wait()
        else:
            copy.wait_recv()
    text_sum[0] = narrow(wide(text_parts[:size]) + wide(text_parts[size:]))
    text_c.start()
    text_c.wait_recv()
    text_sum[1] = narrow(wide(text_sum[0]) + wide(text_held[0]))
    text_x.start()
    over.wait_recv()
    cots[1].start()
    y_near.wait_recv()
    more = [swap(near_y, near_yc, c_sem, 2, c_side)]
    more[0].start()
    text_x.wait_recv()
    text_sum[2] = narrow(wide(text_sum[1]) + wide(text_held[1]))
    last = pltpu.make_async_copy(text_sum.at[2], text_out, out_sem.at[0])
    last.start()
    y_side_copy.wait_recv()
    more.append(swap(side_y, side_yc, c_sem, 3, c_side))
    more[1].start()
    cots[1].wait_recv()
    cots[2].start()
    last.wait()
    for copy in pieces_c + more:
        copy.wait()
    core_near.wait()
    over.wait_send()
    cots[0].wait()
    cots[1].wait_send()
    cots[2].wait()
    for copy in exchange[1:]:
        copy.wait_send()
    for copy in (core_far, y_near, y_side_copy, text_c, text_x):
        copy.wait_send()


def middle(parts, near, side, text, cot):
    size = lax.axis_size("z")
    vmem = pl.BlockSpec(memory_space=pltpu.VMEM)
    dma = pltpu.SemaphoreType.DMA
    rows = like(parts[0].shape)
    piece = like(near.shape)
    out = pl.pallas_call(
        functools.partial(middle_kernel, size),
        in_specs=[vmem] * 8,
        out_specs=[ANYWHERE] * 12,
        out_shape=[rows, rows] + [piece] * 6 + [like((size,) + text.shape[1:])] + [rows] * 3,
        scratch_shapes=[
            pltpu.VMEM(text.shape, jnp.bfloat16),
            pltpu.VMEM(rows.shape, jnp.bfloat16),
            pltpu.VMEM(rows.shape, jnp.bfloat16),
            pltpu.VMEM((2, size) + text.shape[1:], jnp.bfloat16),
            pltpu.VMEM((3, size) + text.shape[1:], jnp.bfloat16),
            dma((2, 2)),
            dma((2, 1)),
            dma((2, 2)),
            dma((2, 4)),
            dma((2, 2)),
            dma((1,)),
            dma((2 * size,)),
            dma((2 * size,)),
            dma((2, 3)),
        ],
        compiler_params=pltpu.CompilerParams(
            collective_id=3, has_side_effects=True, vmem_limit_bytes=40 * 2**20
        ),
        cost_estimate=pl.CostEstimate(
            flops=10**7, bytes_accessed=100 * 2**20, transcendentals=0
        ),
        name="middle",
    )(*parts, near, side, text, cot)
    near_y, side_y, near_c, side_c, near_yc, side_yc = out[2:8]
    pieces = [near, near_y, side, side_y, near_c, near_yc, side_c, side_yc]
    return [parts[0], out[0], out[1]], pieces, out[8], [cot] + list(out[9:])


def end_kernel(
    size,
    far,
    near,
    part_own,
    part_c,
    part_x,
    part_xc,
    upstream,
    clip,
    norm,
    norm_in,
    cross,
    text,
    text_rows,
    text_weights,
    grad_out,
    norm_out,
    unit_own,
    unit_x,
    cross_out,
    text_out,
    memory_out,
    y_held,
    folded,
    both,
    moved,
    ring_held,
    unit_held,
    core_held,
    x_moved,
    x_held,
    grads,
    grads_held,
    sums,
    sums_held,
    y_send,
    y_recv,
    c_send,
    c_recv,
    core_sem,
    x_sem,
    ring_send,
    ring_recv,
    clip_send,
    clip_recv,
    hop_send,
    hop_recv,
    unit_sem,
    out_sem,
    cross_held,
    cross_moved,
    cross_final,
    cross_sem,
    text_held,
    text_sum,
    text_sem,
    text_final,
    memory_part,
    memory_held,
    memory_all,
    memory_sem,
    all_send,
    all_recv,
):
    at_y, at_x, at_c, at_z = where_am_i()
    x_side = (at_y, 1 - at_x, at_c, at_z)
    y_side = (1 - at_y, at_x, at_c, at_z)
    c_side = (at_y, at_x, 1 - at_c, at_z)
    z_next = (at_y, at_x, at_c, (at_z + 1) % size)
    half = size // 2
    meet(size)

    def across(core, at, side):
        return send_to(
            far.at[core, at, side],
            y_held.at[core, at, side],
            y_send.at[core, at, side],
            y_recv.at[core, at, side],
            y_side,
        )

    places = [(at, side) for at in range(half) for side in range(2)]
    core_far = send_to(part_xc, core_held.at[1], core_sem.at[0], core_sem.at[1], c_side)
    core_near = send_to(part_c, core_held.at[0], core_sem.at[2], core_sem.at[3], c_side)
    z_sides = []
    for bit in (1, 2):
        low = at_z % 2
        other = (at_z + 1 - 2 * low) if bit == 1 else (at_z + 2) % size
        z_sides.append((at_y, at_x, at_c, other))

    def cross_ring(step):
        return send_to(
            cross.at[1] if step == 0 else cross_moved.at[step - 1],
            cross_held.at[step],
            cross_sem.at[0, step],
            cross_sem.at[1, step],
            z_next,
        )

    def cross_next(step):
        cross_ring(step - 1).wait_recv()
        total = wide(cross_held[step - 1]) + wide(cross[(step + 1) % size])
        if step < size - 1:
            cross_moved[step - 1] = narrow(total)
            cross_ring(step).start()
        else:
            cross_final[...] = total

    text_c = send_to(text, text_held.at[0], text_sem.at[0], text_sem.at[1], c_side)
    text_x = send_to(text_sum.at[0], text_held.at[1], text_sem.at[2], text_sem.at[3], x_side)

    def memory_hop(number):
        return send_to(
            memory_part.at[number],
            memory_held.at[number],
            memory_sem.at[0, number],
            memory_sem.at[1, number],
            z_sides[number],
        )

    def block_at(near_y, near_x, near_c):
        return (((at_y + near_y) % 2) * 2 + (at_x + near_x) % 2) * 2 + (at_c + near_c) % 2

    def memory_copies(stage):
        if stage == 0:
            blocks, device = [block_at(0, 0, 0)], y_side
        elif stage == 1:
            blocks, device = [block_at(i, 0, 0) for i in range(2)], x_side
        else:
            blocks, device = [block_at(i // 2, i % 2, 0) for i in range(4)], c_side
        return [
            send_to(
                memory_all.at[block],
                memory_all.at[block],
                all_send.at[stage, i],
                all_recv.at[stage, i],
                device,
            )
            for i, block in enumerate(blocks)
        ]

    def text_step(step):
        if step == 0:
            text_c.wait_recv()
            text_sum[0] = narrow(wide(text[...]) + wide(text_held[0]))
            text_x.start()
        elif step == 2:
            text_x.wait_recv()
            text_sum[1] = narrow(wide(text_sum[0]) + wide(text_held[1]))
            whole = text_sum[1].reshape(-1, text.shape[2])
            text_final[...] = dot_tn(text_rows[...], whole)
            memory_part[0] = narrow(dot_nt(text_weights[...], whole))
            memory_hop(0).start()
        elif step == 3:
            memory_hop(0).wait_recv()
            memory_part[1] = narrow(wide(memory_part[0]) + wide(memory_held[0]))
            memory_hop(1).start()
        elif step == 4:
            memory_hop(1).wait_recv()
            memory_all[block_at(0, 0, 0)] = narrow(wide(memory_part[1]) + wide(memory_held[1]))
            memory_copies(0)[0].start()
        elif step < 7:
            for copy in memory_copies(step - 5):
                copy.wait_recv()
            for copy in memory_copies(step - 4):
                copy.start()
        else:
            for copy in memory_copies(2):
                copy.wait_recv()

    def to_core(at, side):
        return send_to(
            folded.at[at, side],
            both.at[1, at, side],
            c_send.at[at, side],
            c_recv.at[at, side],
            c_side,
        )

    def fold(at, side):
        across(1, at, side).wait_recv()
        folded[at, side] = narrow(wide(near[1, at, side]) + wide(y_held[1, at, side]))
        to_core(at, side).start()
        across(0, at, side).wait_recv()
        both[0, at, side] = narrow(wide(near[0, at, side]) + wide(y_held[0, at, side]))
        to_core(at, side).wait_recv()

    def chunk(step):
        return ((step // half) + at_c) % 2, step % half

    def ring(step, side):
        source = both.at[chunk(1) + (side,)] if step == 0 else moved.at[step - 1, side]
        return send_to(
            source,
            ring_held.at[step, side],
            ring_send.at[step, side],
            ring_recv.at[step, side],
            z_next,
        )

    def ring_next(step, side):
        which, at = chunk((step + 1) % size)
        ring(step - 1, side).wait_recv()
        moved[step - 1, side] = narrow(
            wide(ring_held[step - 1, side]) + wide(both[which, at, side])
        )
        if step < size - 1:
            ring(step, side).start()

    core_far.start()
    def across_start(side):
        for at in range(half - 1, -1, -1):
            for core in (1, 0):
                across(core, at, side).start()

    across_start(1)
    across_start(0)
    cross_ring(0).start()
    core_near.start()
    frames = clip.shape[1]

    def rows_of(at):
        return pl.ds(pl.multiple_of(at * frames, frames), frames)

    core_far.wait_recv()

    def add_far(at, carry):
        here = rows_of(at)
        x_moved[here, :] = narrow(wide(part_x[here, :]) + wide(core_held[1, here, :]))
        return carry

    lax.fori_loop(0, clip.shape[0], add_far, 0)
    over = send_to(x_moved, x_held, x_sem.at[0], x_sem.at[1], x_side)
    over.start()
    text_c.start()
    fold(1, 1)
    ring(0, 1).start()
    cross_next(1)
    fold(0, 1)
    ring_next(1, 1)
    cross_next(2)
    text_step(0)
    fold(1, 0)
    ring(0, 0).start()
    ring_next(2, 1)
    cross_next(3)
    core_near.wait_recv()
    over.wait_recv()
    sums[...] = jnp.zeros_like(sums)
    sums[2:6, :] = norm_in[...]
    gain, bias = norm[0:1, :], norm[1:2, :]

    def one_block(at, carry):
        here = rows_of(at)
        change = wide(part_own[here, :]) + wide(core_held[0, here, :]) + wide(x_held[here, :])
        back, gain_g, bias_g = norm_gradient(change, wide(clip[at]), gain, bias)
        grads[at] = narrow(upstream[here, :] + back)
        sums[0:1, :] += gain_g
        sums[1:2, :] += bias_g
        return carry

    lax.fori_loop(0, clip.shape[0], one_block, 0)
    exchange = exchange_copies(grads, grads_held, size, clip_send, clip_recv)
    for copy in exchange:
        copy.start()
    hops = [c_side, x_side, y_side] + z_sides

    def hop(number):
        source = sums if number == 0 else sums_held.at[1, number - 1]
        return send_to(
            source, sums_held.at[0, number], hop_send.at[number], hop_recv.at[number], hops[number]
        )

    def hop_next(number):
        hop(number).wait_recv()
        source = sums[...] if number == 0 else sums_held[1, number - 1]
        sums_held[1, number] = source + sums_held[0, number]
        if number + 1 < len(hops):
            hop(number + 1).start()

    hop(0).start()
    ring_next(3, 1)
    last = send_to(moved.at[size - 2, 1], unit_held, unit_sem.at[0], unit_sem.at[1], x_side)
    last.start()
    text_step(2)
    fold(0, 0)
    text_step(3)
    ring_next(1, 0)
    text_step(4)
    hop_next(0)
    hop_next(1)
    text_step(5)
    ring_next(2, 0)
    hop_next(2)
    text_step(6)
    ring_next(3, 0)
    hop_next(3)
    text_step(7)
    hop_next(4)
    for copy in exchange:
        if copy is exchange[0]:
            copy.wait()
        else:
            copy.wait_recv()
    outs = [
        pltpu.make_async_copy(grads_held, grad_out, out_sem.at[0]),
        pltpu.make_async_copy(moved.at[size - 2, 0], unit_own, out_sem.at[1]),
        pltpu.make_async_copy(sums_held.at[1, len(hops) - 1], norm_out, out_sem.at[2]),
        pltpu.make_async_copy(cross_final, cross_out, out_sem.at[4]),
        pltpu.make_async_copy(text_final, text_out, out_sem.at[5]),
        pltpu.make_async_copy(memory_all, memory_out, out_sem.at[6]),
    ]
    for copy in outs:
        copy.start()
    last.wait_recv()
    final = pltpu.make_async_copy(unit_held, unit_x, out_sem.at[3])
    final.start()
    for copy in outs:
        copy.wait()
    final.wait()
    last.wait_send()
    core_far.wait_send()
    core_near.wait_send()
    over.wait_send()
    for at, side in places:
        across(0, at, side).wait_send()
        across(1, at, side).wait_send()
        to_core(at, side).wait_send()
    for step in range(size - 1):
        for side in range(2):
            ring(step, side).wait_send()
    for copy in exchange[1:]:
        copy.wait_send()
    for number in range(len(hops)):
        hop(number).wait_send()
    for step in range(size - 1):
        cross_ring(step).wait_send()
    text_c.wait_send()
    text_x.wait_send()
    for number in range(2):
        memory_hop(number).wait_send()
    for stage in range(3):
        for copy in memory_copies(stage):
            copy.wait_send()


def end(far, near, parts, upstream, clip, norm, norm_in, cross, text, text_rows, text_weights):
    size = lax.axis_size("z")
    half = size // 2
    groups, frames, model = clip.shape
    rows, units = far.shape[-2:]
    vmem = pl.BlockSpec(memory_space=pltpu.VMEM)
    dma = pltpu.SemaphoreType.DMA

    def buffer(*shape, dtype=jnp.bfloat16):
        return pltpu.VMEM(shape, dtype)

    return pl.pallas_call(
        functools.partial(end_kernel, size),
        in_specs=[vmem] * 14,
        out_specs=[ANYWHERE] * 7,
        out_shape=[
            like(clip.shape),
            like((8, model), jnp.float32),
            like((rows, units)),
            like((rows, units)),
            like(cross.shape[1:], jnp.float32),
            like((text_rows.shape[1], text.shape[2]), jnp.float32),
            like((8, text_weights.shape[0], text_rows.shape[0])),
        ],
        scratch_shapes=[
            buffer(2, half, 2, rows, units),
            buffer(half, 2, rows, units),
            buffer(2, half, 2, rows, units),
            buffer(size - 1, 2, rows, units),
            buffer(size - 1, 2, rows, units),
            buffer(rows, units),
            buffer(2, groups * frames, model),
            buffer(groups * frames, model),
            buffer(groups * frames, model),
            buffer(groups, frames, model),
            buffer(groups, frames, model),
            buffer(8, model, dtype=jnp.float32),
            buffer(2, 5, 8, model, dtype=jnp.float32),
            dma((2, half, 2)),
            dma((2, half, 2)),
            dma((half, 2)),
            dma((half, 2)),
            dma((4,)),
            dma((2,)),
            dma((size - 1, 2)),
            dma((size - 1, 2)),
            dma((groups,)),
            dma((groups,)),
            dma((5,)),
            dma((5,)),
            dma((2,)),
            dma((7,)),
            buffer(size - 1, *cross.shape[1:]),
            buffer(size - 2, *cross.shape[1:]),
            buffer(*cross.shape[1:], dtype=jnp.float32),
            dma((2, size - 1)),
            buffer(2, *text.shape),
            buffer(2, *text.shape),
            dma((4,)),
            buffer(text_rows.shape[1], text.shape[2], dtype=jnp.float32),
            buffer(2, text_weights.shape[0], text_rows.shape[0]),
            buffer(2, text_weights.shape[0], text_rows.shape[0]),
            buffer(8, text_weights.shape[0], text_rows.shape[0]),
            dma((2, 2)),
            dma((3, 4)),
            dma((3, 4)),
        ],
        compiler_params=pltpu.CompilerParams(
            collective_id=2, has_side_effects=True, vmem_limit_bytes=56 * 2**20
        ),
        cost_estimate=pl.CostEstimate(
            flops=10**7, bytes_accessed=300 * 2**20, transcendentals=0
        ),
        name="end",
    )(
        far,
        near,
        *parts,
        upstream,
        clip,
        norm,
        norm_in,
        cross,
        text,
        text_rows,
        text_weights,
    )


def clip_body(
    tokens,
    memory,
    text_len,
    cotangent,
    gain_one,
    bias_one,
    gain_two,
    bias_two,
    gain_three,
    bias_three,
    w_query,
    w_key,
    w_value,
    w_out,
    c_query,
    c_key,
    c_value,
    c_out,
    w_up,
    w_down,
):
    at_y, at_x, at_c, at_z = (lax.axis_index(name) for name in ("y", "x", "c", "z"))
    ids = jnp.stack([at_y, at_x, at_c, at_z]).astype(jnp.int32)
    model = tokens.shape[-1]
    shard_rows, shard_width = w_query.shape
    slots = memory.shape[2]
    size = lax.axis_size("z")
    frame_block = tokens.shape[2]

    both = gather_units([w_up, w_down.T])
    split = split_heads([w_query, w_key, w_value, w_out.T])
    norm_one = jnp.stack([gain_one, bias_one])
    at_f = block_of(at_y, at_x, at_c)
    text_mine = lax.dynamic_slice_in_dim(
        memory.reshape(-1, model), at_f * shard_rows, shard_rows, 1
    )
    text_shard = jnp.concatenate([c_key, c_value], axis=1)
    text_part = narrow(dot_nn(text_mine, text_shard)).reshape(-1, slots, 2 * shard_width)
    clip_tokens, rows_one, attend_weights, cross_pieces = start_up(
        tokens.reshape(-1, frame_block, model),
        split,
        norm_one,
        jnp.concatenate([c_query, c_out.T], axis=1),
    )
    near, side = cross_pieces
    upstream = after(cotangent.reshape(-1, frame_block, model), clip_tokens)
    upstream = exchange_clips(upstream).reshape(-1, model)
    count = take(take(text_len, at_y), at_z).reshape(1)
    norms = jnp.stack([gain_two, bias_two, gain_three, bias_three])

    self_parts, qkv, mixed_one, log_total = attend_forward(ids, rows_one, attend_weights)
    self_terms, cross_pieces, text_clip, grad_rows3 = middle(
        self_parts, near, side, text_part, upstream
    )
    text_clip = text_clip.reshape(size, slots, 2, shard_width)
    keys_values = jnp.transpose(text_clip, (1, 2, 0, 3)).reshape(slots, -1)
    after_self, rows_two, cross_q, mixed_two, after_cross, own_three = cross_forward(
        ids, count, clip_tokens, self_terms, norms, keys_values, cross_pieces
    )
    rows_three = group_rows(own_three)

    feed_parts, back_parts, active, grad_hidden = feed(
        ids, rows_three, grad_rows3, both
    )
    back_far = far_sum(back_parts)
    back_terms = group_terms(back_parts, back_far)
    part_down = feed_grads(after(ids, back_far), grad_rows3, active)
    part_up = feed_grads(ids, rows_three, grad_hidden)
    sum_down, sum_up = scatter_units(part_down), scatter_units(part_up)
    grad_one_rows, own_one, own_two, grad_cq, grad_text, norm_grads = cross_backward(
        ids,
        count,
        upstream,
        back_terms,
        norms,
        keys_values,
        after_self,
        after_cross,
        cross_q,
        cross_pieces,
    )
    across = pair_swap(own_one, "x")
    grad_rows1 = [own_one, pair_swap(own_one, "c"), across]
    cross_keep, cross_send = cross_grads(ids, rows_two, grad_cq, own_two, mixed_two)
    cross_near, cross_away = sum_plane(cross_keep, cross_send)
    relay = pair_swap(after(across, part_up, part_down, cross_near, cross_away), "c")
    grad_rows1 = grad_rows1 + [relay]
    cross_sum = (cross_near, pair_swap(after(cross_away, grad_rows1), "x"))
    grad_text = exchange_clips(jnp.concatenate([grad_text, grad_text]))

    feed_parts = after(feed_parts, grad_rows1)
    feed_terms = group_terms(feed_parts, far_sum(feed_parts))
    self_back, grad_qkv = attend_backward(
        after(ids, cross_keep, part_up, part_down),
        grad_rows1,
        attend_weights,
        qkv,
        mixed_one,
        log_total,
    )
    feed_terms = after(feed_terms, self_back)
    result = after_cross + wide(feed_terms[0]) + wide(feed_terms[1]) + wide(feed_terms[2])
    result = narrow(result)
    result = after(result.reshape(-1, frame_block, model), grad_text)
    result = exchange_clips(result).reshape(tokens.shape)

    cross_part = sum_plane_rest(*after(cross_sum, self_back))
    far = attend_grads(ids, rows_one, grad_rows1, grad_qkv, mixed_one, 1)
    near = attend_grads(ids, rows_one, grad_rows1, grad_qkv, mixed_one, 0)
    input_grad, norm_grads, unit_own, unit_away, fin_cross, fin_text, grad_memory = end(
        after(far, result),
        near,
        self_back,
        grad_one_rows,
        clip_tokens.reshape(-1, frame_block, model),
        norm_one,
        norm_grads,
        cross_part,
        grad_text,
        text_mine,
        text_shard,
    )
    fin_down = join_units(sum_down).T
    fin_up = join_units(after(sum_up, input_grad))
    fin_cquery, fin_cout = fin_cross[:, :shard_width], fin_cross[:, shard_width:].T
    fin_ckey, fin_cvalue = fin_text[:, :shard_width], fin_text[:, shard_width:]
    grad_memory = wide(grad_memory.reshape(model, -1).T).reshape(memory.shape)
    input_grad = wide(input_grad).reshape(tokens.shape)
    fin_query, fin_key, fin_value, fin_out = join_heads(unit_own, unit_away)

    return (
        result,
        input_grad,
        grad_memory,
        norm_grads[0],
        norm_grads[1],
        norm_grads[2],
        norm_grads[3],
        norm_grads[4],
        norm_grads[5],
        fin_query,
        fin_key,
        fin_value,
        fin_out.T,
        fin_cquery,
        fin_ckey,
        fin_cvalue,
        fin_cout,
        fin_up,
        fin_down,
    )


def clip_groups(mesh):
    outer, inner = mesh.shape["fsdp"], mesh.shape["tp"]
    return (2, 2, 2, inner) if outer == 8 and inner == 4 else None


def solution(mesh):
    sizes = clip_groups(mesh)
    if sizes is None:
        rows, columns, program, used = "fsdp", "tp", body, mesh
    else:
        rows, columns, program = ("y", "x", "c"), "z", clip_body
        used = jax.sharding.Mesh(mesh.devices.reshape(sizes), ("y", "x", "c", "z"))
    both = ("fsdp", "tp") if sizes is None else ("y", "x", "c", "z")
    frames = P(None, None, both, None)
    tall, wide = P(rows, columns), P(columns, rows)
    weights = (tall, tall, tall, wide, tall, tall, tall, wide, tall, wide)
    return jax.shard_map(
        program,
        mesh=used,
        in_specs=(frames, P(), P(), frames) + (P(),) * 6 + weights,
        out_specs=(frames, frames, P()) + (P(),) * 6 + weights,
        check_vma=False,
    )
```
